32 devices in a mesh: wide: 8 (over z, x), blk: 4 (over y, core).
Axes of the slice: x: 2, y: 2, z: 4, core: 2. Of those that a mesh axis runs over, the one named last changes fastest.
Arguments:
- patches: bfloat16 [64, 512, 768], P('wide', 'blk'), may hold values from -6 to 6
- pos_ids: int32 [64, 512], P('wide', 'blk'), may hold values from 0 to 639, as said below
- lengths: int32 [64], P('wide'), may hold values from 64 to 512, as said below
- pos_table: bfloat16 [768, 640], replicated, may hold values from -3 to 3
- ln1_gain: bfloat16 [768], replicated, may hold values from 0.5 to 1.5
- ln1_bias: bfloat16 [768], replicated, may hold values from -3 to 3
- w_qkv: bfloat16 [768, 2304], replicated, may hold values from -0.21875 to 0.21875
- q_bias: bfloat16 [768], replicated, may hold values from -3 to 3
- v_bias: bfloat16 [768], replicated, may hold values from -3 to 3
- w_proj: bfloat16 [768, 768], replicated, may hold values from -2.5 to 2.5
- proj_bias: bfloat16 [768], replicated, may hold values from -3 to 3
- ln2_gain: bfloat16 [768], replicated, may hold values from 0.5 to 1.5
- ln2_bias: bfloat16 [768], replicated, may hold values from -3 to 3
- w_fc1: bfloat16 [768, 3072], replicated, may hold values from -0.21875 to 0.21875
- fc1_bias: bfloat16 [3072], replicated, may hold values from -3 to 3
- w_fc2: bfloat16 [3072, 768], replicated, may hold values from -0.109375 to 0.109375
- fc2_bias: bfloat16 [768], replicated, may hold values from -3 to 3
- cotangent: bfloat16 [64, 512, 768], P('wide', 'blk'), may hold values from -6 to 6
Outputs:
- mixed: bfloat16 [64, 512, 768], P('wide', 'blk')
- patches_grad: bfloat16 [64, 512, 768], P('wide', 'blk')
- pos_table_grad: float32 [768, 640], P(('wide', 'blk'))
- ln1_gain_grad: float32 [768], P(('wide', 'blk'))
- ln1_bias_grad: float32 [768], P(('wide', 'blk'))
- w_qkv_grad: float32 [768, 2304], P(('wide', 'blk'))
- q_bias_grad: float32 [768], P(('wide', 'blk'))
- v_bias_grad: float32 [768], P(('wide', 'blk'))
- w_proj_grad: float32 [768, 768], P(('wide', 'blk'))
- proj_bias_grad: float32 [768], P(('wide', 'blk'))
- ln2_gain_grad: float32 [768], P(('wide', 'blk'))
- ln2_bias_grad: float32 [768], P(('wide', 'blk'))
- w_fc1_grad: float32 [768, 3072], P(('wide', 'blk'))
- fc1_bias_grad: float32 [3072], P(('wide', 'blk'))
- w_fc2_grad: float32 [3072, 768], P(('wide', 'blk'))
- fc2_bias_grad: float32 [768], P(('wide', 'blk'))
The draws below stay inside these ranges and needn't reach their ends.
Inputs may be any that keep to these rules, and one draw needn't show every extreme that they name: `lengths`: in every aligned block of 8 samples one sample, drawn from the seed, has all 512 slots valid and another exactly 64; slots at or past a sample's length are padding. `pos_ids`: the ids of one sample are distinct.
All inputs are finite; a program needn't handle non-finite values.
Results may differ from the reference program's by a relative error of at most 0.017.
Values may be sent and summed in bfloat16 or wider, within the bound.
No kernel may reach another device: no remote copies, remote signals or barrier semaphores. Data moves between devices by JAX's collectives and lax.ppermute only.
A program may use at most 256 MiB of HBM per device.

```python
import jax
import jax.numpy as jnp
from jax import lax

D = 768
HEADS = 12
HEAD_DIM = 64
FF = 3072
POS = 640
L = 512
S_DEV = 8
SAMPLES = 64


def draw_pos_ids(key, part):
    key = jax.random.fold_in(key, 2)
    sample_keys = jax.random.split(key, SAMPLES)
    rows = jax.vmap(lambda subkey: jax.random.permutation(subkey, POS)[:L])(sample_keys)
    return rows.astype(jnp.int32)


def draw_lengths(key, part):
    key = jax.random.fold_in(key, 1)
    first_key, second_key = jax.random.split(key)
    groups = SAMPLES // S_DEV
    base = jax.random.randint(first_key, (groups, S_DEV), L // 8, L + 1)
    chosen = jax.random.randint(second_key, (groups,), 0, S_DEV)
    slots = jnp.arange(S_DEV)[None, :]
    longest = slots == chosen[:, None]
    minimum_length = slots == ((chosen + 1) % S_DEV)[:, None]
    result = jnp.where(longest, L, jnp.where(minimum_length, L // 8, base))
    return result.reshape(SAMPLES).astype(jnp.int32)


def raised(values, stream_key, source, target, parts, factor):
    owner, partner = [(jnp.arange(values.shape[position]) // (values.shape[position] // parts)).reshape([-1 if axis == position else 1 for axis in range(values.ndim)]) for position in (source, target)]
    chosen = jax.random.permutation(stream_key, parts)[partner]
    strong = (owner == chosen) | (owner == (partner + parts // 2) % parts)
    return jnp.where(strong, factor * values, values)


def block_levels(key, shape, pieces, low, high):
    loudness, own = 1.0, jax.random.fold_in(key, 6)
    for axis_at, parts in pieces:
        heights = jnp.exp(jax.random.uniform(jax.random.fold_in(own, axis_at), (parts,), jnp.float32, low / len(pieces), high / len(pieces)))
        loudness = loudness * jnp.repeat(heights, shape[axis_at] // parts).reshape([-1 if axis == axis_at else 1 for axis in range(len(shape))])
    return loudness


def normal_values(own_key, extent, scale, bound, pieces=(), kind=jnp.bfloat16):
    level = block_levels(own_key, extent, pieces, -0.22, 0.18) if pieces else 1.0
    array = jax.random.normal(own_key, extent, jnp.float32) * scale * level
    return jnp.minimum(jnp.maximum(array, -bound), bound).astype(kind)


def gaussian_with(own_key, shape, width, most, cuts, heavy, kind=jnp.bfloat16):
    values = width * jax.random.normal(own_key, shape, jnp.float32)
    if cuts:
        values = values * block_levels(own_key, shape, cuts, -0.22, 0.18)
    return jnp.clip(raised(values, jax.random.fold_in(own_key, 3), *heavy), -most, most).astype(kind)


def setup_inputs(seed: int = 0) -> dict:
    keys = jax.random.split(jax.random.key(seed), 19)
    return {
        "patches": normal_values(keys[0], (SAMPLES, L, D), 1.0, 6.0, ((0, 8), (1, 4))),
        "pos_ids": draw_pos_ids(jax.random.fold_in(keys[18], 71), 0),
        "lengths": draw_lengths(jax.random.fold_in(keys[18], 71), 0),
        "pos_table": normal_values(keys[3], (D, POS), 0.5, 3.0),
        "ln1_gain": jnp.clip(1.0 + 0.1 * jax.random.normal(keys[4], (D,), jnp.float32), 0.5, 1.5).astype(jnp.bfloat16),
        "ln1_bias": normal_values(keys[5], (D,), 0.3, 3.0),
        "w_qkv": normal_values(keys[6], (D, 3 * D), D ** -0.5, 0.21875),
        "q_bias": normal_values(keys[7], (D,), 0.3, 3.0),
        "v_bias": normal_values(keys[8], (D,), 0.3, 3.0),
        "w_proj": normal_values(keys[9], (D, D), (D * 4 // L) ** -0.5, 2.5),
        "proj_bias": normal_values(keys[10], (D,), 0.3, 3.0),
        "ln2_gain": jnp.clip(1.0 + 0.1 * jax.random.normal(keys[11], (D,), jnp.float32), 0.5, 1.5).astype(jnp.bfloat16),
        "ln2_bias": normal_values(keys[12], (D,), 0.3, 3.0),
        "w_fc1": normal_values(keys[13], (D, FF), D ** -0.5, 0.21875),
        "fc1_bias": normal_values(keys[14], (FF,), 0.3, 3.0),
        "w_fc2": normal_values(keys[15], (FF, D), FF ** -0.5, 0.109375),
        "fc2_bias": normal_values(keys[16], (D,), 0.3, 3.0),
        "cotangent": gaussian_with(keys[17], (SAMPLES, L, D), 1.0, 6.0, ((0, 8), (1, 4)), (0, 2, 8, 2.0)),
    }


@jax.custom_vjp
def low(v):
    return lax.optimization_barrier(v.astype(jnp.bfloat16)).astype(jnp.float32)

@jax.custom_vjp
def low_back(v):
    return v

def low_keep(v):
    return (low(v), None)

def low_pass(kept, grad):
    return (grad,)

def back_keep(v):
    return (v, None)

def back_low(kept, grad):
    return (low(grad),)
low.defvjp(low_keep, low_pass)
low_back.defvjp(back_keep, back_low)
epsilon = 1e-06
topmost_level = lax.Precision.HIGHEST

def norm_rows(stream, gain, shift):
    center = stream - lax.optimization_barrier(jnp.mean(stream, axis=-1, keepdims=True))
    variance = lax.optimization_barrier(jnp.mean(center * center, axis=-1, keepdims=True))
    return center * lax.rsqrt(variance + epsilon) * gain + shift

def dense(remaining_part, weight_matrix):
    return jnp.einsum('vyu,ur->vyr', remaining_part, weight_matrix, precision=topmost_level)

def encoder_layer(params, inputs, position_ids, lengths_here):
    pos_table, ln1_gain, ln1_bias, w_qkv, q_bias, v_bias, w_proj, proj_bias, ln2_gain, ln2_bias, w_fc1, fc1_bias, w_fc2, fc2_bias = params
    samples_here = inputs.shape[0]
    stream = inputs + jnp.transpose(pos_table)[position_ids]
    attn_in = low(norm_rows(stream, ln1_gain, ln1_bias))
    joined = dense(attn_in, w_qkv) + jnp.concatenate([q_bias, jnp.zeros_like(q_bias), v_bias])
    joined = low(low_back(joined))
    queries = joined[..., :D].reshape(samples_here, L, HEADS, HEAD_DIM)
    key_heads = joined[..., D:2 * D].reshape(samples_here, L, HEADS, HEAD_DIM)
    value_heads = joined[..., 2 * D:].reshape(samples_here, L, HEADS, HEAD_DIM)
    scores = jnp.einsum('sqhd,skhd->shqk', queries, key_heads, precision=topmost_level) * HEAD_DIM ** (-0.5)
    scores = low_back(scores)
    visible = (jnp.arange(L).astype(jnp.int32)[None, :] < lengths_here[:, None])[:, None, None, :]
    scores = jnp.where(visible, scores, -1e+30)
    weights = low(jax.nn.softmax(scores, axis=-1))
    attended = jnp.einsum('shqk,skhd->sqhd', weights, value_heads, precision=topmost_level).reshape(samples_here, L, D)
    attn_low = low(low_back(attended))
    stream = stream + low_back(dense(attn_low, w_proj) + proj_bias)
    mlp_in = low(norm_rows(stream, ln2_gain, ln2_bias))
    pre_act = low_back(dense(mlp_in, w_fc1) + fc1_bias)
    act_low = low(jax.nn.gelu(pre_act, approximate=False))
    return stream + low_back(dense(act_low, w_fc2) + fc2_bias)

def reference(patches, pos_ids, lengths, pos_table, ln1_gain, ln1_bias, w_qkv, q_bias, v_bias, w_proj, proj_bias, ln2_gain, ln2_bias, w_fc1, fc1_bias, w_fc2, fc2_bias, cotangent):
    params = tuple((weight_matrix.astype(jnp.float32) for weight_matrix in (pos_table, ln1_gain, ln1_bias, w_qkv, q_bias, v_bias, w_proj, proj_bias, ln2_gain, ln2_bias, w_fc1, fc1_bias, w_fc2, fc2_bias)))
    groups = SAMPLES // S_DEV
    inputs = patches.astype(jnp.float32).reshape(groups, S_DEV, L, D)
    pulled = cotangent.astype(jnp.float32).reshape(groups, S_DEV, L, D)
    id_groups = pos_ids.reshape(groups, S_DEV, L)
    length_groups = lengths.reshape(groups, S_DEV)

    def group_stride(summed, item):
        inputs_here, ids_here, lengths_here, pulled_here = item

        def apply_layer(weights_now, tokens_now):
            return encoder_layer(weights_now, tokens_now, ids_here, lengths_here)
        result, backward = jax.vjp(apply_layer, params, inputs_here)
        weight_grads, input_grad = backward(pulled_here)
        summed = jax.tree.map(lambda remaining_part, right: remaining_part + right, summed, weight_grads)
        return (summed, (result.astype(jnp.bfloat16), input_grad.astype(jnp.bfloat16)))
    start_sums = tuple((jnp.zeros_like(weight_matrix) for weight_matrix in params))
    summed, (results, input_grads) = lax.scan(group_stride, start_sums, (inputs, id_groups, length_groups, pulled))
    return (results.reshape(SAMPLES, L, D), input_grads.reshape(SAMPLES, L, D), summed[0], summed[1], summed[2], summed[3], summed[4], summed[5], summed[6], summed[7], summed[8], summed[9], summed[10], summed[11], summed[12], summed[13])
```

```python
import functools

import jax
import jax.numpy as jnp
from jax import lax
from jax.experimental import pallas as pl
from jax.experimental.pallas import tpu as pltpu
from jax.sharding import PartitionSpec as P

HEADS = 12
F32, BF16 = jnp.float32, jnp.bfloat16
NN = (((1,), (0,)), ((), ()))
NT = (((1,), (1,)), ((), ()))
TN = (((0,), (0,)), ((), ()))
EPS = 1e-6
MASKED = -1e30
AXES = ("wide", "blk")
MIB = 2**20


def dot(a, b, dims=NN):
    return lax.dot_general(a, b, dims, preferred_element_type=F32)


def whole(shape):
    return pl.BlockSpec(shape, lambda *_: (0,) * len(shape))


def normalize(x):
    center = x - jnp.mean(x, axis=-1, keepdims=True)
    inverse = lax.rsqrt(jnp.mean(center * center, axis=-1, keepdims=True) + EPS)
    return center * inverse, inverse


def normalize_back(g, normed, inverse):
    return inverse * (
        g - jnp.mean(g, axis=-1, keepdims=True) - normed * jnp.mean(g * normed, axis=-1, keepdims=True)
    )


def gelu_both(x):
    cdf = 0.5 + 0.5 * lax.erf(x * 0.7071067811865476)
    return x * cdf, cdf + x * (jnp.exp(x * x * -0.5) * 0.3989422804014327)


def row_sum(x):
    return jnp.sum(x.astype(F32), axis=0, keepdims=True)


def owner_dims(owner, order):
    x, y = (owner // 4) % 2, (owner // 2) % 2
    return (owner % 2,) + ((x, y) if order == "xy" else (y, x)) + (owner // 8,)


def store_packed(ref, order, result, first_row, tile_at):
    per = 24
    for k in range(result.shape[0] // per):
        where = owner_dims(first_row // per + k, order)
        rows = result[k * per : (k + 1) * per]
        for c in range(result.shape[1] // 256):
            two = jnp.concatenate([rows[:, c * 256 : c * 256 + 128], rows[:, c * 256 + 128 : c * 256 + 256]], 0)
            start = (tile_at + 2 * c) * per
            ref[where + (slice(start, start + 2 * per), slice(None))] = two.astype(BF16)


def attend_kernel(
    length_ref, x_ref, ids_ref, table_ref, gain_ref, bias_ref, wqkv_ref, bqkv_ref, wproj_ref, bproj_ref, *rest
):
    stream_ref, joined_ref, probs_ref, low_ref, mid_ref, stream, joined, low = rest[-8:]
    j = pl.program_id(0)
    rows, width = stream.shape
    half = 64

    @pl.when(j == 0)
    def _():
        positions = table_ref.shape[1]
        onehot = (ids_ref[0] == lax.broadcasted_iota(jnp.int32, (rows, positions), 1)).astype(F32).astype(BF16)
        value = x_ref[...].reshape(rows, width).astype(F32) + dot(onehot, table_ref[...], NT)
        stream[...] = value
        stream_ref[0] = value
        normed, _ = normalize(value)
        attn_in = (normed * gain_ref[...].astype(F32) + bias_ref[...].astype(F32)).astype(BF16)
        for c in range(3):
            cols = slice(c * width, (c + 1) * width)
            part = (dot(attn_in, wqkv_ref[:, cols]) + bqkv_ref[:, cols].astype(F32)).astype(BF16)
            if c == 0:
                part = part * jnp.asarray(half**-0.5, BF16)
            joined[:, cols] = part
            joined_ref[0, :, cols] = part

    at = pl.multiple_of(j * 128, 128)
    q = joined[:, pl.ds(at, 128)]
    k = joined[:, pl.ds(pl.multiple_of(width + j * 128, 128), 128)]
    v = joined[:, pl.ds(pl.multiple_of(2 * width + j * 128, 128), 128)]
    v_t = v.T
    lane = lax.broadcasted_iota(jnp.int32, (rows, 128), 1)
    visible = lax.broadcasted_iota(jnp.int32, (rows, rows), 0) < length_ref[0]
    outs = []
    for h in range(2):
        q_h = jnp.where((lane < half) == (h == 0), q, jnp.zeros_like(q))
        scores = jnp.where(visible, dot(k, q_h, NT), MASKED)
        weights = jnp.exp(scores - jnp.max(scores, axis=0, keepdims=True))
        probs = (weights * (1.0 / jnp.sum(weights, axis=0, keepdims=True))).astype(BF16)
        probs_ref[0, h] = probs
        outs.append(dot(v_t[h * half : (h + 1) * half], probs))
    low[:, pl.ds(at, 128)] = jnp.concatenate(outs, 0).T.astype(BF16)

    @pl.when(j == pl.num_programs(0) - 1)
    def _():
        low_ref[0] = low[...]
        mid_ref[0] = stream[...] + dot(low[...], wproj_ref[...]) + bproj_ref[...].astype(F32)


def attend(sample, samples, length, x, ids, table, gain, bias, w_qkv, b_qkv, w_proj, b_proj, previous):
    parts, _, piece, width = x.shape
    rows = parts * piece
    pairs = HEADS // 2
    place = lambda j: (sample, 0, 0)
    ops = [length, x, ids, table, gain, bias, w_qkv, b_qkv, w_proj, b_proj]
    in_specs = [
        pl.BlockSpec(memory_space=pltpu.SMEM),
        pl.BlockSpec((parts, 1, piece, width), lambda j: (0, 0, 0, 0)),
        pl.BlockSpec((1, rows, 1), place),
    ] + [whole(a.shape) for a in ops[3:]]
    shapes = [
        ((samples, rows, width), F32),
        ((samples, rows, 3 * width), BF16),
        ((samples, HEADS, rows, rows), BF16),
        ((samples, rows, width), BF16),
        ((samples, rows, width), F32),
    ]
    aliases = {}
    if previous is not None:
        aliases = {len(ops) + i: i for i in range(len(shapes))}
        ops += list(previous)
        in_specs += [pl.BlockSpec(memory_space=pl.ANY)] * len(shapes)
    return pl.pallas_call(
        attend_kernel,
        grid=(pairs,),
        in_specs=in_specs,
        out_specs=[
            pl.BlockSpec((1, rows, width), place),
            pl.BlockSpec((1, rows, 3 * width), place),
            pl.BlockSpec((1, 2, rows, rows), lambda j: (sample, j, 0, 0)),
            pl.BlockSpec((1, rows, width), place),
            pl.BlockSpec((1, rows, width), place),
        ],
        out_shape=[jax.ShapeDtypeStruct(*s) for s in shapes],
        scratch_shapes=[
            pltpu.VMEM((rows, width), F32),
            pltpu.VMEM((rows, 3 * width), BF16),
            pltpu.VMEM((rows, width), BF16),
        ],
        input_output_aliases=aliases,
        compiler_params=pltpu.CompilerParams(vmem_limit_bytes=56 * MIB),
        cost_estimate=pl.CostEstimate(flops=12 * 10**9, bytes_accessed=30 * 10**6, transcendentals=0),
        name=f"attend_{sample}",
    )(*ops)


def mlp_kernel(
    packed, x_ref, gt_ref, w1_ref, b1_ref, w2_ref, b2_ref, gain_ref, bias_ref,
    mixed_ref, gmid_ref, gone_ref, dw1_ref, dw2_ref, db1_ref, small_ref,
    mlp_in, mlp_in_t, gt, act, gpre, acc, gacc,
):
    j = pl.program_id(0)
    samples, rows, width = x_ref.shape
    piece = gt_ref.shape[2]
    columns = w1_ref.shape[1]
    tile = 2 * piece
    per_sample = rows // tile
    tiles = samples * per_sample

    @pl.when(j == 0)
    def _():
        for i in range(tiles):
            s, t = i // per_sample, i % per_sample
            here = slice(i * tile, (i + 1) * tile)
            normed, _ = normalize(x_ref[s, t * tile : (t + 1) * tile])
            value = (normed * gain_ref[...].astype(F32) + bias_ref[...].astype(F32)).astype(BF16)
            mlp_in[here] = value
            mlp_in_t[:, here] = value.T
            gt[here] = gt_ref[2 * t : 2 * t + 2, s].reshape(tile, width)
            acc[here] = jnp.zeros((tile, width), F32)
            gacc[here] = jnp.zeros((tile, width), F32)

    b1 = b1_ref[...].astype(F32)
    db1 = jnp.zeros((1, columns), F32)
    for i in range(tiles):
        here = slice(i * tile, (i + 1) * tile)
        value, slope = gelu_both(dot(mlp_in[here], w1_ref[...]) + b1)
        value = value.astype(BF16)
        act[here] = value
        g = (dot(gt[here], w2_ref[...], NT) * slope).astype(BF16)
        gpre[here] = g
        db1 = db1 + row_sum(g)
        acc[here] += dot(value, w2_ref[...])
        gacc[here] += dot(g, w1_ref[...], NT)
    db1_ref[...] = db1
    if packed:
        step = 192
        for i in range(width // step):
            store_packed(dw1_ref, "xy", dot(mlp_in_t[i * step : (i + 1) * step], gpre[...]), i * step, 0)
        result = dot(act[...], gt[...], TN)
        for k in range(columns // 96):
            where = owner_dims(k, "yx")[:3] + (0,)
            dw2_ref[where] = result[k * 96 : (k + 1) * 96].astype(BF16)
    else:
        dw1_ref[...] = dot(mlp_in_t[...], gpre[...])
        dw2_ref[...] = dot(act[...], gt[...], TN)

    @pl.when(j == pl.num_programs(0) - 1)
    def _():
        gain = gain_ref[...].astype(F32)
        sums = [jnp.zeros((1, width), F32) for _ in range(4)]
        for i in range(tiles):
            s, t = i // per_sample, i % per_sample
            here = slice(i * tile, (i + 1) * tile)
            x = x_ref[s, t * tile : (t + 1) * tile]
            normed, inverse = normalize(x)
            mixed = (x + acc[here] + b2_ref[...].astype(F32)).astype(BF16)
            mixed_ref[2 * t : 2 * t + 2, s] = mixed.reshape(2, piece, width)
            cot = gt[here].astype(F32)
            g = gacc[here]
            gmid = cot + normalize_back(g * gain, normed, inverse)
            gmid_ref[s, t * tile : (t + 1) * tile] = gmid
            low = gmid.astype(BF16)
            gone_ref[s, t * tile : (t + 1) * tile] = low
            sums = [a + row_sum(b) for a, b in zip(sums, (g * normed, g, cot, low))]
        for k in range(4):
            small_ref[k : k + 1] = sums[k]


def mlp(packed, x, gt, w1, b1, w2, b2, gain, bias):
    samples, rows, width = x.shape
    parts, _, piece, _ = gt.shape
    hidden = w1.shape[1]
    columns = 768 if hidden % 768 == 0 else hidden
    tokens = samples * rows
    if packed:
        dw1 = ((2, 2, 2, 4, 24 * hidden // 128, 128), BF16)
        dw1_spec = pl.BlockSpec((2, 2, 2, 4, 24 * columns // 128, 128), lambda j: (0, 0, 0, 0, j, 0))
        dw2 = ((2, 2, 2, 4, 96, width), BF16)
        dw2_spec = pl.BlockSpec((2, 2, 2, 1, 96, width), lambda j: (0, 0, 0, j, 0, 0))
    else:
        dw1 = ((width, hidden), F32)
        dw1_spec = pl.BlockSpec((width, columns), lambda j: (0, j))
        dw2 = ((hidden, width), F32)
        dw2_spec = pl.BlockSpec((columns, width), lambda j: (j, 0))
    shapes = [
        ((parts, samples, piece, width), BF16),
        (x.shape, F32),
        (x.shape, BF16),
        dw1,
        dw2,
        ((1, hidden), F32),
        ((4, width), F32),
    ]
    return pl.pallas_call(
        functools.partial(mlp_kernel, packed),
        grid=(hidden // columns,),
        in_specs=[
            whole(x.shape),
            whole(gt.shape),
            pl.BlockSpec((width, columns), lambda j: (0, j)),
            pl.BlockSpec((1, columns), lambda j: (0, j)),
            pl.BlockSpec((columns, width), lambda j: (j, 0)),
            whole((1, width)),
            whole((1, width)),
            whole((1, width)),
        ],
        out_specs=[
            whole(shapes[0][0]),
            whole(x.shape),
            whole(x.shape),
            dw1_spec,
            dw2_spec,
            pl.BlockSpec((1, columns), lambda j: (0, j)),
            whole((4, width)),
        ],
        out_shape=[jax.ShapeDtypeStruct(*s) for s in shapes],
        scratch_shapes=[
            pltpu.VMEM((tokens, width), BF16),
            pltpu.VMEM((width, tokens), BF16),
            pltpu.VMEM((tokens, width), BF16),
            pltpu.VMEM((tokens, columns), BF16),
            pltpu.VMEM((tokens, columns), BF16),
            pltpu.VMEM((tokens, width), F32),
            pltpu.VMEM((tokens, width), F32),
        ],
        compiler_params=pltpu.CompilerParams(vmem_limit_bytes=60 * MIB),
        cost_estimate=pl.CostEstimate(flops=30 * 10**9, bytes_accessed=30 * 10**6, transcendentals=0),
        name="mlp",
    )(x, gt, w1, b1, w2, b2, gain, bias)


def attend_back_kernel(gone_ref, low_ref, joined_ref, probs_ref, wproj_ref, gjoined_ref, gatt, delta):
    j = pl.program_id(1)
    _, rows, width = gone_ref.shape
    half = 64

    @pl.when(j == 0)
    def _():
        grad = dot(gone_ref[0], wproj_ref[...], NT).astype(BF16)
        gatt[...] = grad
        product = grad.astype(F32) * low_ref[0].astype(F32)
        high = product.astype(BF16)
        rest = (product - high.astype(F32)).astype(BF16)
        heads = lax.broadcasted_iota(jnp.int32, (16, width), 0)
        owner = lax.broadcasted_iota(jnp.int32, (16, width), 1) // half
        pick = (heads == owner).astype(F32).astype(BF16)
        delta[...] = dot(pick, high, NT) + dot(pick, rest, NT)

    at = pl.multiple_of(j * 128, 128)
    at_k = pl.multiple_of(width + j * 128, 128)
    at_v = pl.multiple_of(2 * width + j * 128, 128)
    q = joined_ref[0, :, pl.ds(at, 128)]
    k = joined_ref[0, :, pl.ds(at_k, 128)]
    v = joined_ref[0, :, pl.ds(at_v, 128)]
    g = gatt[:, pl.ds(at, 128)]
    k_t = k.T
    left = lax.broadcasted_iota(jnp.int32, (rows, 128), 1) < half
    g_q, g_k, g_v = [], [], []
    for h in range(2):
        g_h = jnp.where(left == (h == 0), g, jnp.zeros_like(g))
        probs = probs_ref[0, h]
        back = dot(v, g_h, NT) - delta[pl.ds(2 * j + h, 1), :]
        scores = (probs.astype(F32) * back).astype(BF16)
        g_v.append(dot(probs, g))
        g_k.append(dot(scores, q))
        g_q.append(dot(k_t[h * half : (h + 1) * half], scores))
    gjoined_ref[0, :, pl.ds(at, 128)] = (jnp.concatenate(g_q, 0).T * half**-0.5).astype(BF16)
    gjoined_ref[0, :, pl.ds(at_k, 128)] = jnp.where(left, g_k[0], g_k[1]).astype(BF16)
    gjoined_ref[0, :, pl.ds(at_v, 128)] = jnp.where(left, g_v[0], g_v[1]).astype(BF16)


def attend_back(gone, low, joined, probs, w_proj):
    samples, rows, width = gone.shape
    by_sample = lambda shape: pl.BlockSpec((1,) + shape, lambda s, j: (s, 0, 0))
    return pl.pallas_call(
        attend_back_kernel,
        grid=(samples, HEADS // 2),
        in_specs=[
            by_sample((rows, width)),
            by_sample((rows, width)),
            by_sample((rows, 3 * width)),
            pl.BlockSpec((1, 2, rows, rows), lambda s, j: (s, j, 0, 0)),
            whole(w_proj.shape),
        ],
        out_specs=by_sample((rows, 3 * width)),
        out_shape=jax.ShapeDtypeStruct((samples, rows, 3 * width), BF16),
        scratch_shapes=[pltpu.VMEM((rows, width), BF16), pltpu.VMEM((16, rows), F32)],
        compiler_params=pltpu.CompilerParams(vmem_limit_bytes=56 * MIB),
        cost_estimate=pl.CostEstimate(flops=20 * 10**9, bytes_accessed=30 * 10**6, transcendentals=0),
        name="attend_back",
    )(gone, low, joined, probs, w_proj)


def finish_kernel(
    packed, misc_cols, gjoined_ref, w_ref, stream_ref, gmid_ref, gone_ref, low_ref, ids_ref, gain_ref, bias_ref, small_ref, db1_ref,
    dwqkv_ref, misc_ref, pgrad_ref, normed, inverse, attn_in_t, gacc, sums,
):
    j = pl.program_id(0)
    samples, rows, width = stream_ref.shape
    tokens = samples * rows
    piece = pgrad_ref.shape[2]
    positions = misc_cols - width - 128
    tile = 2 * piece
    per_sample = rows // tile
    tiles = samples * per_sample
    step = 192

    def put(first_tile, lhs, rhs):
        if packed:
            for i in range(width // step):
                result = dot(lhs[i * step : (i + 1) * step], rhs)
                store_packed(misc_ref, "yx", result, i * step, first_tile)
        else:
            misc_ref[:, first_tile * 128 : first_tile * 128 + rhs.shape[1]] = dot(lhs, rhs)

    @pl.when(j == 0)
    def _():
        for i in range(tiles):
            s, t = i // per_sample, i % per_sample
            here = slice(i * tile, (i + 1) * tile)
            n, inv = normalize(stream_ref[s, t * tile : (t + 1) * tile])
            normed[here] = n
            inverse[here] = inv
            value = (n * gain_ref[...].astype(F32) + bias_ref[...].astype(F32)).astype(BF16)
            attn_in_t[:, here] = value.T
            gacc[here] = jnp.zeros((tile, width), F32)
        put(0, low_ref[...].reshape(tokens, width).T, gone_ref[...].reshape(tokens, width))

    g = gjoined_ref[...].reshape(tokens, width)
    for i in range(tiles):
        here = slice(i * tile, (i + 1) * tile)
        gacc[here] += dot(g[here], w_ref[...], NT)
    sums[pl.ds(j, 1)] = row_sum(g)
    if packed:
        for i in range(width // step):
            store_packed(dwqkv_ref, "xy", dot(attn_in_t[i * step : (i + 1) * step], g), i * step, 0)
    else:
        dwqkv_ref[...] = dot(attn_in_t[...], g)

    @pl.when(j == pl.num_programs(0) - 1)
    def _():
        gain = gain_ref[...].astype(F32)
        g_gain = jnp.zeros((1, width), F32)
        g_bias = jnp.zeros((1, width), F32)
        hots = []
        for i in range(tiles):
            s, t = i // per_sample, i % per_sample
            here = slice(i * tile, (i + 1) * tile)
            n = normed[here]
            grad = gacc[here]
            total = gmid_ref[s, t * tile : (t + 1) * tile] + normalize_back(grad * gain, n, inverse[here])
            low = total.astype(BF16)
            pgrad_ref[2 * t : 2 * t + 2, s] = low.reshape(2, piece, width)
            attn_in_t[:, here] = low.T
            g_gain = g_gain + row_sum(grad * n)
            g_bias = g_bias + row_sum(grad)
            ids = ids_ref[s, t * tile : (t + 1) * tile]
            hots.append((ids == lax.broadcasted_iota(jnp.int32, (tile, positions), 1)).astype(F32).astype(BF16))
        zero = jnp.zeros((1, width), F32)
        few = [g_gain, g_bias, sums[0:1], sums[2:3], small_ref[3:4], small_ref[0:1], small_ref[1:2], small_ref[2:3]]
        few += [db1_ref[...]] + [zero] * 4
        few = jnp.concatenate(few, 0)
        few_t = jnp.concatenate([few, jnp.zeros((112, width), F32)], 0).T
        hot = jnp.concatenate(hots, 0)
        if packed:
            for i in range(width // step):
                cut = slice(i * step, (i + 1) * step)
                result = jnp.concatenate([dot(attn_in_t[cut], hot), few_t[cut]], 1)
                store_packed(misc_ref, "yx", result, i * step, 6)
        else:
            misc_ref[:, width:] = jnp.concatenate([dot(attn_in_t[...], hot), few_t], 1)


def finish(packed, gjoined, w_qkv, stream, gmid, gone, low, ids, gain, bias, small, db1, parts, positions):
    samples, rows, width = stream.shape
    tokens = samples * rows
    piece = rows // parts
    misc_cols = width + positions + 128
    if packed:
        dwqkv = ((2, 2, 2, 4, 24 * 18, 128), BF16)
        dwqkv_spec = pl.BlockSpec((2, 2, 2, 4, 24 * 6, 128), lambda j: (0, 0, 0, 0, j, 0))
        misc = ((2, 2, 2, 4, 24 * misc_cols // 128, 128), BF16)
    else:
        dwqkv = ((width, 3 * width), F32)
        dwqkv_spec = pl.BlockSpec((width, width), lambda j: (0, j))
        misc = ((width, misc_cols), F32)
    pgrad = ((parts, samples, piece, width), BF16)
    return pl.pallas_call(
        functools.partial(finish_kernel, packed, misc_cols),
        grid=(3,),
        in_specs=[
            pl.BlockSpec((samples, rows, width), lambda j: (0, 0, j)),
            pl.BlockSpec((width, width), lambda j: (0, j)),
        ]
        + [whole(a.shape) for a in (stream, gmid, gone, low, ids, gain, bias, small, db1)],
        out_specs=[dwqkv_spec, whole(misc[0]), whole(pgrad[0])],
        out_shape=[jax.ShapeDtypeStruct(*s) for s in (dwqkv, misc, pgrad)],
        scratch_shapes=[
            pltpu.VMEM((tokens, width), F32),
            pltpu.VMEM((tokens, 1), F32),
            pltpu.VMEM((width, tokens), BF16),
            pltpu.VMEM((tokens, width), F32),
            pltpu.VMEM((8, width), F32),
        ],
        compiler_params=pltpu.CompilerParams(vmem_limit_bytes=60 * MIB),
        cost_estimate=pl.CostEstimate(flops=12 * 10**9, bytes_accessed=30 * 10**6, transcendentals=0),
        name="finish",
    )(gjoined, w_qkv, stream, gmid, gone, low, ids, gain, bias, small, db1)


def swap_bit(x, bit, count):
    return lax.ppermute(x, AXES, [(i, i ^ bit) for i in range(count)])


def reduce_packed(grad, order, count):
    here = lax.axis_index(AXES)
    x = lax.psum_scatter(grad, "blk", scatter_dimension=0, tiled=False, axis_index_groups=[[0, 1], [2, 3]])
    for name in order:
        bit = {"x": 4, "y": 2}[name]
        mine = (here // bit) % 2
        keep = lax.dynamic_index_in_dim(x, mine, 0, keepdims=False)
        send = lax.dynamic_index_in_dim(x, 1 - mine, 0, keepdims=False)
        x = keep + swap_bit(send, bit, count)
    pieces = lax.all_to_all(x, "wide", 0, 0, axis_index_groups=[[0, 2, 4, 6], [1, 3, 5, 7]], tiled=True)
    return jnp.sum(pieces.astype(F32), axis=0)


def unpack(x):
    tiles = x.shape[0] // 24
    return jnp.transpose(x.reshape(tiles, 24, 128), (1, 0, 2)).reshape(24, tiles * 128)


def shards(
    patches, pos_ids, lengths, pos_table, ln1_gain, ln1_bias, w_qkv, q_bias, v_bias, w_proj, proj_bias,
    ln2_gain, ln2_bias, w_fc1, fc1_bias, w_fc2, fc2_bias, cotangent, *, wide, parts,
):
    samples_here, piece, width = patches.shape
    samples = samples_here // parts
    rows = parts * piece
    count = wide * parts
    packed = wide == 8 and parts == 4
    row = lambda a: a.reshape(1, -1)
    swap = lambda a: lax.all_to_all(a, "blk", 0, 0, tiled=True)

    cut = patches.reshape(parts, samples, piece, width)
    xs = [swap(cut[:, s : s + 1]) for s in range(samples)]
    ids = swap(pos_ids.reshape(parts, samples, piece))
    ids = jnp.transpose(ids, (1, 0, 2)).reshape(samples, rows, 1)
    me = lax.axis_index("blk")
    own_lengths = lax.dynamic_slice_in_dim(lengths, me * samples, samples)
    gt = swap(cotangent.reshape(parts, samples, piece, width))
    b_qkv = row(jnp.concatenate([q_bias, jnp.zeros_like(q_bias), v_bias]))

    saved = None
    for s in range(samples):
        saved = attend(
            s, samples, own_lengths[s : s + 1], xs[s], ids, pos_table, row(ln1_gain), row(ln1_bias),
            w_qkv, b_qkv, w_proj, row(proj_bias), saved,
        )
    stream, joined, probs, low, mid = saved
    mixed, gmid, gone, dw1, dw2, db1, small = mlp(
        packed, mid, gt, w_fc1, row(fc1_bias), w_fc2, row(fc2_bias), row(ln2_gain), row(ln2_bias)
    )
    mixed = swap(mixed).reshape(patches.shape)
    gjoined = attend_back(gone, low, joined, probs, w_proj)
    dwqkv, misc, pgrad = finish(
        packed, gjoined, w_qkv, stream, gmid, gone, low, ids, row(ln1_gain), row(ln1_bias), small,
        jnp.transpose(db1.reshape(width, -1)), parts, pos_table.shape[1],
    )
    pgrad = swap(pgrad).reshape(patches.shape)
    if packed:
        dw1 = unpack(reduce_packed(dw1, "xy", count))
        dw2 = reduce_packed(dw2, "yx", count)
        dwqkv = unpack(reduce_packed(dwqkv, "xy", count))
        misc = unpack(reduce_packed(misc, "yx", count))
    else:
        share = lambda a: lax.psum_scatter(a.astype(BF16), AXES, scatter_dimension=0, tiled=True).astype(F32)
        dw1, dw2, dwqkv, misc = share(dw1), share(dw2), share(dwqkv), share(misc)
    dwproj, table, few = misc[:, :width], misc[:, width:-128], misc[:, -128:]
    (g_gain1, g_bias1, g_q, g_v, g_proj, g_gain2, g_bias2, g_fc2) = [few[:, k] for k in range(8)]
    g_fc1 = few[:, 8:12].reshape(-1)
    return (
        mixed, pgrad, table, g_gain1, g_bias1, dwqkv, g_q, g_v, dwproj, g_proj, g_gain2, g_bias2,
        dw1, g_fc1, dw2, g_fc2,
    )


def solution(mesh):
    wide, parts = mesh.shape["wide"], mesh.shape["blk"]
    tokens = P("wide", "blk", None)
    in_specs = (tokens, P("wide", "blk"), P("wide")) + (P(),) * 14 + (tokens,)
    vector, matrix = P(AXES), P(AXES, None)
    out_specs = (
        tokens, tokens, matrix, vector, vector, matrix, vector, vector, matrix, vector, vector, vector,
        matrix, vector, matrix, vector,
    )
    return jax.shard_map(
        functools.partial(shards, wide=wide, parts=parts),
        mesh=mesh, in_specs=in_specs, out_specs=out_specs, check_vma=False,
    )
```

```python
import functools

import jax
import jax.numpy as jnp
from jax import lax
from jax.experimental import pallas as pl
from jax.experimental.pallas import tpu as pltpu
from jax.sharding import PartitionSpec as P

HEADS = 12
HALF = 64
F32, BF16 = jnp.float32, jnp.bfloat16
NN = (((1,), (0,)), ((), ()))
NT = (((1,), (1,)), ((), ()))
TN = (((0,), (0,)), ((), ()))
EPS = 1e-6
MASKED = -1e30
AXES = ("wide", "blk")
MIB = 2**20
CORE, Y, X, Z0, Z1 = 1, 2, 4, 8, 16
X_FIRST = (CORE, X, Y, Z0)
Z_FIRST = (CORE, Z0, X, Y)
PER = 24
VMEM = pl.BlockSpec(memory_space=pltpu.VMEM)
ANY = pl.BlockSpec(memory_space=pl.ANY)
SMEM = pl.BlockSpec(memory_space=pltpu.SMEM)


def dot(a, b, dims=NN):
    return lax.dot_general(a, b, dims, preferred_element_type=F32)


def near(*arrays):
    return [pltpu.with_memory_space_constraint(a, pltpu.VMEM) for a in arrays]


def far(*arrays):
    return [pltpu.with_memory_space_constraint(a, pltpu.HBM) for a in arrays]


def after(value, *others):
    return lax.optimization_barrier((value,) + others)[0]


def place():
    lane = lax.axis_index("blk")
    return lax.axis_index("wide") * lax.axis_size("blk") + lane, lane


def params(vmem):
    return pltpu.CompilerParams(vmem_limit_bytes=vmem * MIB)


def cost(us):
    return pl.CostEstimate(flops=int(us * 10**9), bytes_accessed=0, transcendentals=0)


def normalize(x):
    center = x - jnp.mean(x, axis=-1, keepdims=True)
    inverse = lax.rsqrt(jnp.mean(center * center, axis=-1, keepdims=True) + EPS)
    return center * inverse, inverse


def normalize_back(g, normed, inverse):
    return inverse * (
        g - jnp.mean(g, axis=-1, keepdims=True) - normed * jnp.mean(g * normed, axis=-1, keepdims=True)
    )


def gelu_both(x):
    cdf = 0.5 + 0.5 * lax.erf(x * 0.7071067811865476)
    return x * cdf, cdf + x * (jnp.exp(x * x * -0.5) * 0.3989422804014327)


def row_sum(x):
    return jnp.sum(x.astype(F32), axis=0, keepdims=True)


def relative(position, order):
    return sum(bit for i, bit in enumerate(order) if (position >> (len(order) - 1 - i)) & 1)


def store_packed(keep_ref, send_ref, order, me, result_ref, base=0, extra=0):
    half = 2 ** (len(order) - 1)
    for position in range(2 * half):
        ref = (keep_ref, send_ref)[position // half]
        start = pl.multiple_of((me ^ (relative(position, order) | extra)) * PER, 8)
        for c in range(result_ref.shape[1] // 256):
            two = [result_ref[pl.ds(start, PER), (2 * c + i) * 128 : (2 * c + i + 1) * 128] for i in range(2)]
            here = pl.ds(base + 2 * c * PER, 2 * PER)
            ref[position % half, here] = jnp.concatenate(two, 0).astype(BF16)


def part_kernel(sample, ids_ref, patches_ref, *rest):
    outs, (sems,) = rest[:-1], rest[-1:]
    piece, width = patches_ref.shape[1:]
    lane_me = place()[1]
    copies = []
    for k, out in enumerate(outs):
        at = 2 * (lane_me ^ k) + sample
        copies.append(pltpu.make_async_copy(patches_ref.at[at], out.at[0:piece], sems.at[k]))
        copies[-1].start()
    for k, out in enumerate(outs):
        ids = ids_ref[pl.ds(2 * (lane_me ^ k) + sample, 1)]
        row = jnp.concatenate([ids >> 8, ids & 255, jnp.zeros((1, width - 2 * piece), jnp.int32)], 1)
        out[piece : piece + 16] = jnp.broadcast_to(row.astype(F32), (16, width)).astype(BF16)
    for copy in copies:
        copy.wait()


def part(sample, parts, pos_ids, patches):
    _, piece, width = patches.shape
    return pl.pallas_call(
        functools.partial(part_kernel, sample),
        in_specs=[VMEM, ANY],
        out_specs=[VMEM] * parts,
        out_shape=[pltpu.VMEM((piece + 16, width), BF16)] * parts,
        scratch_shapes=[pltpu.SemaphoreType.DMA((parts,))],
        compiler_params=params(4),
        cost_estimate=cost(1),
        name=f"part_{sample}",
    )(pos_ids, *far(patches))


def spread_kernel(x_ref, *rest):
    outs, (sems,) = rest[:-1], rest[-1:]
    lane_me = place()[1]
    copies = [
        pltpu.make_async_copy(x_ref.at[pl.ds(2 * (lane_me ^ k), 2)], out, sems.at[k]) for k, out in enumerate(outs)
    ]
    for copy in copies:
        copy.start()
    for copy in copies:
        copy.wait()


def spread(parts, x):
    return pl.pallas_call(
        spread_kernel,
        in_specs=[ANY],
        out_specs=[VMEM] * parts,
        out_shape=[pltpu.VMEM((2,) + x.shape[1:], x.dtype)] * parts,
        scratch_shapes=[pltpu.SemaphoreType.DMA((parts,))],
        compiler_params=params(4),
        cost_estimate=cost(1),
        name="spread",
    )(*far(x))


def gather_kernel(*refs):
    pieces, out, sems = refs[:-2], refs[-2], refs[-1]
    lane_me = place()[1]
    copies = [
        pltpu.make_async_copy(a, out.at[pl.ds(2 * (lane_me ^ k), 2)], sems.at[k]) for k, a in enumerate(pieces)
    ]
    for copy in copies:
        copy.start()
    for copy in copies:
        copy.wait()


def gather(pieces):
    parts = len(pieces)
    return pl.pallas_call(
        gather_kernel,
        in_specs=[VMEM] * parts,
        out_specs=ANY,
        out_shape=pltpu.HBM((2 * parts,) + pieces[0].shape[1:], BF16),
        scratch_shapes=[pltpu.SemaphoreType.DMA((parts,))],
        compiler_params=params(4),
        cost_estimate=cost(1),
        name="gather",
    )(*near(*pieces))


def warm_kernel(*refs):
    vectors, big = refs[:9], refs[9:12]
    vec_ref, outs, sems = refs[12], refs[13:16], refs[16]
    copies = [pltpu.make_async_copy(a, b, sems.at[i]) for i, (a, b) in enumerate(zip(big, outs))]
    for copy in copies:
        copy.start()
    width = vec_ref.shape[1]
    row = 0
    for ref in vectors:
        for k in range(ref.shape[0] // width):
            vec_ref[row : row + 1] = ref[k * width : (k + 1) * width].astype(F32).reshape(1, width)
            row += 1
    vec_ref[row:] = jnp.zeros((vec_ref.shape[0] - row, width), F32)
    for copy in copies:
        copy.wait()


def warm(vectors, big):
    width = vectors[0].shape[0]
    return pl.pallas_call(
        warm_kernel,
        in_specs=[VMEM] * len(vectors) + [ANY] * len(big),
        out_specs=[VMEM] * (1 + len(big)),
        out_shape=[pltpu.VMEM((16, width), F32)] + [pltpu.VMEM(a.shape, a.dtype) for a in big],
        scratch_shapes=[pltpu.SemaphoreType.DMA((len(big),))],
        compiler_params=params(4),
        cost_estimate=cost(1),
        name="warm",
    )(*vectors, *far(*big))


def attend_kernel(
    sample, fetch, lengths_ref, x0_ref, x1_ref, x2_ref, x3_ref, table_ref, vec_ref, wqkv_ref, wproj_ref, *rest
):
    fetches, rest = rest[:fetch], rest[fetch:]
    mid_ref, ids_ref, probs_ref, rest = rest[0], rest[1], rest[2], rest[3:]
    fetched, rest = rest[:fetch], rest[fetch:]
    outs, (stream, joined, attn_in, attn_in_t, low, low_t, sems, fetch_sems) = rest[:5], rest[5:]
    saved = (stream, joined, attn_in_t, low, low_t)
    copies = [pltpu.make_async_copy(a, b, sems.at[i]) for i, (a, b) in enumerate(zip(saved, outs))]
    loads = [pltpu.make_async_copy(a, b, fetch_sems.at[i]) for i, (a, b) in enumerate(zip(fetches, fetched))]
    j = pl.program_id(0)
    pieces = (x0_ref, x1_ref, x2_ref, x3_ref)
    rows, width = stream.shape
    piece = rows // len(pieces)

    @pl.when(j == 0)
    def _():
        for load in loads:
            load.start()
        positions = table_ref.shape[1]
        ids = []
        for k, ref in enumerate(pieces):
            coded = ref[piece : piece + 16].astype(F32)
            ids.append(coded[0:8, 0:piece] * 256.0 + coded[0:8, piece : 2 * piece])
        ids_ref[...] = jnp.concatenate(ids, 1)
        for k, ref in enumerate(pieces):
            here = slice(k * piece, (k + 1) * piece)
            column = jnp.broadcast_to(ids[k][0:1], (piece, piece)).T.astype(jnp.int32)
            iota = lax.broadcasted_iota(jnp.int32, (piece, piece), 1)
            onehot = jnp.concatenate([(column == iota + piece * c).astype(F32) for c in range(positions // piece)], 1)
            value = ref[0:piece].astype(F32) + dot(onehot.astype(BF16), table_ref[...], NT)
            stream[here] = value
            normed, _ = normalize(value)
            normed = (normed * vec_ref[0:1] + vec_ref[1:2]).astype(BF16)
            attn_in[here] = normed
            attn_in_t[:, here] = normed.T
        copies[0].start()
        copies[2].start()
        for c in range(3):
            cols = slice(c * width, (c + 1) * width)
            part = dot(attn_in[...], wqkv_ref[:, cols])
            if c != 1:
                part = part + vec_ref[2 + c // 2 : 3 + c // 2]
            part = part.astype(BF16)
            if c == 0:
                part = part * jnp.asarray(HALF**-0.5, BF16)
            joined[:, cols] = part
        copies[1].start()

    at = pl.multiple_of(j * 128, 128)
    q = joined[:, pl.ds(at, 128)]
    k = joined[:, pl.ds(pl.multiple_of(width + j * 128, 128), 128)]
    v = joined[:, pl.ds(pl.multiple_of(2 * width + j * 128, 128), 128)]
    v_t = v.T
    left = lax.broadcasted_iota(jnp.int32, (rows, 128), 1) < HALF
    part = lax.broadcasted_iota(jnp.int32, (piece, rows), 0)
    lane_me = place()[1]
    length = lengths_ref[2 * lane_me + sample]
    visible = jnp.concatenate([part + (lane_me ^ i) * piece < length for i in range(len(pieces))], 0)
    heads = []
    for h in range(2):
        q_h = jnp.where(left == (h == 0), q, jnp.zeros_like(q))
        scores = jnp.where(visible, dot(k, q_h, NT), MASKED)
        weights = jnp.exp(scores - jnp.max(scores, axis=0, keepdims=True))
        probs = (weights * (1.0 / jnp.sum(weights, axis=0, keepdims=True))).astype(BF16)
        probs_ref[h] = probs
        heads.append(dot(v_t[h * HALF : (h + 1) * HALF], probs))
    heads = jnp.concatenate(heads, 0)
    low_t[pl.ds(at, 128)] = heads.astype(BF16)
    low[:, pl.ds(at, 128)] = heads.T.astype(BF16)

    @pl.when(j == pl.num_programs(0) - 1)
    def _():
        copies[3].start()
        copies[4].start()
        mid_ref[...] = stream[...] + dot(low[...], wproj_ref[...]) + vec_ref[4:5]
        for copy in copies + loads:
            copy.wait()


def attend(sample, lengths, pieces, table, vec, w_qkv, w_proj, fetches):
    rows = len(pieces) * (pieces[0].shape[0] - 16)
    width = w_proj.shape[0]
    fetch = len(fetches)
    saved = [
        ((rows, width), F32),
        ((rows, 3 * width), BF16),
        ((width, rows), BF16),
        ((rows, width), BF16),
        ((width, rows), BF16),
    ]
    stream, joined, attn_in_t, low, low_t = [pltpu.VMEM(*a) for a in saved]
    mid, ids, probs, *rest = pl.pallas_call(
        functools.partial(attend_kernel, sample, fetch),
        grid=(HEADS // 2,),
        in_specs=[SMEM] + [VMEM] * 8 + [ANY] * fetch,
        out_specs=[VMEM] * 2 + [pl.BlockSpec((2, rows, rows), lambda j: (j, 0, 0))] + [VMEM] * fetch + [ANY] * 5,
        out_shape=[pltpu.VMEM((rows, width), F32), pltpu.VMEM((8, rows), F32), pltpu.HBM((HEADS, rows, rows), BF16)]
        + [pltpu.VMEM(a.shape, a.dtype) for a in fetches]
        + [pltpu.HBM(*a) for a in saved],
        scratch_shapes=[stream, joined, pltpu.VMEM((rows, width), BF16), attn_in_t, low, low_t]
        + [pltpu.SemaphoreType.DMA((5,)), pltpu.SemaphoreType.DMA((max(fetch, 1),))],
        compiler_params=params(14),
        cost_estimate=cost(1),
        name=f"attend_{sample}",
    )(lengths, *near(*pieces, table, vec, w_qkv, w_proj), *far(*fetches))
    return mid, ids, probs, rest[:fetch], rest[fetch:]


def mlp_kernel(packed, last, x0_ref, x1_ref, c0_ref, c1_ref, c2_ref, c3_ref, w1_ref, w2_ref, vec_ref, *rest):
    cots = (c0_ref, c1_ref, c2_ref, c3_ref)
    if last:
        held, wproj_ref, rest = rest[:5], rest[5], rest[6:]
        db1_ref, gone_ref, small_ref, wproj_out, gmid_ref = rest[:5]
        mixed_refs, rest = rest[5:9], rest[9:]
    else:
        held, db1_ref, rest = rest[:5], rest[5], rest[6:]
    dw_refs, (act, gpre, result, keep, send, sems) = rest[:2], rest[2:]
    mlp_in, mlp_in_t, gt, acc, gacc = held
    j = pl.program_id(0)
    xs = (x0_ref, x1_ref)
    rows, width = x0_ref.shape
    piece = c0_ref.shape[1]
    columns = result.shape[1]
    tile = 2 * piece
    per_sample = rows // tile
    tiles = len(xs) * per_sample
    me = place()[0]
    chunk = (j + 2 * last) ^ (me // 8) if packed else j + 2 * last

    @pl.when(j == 0)
    def _():
        if last:
            pltpu.make_async_copy(wproj_ref, wproj_out, sems.at[2]).start()
            return
        for i in range(tiles):
            s, t = i // per_sample, i % per_sample
            here = slice(i * tile, (i + 1) * tile)
            normed, _ = normalize(xs[s][t * tile : (t + 1) * tile])
            value = (normed * vec_ref[5:6] + vec_ref[6:7]).astype(BF16)
            mlp_in[here] = value
            mlp_in_t[:, here] = value.T
            for p in range(2):
                gt[i * tile + p * piece : i * tile + (p + 1) * piece] = cots[2 * t + p][s]
            acc[here] = jnp.zeros((tile, width), F32)
            gacc[here] = jnp.zeros((tile, width), F32)

    at = pl.ds(pl.multiple_of(chunk * columns, columns), columns)
    b1 = vec_ref[pl.ds(8 + chunk, 1)]
    db1 = jnp.zeros((1, columns), F32)
    for i in range(tiles):
        here = slice(i * tile, (i + 1) * tile)
        value, slope = gelu_both(dot(mlp_in[here], w1_ref[:, at]) + b1)
        value = value.astype(BF16)
        act[here] = value
        g = (dot(gt[here], w2_ref[at], NT) * slope).astype(BF16)
        gpre[here] = g
        db1 = db1 + row_sum(g)
        acc[here] += dot(value, w2_ref[at])
        gacc[here] += dot(g, w1_ref[:, at], NT)
    db1_ref[pl.ds(chunk % 2, 1)] = db1
    if packed:
        order = Z_FIRST if last else X_FIRST
        result[...] = dot(mlp_in_t[...], gpre[...])
        slot = pl.multiple_of((chunk % 2) * 6 * PER, 16)
        for e in range(2):
            store_packed(keep, send, order, me, result, slot + e * 12 * PER, e * Z1)
        result[...] = dot(act[...], gt[...], TN)
        for position in range(16):
            owner = relative(position, order)
            if owner & Z0:
                continue
            start = pl.multiple_of(((me % 8) ^ (owner % 8)) * 96, 8)
            where = position % 8 + j * 2 ** (3 - order.index(Z0))
            for c in range(width // 128):
                part = result[pl.ds(start, 96), c * 128 : (c + 1) * 128].astype(BF16)
                (keep, send)[position // 8][where, 576 + c * 96 : 672 + c * 96] = part
    else:
        dw_refs[0][...] = dot(mlp_in_t[...], gpre[...])
        dw_refs[1][...] = dot(act[...], gt[...], TN)

    @pl.when(j == pl.num_programs(0) - 1)
    def _():
        copies = []
        if packed:
            copies = [pltpu.make_async_copy(a, b, sems.at[i]) for i, (a, b) in enumerate(zip((send, keep), dw_refs[::-1]))]
            for copy in copies:
                copy.start()
        if last:
            sums = [jnp.zeros((1, width), F32) for _ in range(4)]
            for i in range(tiles):
                s, t = i // per_sample, i % per_sample
                here = slice(i * tile, (i + 1) * tile)
                x = xs[s][t * tile : (t + 1) * tile]
                normed, inverse = normalize(x)
                mixed = (x + acc[here] + vec_ref[7:8]).astype(BF16)
                for p in range(2):
                    mixed_refs[2 * t + p][s] = mixed[p * piece : (p + 1) * piece]
                cot = gt[here].astype(F32)
                g = gacc[here]
                gmid = cot + normalize_back(g * vec_ref[5:6], normed, inverse)
                gmid_ref[s, t * tile : (t + 1) * tile] = gmid
                low = gmid.astype(BF16)
                gone_ref[s, t * tile : (t + 1) * tile] = low
                sums = [a + row_sum(b) for a, b in zip(sums, (g * normed, g, cot, low))]
            for k in range(4):
                small_ref[k : k + 1] = sums[k]
            copies.append(pltpu.make_async_copy(wproj_ref, wproj_out, sems.at[2]))
        for copy in copies:
            copy.wait()


def mlp(packed, last, x0, x1, cots, w1, w2, vec, held, w_proj):
    rows, width = x0.shape
    hidden = w1.shape[1]
    columns = width
    tokens = 2 * rows
    if packed:
        grads = [(pltpu.HBM((8, 48 * PER, 128), BF16), ANY)] * 2
        buffers = [pltpu.VMEM((8, 48 * PER, 128), BF16)] * 2
    else:
        grads = [
            (pltpu.HBM((width, hidden // 2), F32), pl.BlockSpec((width, columns), lambda j: (0, j))),
            (pltpu.HBM((hidden // 2, width), F32), pl.BlockSpec((columns, width), lambda j: (j, 0))),
        ]
        buffers = [pltpu.VMEM((8, 16, 128), BF16)] * 2
    states = [
        ((tokens, width), BF16),
        ((width, tokens), BF16),
        ((tokens, width), BF16),
        ((tokens, width), F32),
        ((tokens, width), F32),
    ]
    if last:
        outs = [pltpu.VMEM((2, columns), F32), pltpu.VMEM((2, rows, width), BF16), pltpu.VMEM((4, width), F32)]
        outs += [pltpu.VMEM(w_proj.shape, BF16), pltpu.HBM((2, rows, width), F32)]
        specs = [VMEM] * 4 + [pl.BlockSpec((2, rows, width), lambda j: (0, 0, 0))]
        outs += [pltpu.VMEM(c.shape, BF16) for c in cots]
        specs += [VMEM] * len(cots)
    else:
        outs = [pltpu.VMEM(*a) for a in states] + [pltpu.VMEM((2, columns), F32)]
        specs = [VMEM] * 6
    return pl.pallas_call(
        functools.partial(mlp_kernel, packed, last),
        grid=(2,),
        in_specs=[VMEM] * 9 + ([VMEM] * 5 + [ANY] if last else []),
        out_specs=specs + [g[1] for g in grads],
        out_shape=outs + [g[0] for g in grads],
        scratch_shapes=[
            pltpu.VMEM((tokens, columns), BF16),
            pltpu.VMEM((tokens, columns), BF16),
            pltpu.VMEM((width, columns), F32),
            *buffers,
            pltpu.SemaphoreType.DMA((3,)),
        ],
        compiler_params=params((22 if last else 17) if packed else 28),
        cost_estimate=cost(1),
        name=f"mlp_{int(last)}",
    )(*near(x0, x1, *cots, w1, w2, vec), *(near(*held) + far(w_proj) if last else []))


def attend_back_kernel(
    sample, fetch, gone_ref, wproj_ref, low_ref, q_ref, k_ref, v_ref, probs_ref, *rest
):
    fetches, gjoined_ref, fetched, (gatt, delta, sems) = rest[:fetch], rest[fetch], rest[fetch + 1 : -3], rest[-3:]
    loads = [pltpu.make_async_copy(a, b, sems.at[i]) for i, (a, b) in enumerate(zip(fetches, fetched))]
    j = pl.program_id(0)
    rows, width = low_ref.shape

    @pl.when(j == 0)
    def _():
        for load in loads:
            load.start()
        grad = dot(gone_ref[sample], wproj_ref[...], NT).astype(BF16)
        gatt[...] = grad
        product = grad.astype(F32) * low_ref[...].astype(F32)
        high = product.astype(BF16)
        rest = (product - high.astype(F32)).astype(BF16)
        heads = lax.broadcasted_iota(jnp.int32, (16, width), 0)
        owner = lax.broadcasted_iota(jnp.int32, (16, width), 1) // HALF
        pick = (heads == owner).astype(F32).astype(BF16)
        delta[...] = dot(pick, high, NT) + dot(pick, rest, NT)

    at = pl.multiple_of(j * 128, 128)
    q, k, v = q_ref[...], k_ref[...], v_ref[...]
    g = gatt[:, pl.ds(at, 128)]
    k_t = k.T
    left = lax.broadcasted_iota(jnp.int32, (rows, 128), 1) < HALF
    g_q, g_k, g_v = [], [], []
    for h in range(2):
        g_h = jnp.where(left == (h == 0), g, jnp.zeros_like(g))
        probs = probs_ref[h]
        back = dot(v, g_h, NT) - delta[pl.ds(2 * j + h, 1), :]
        scores = (probs.astype(F32) * back).astype(BF16)
        g_v.append(dot(probs, g))
        g_k.append(dot(scores, q))
        g_q.append(dot(k_t[h * HALF : (h + 1) * HALF], scores))
    gjoined_ref[:, pl.ds(at, 128)] = (jnp.concatenate(g_q, 0).T * HALF**-0.5).astype(BF16)
    at_k = pl.multiple_of(width + j * 128, 128)
    at_v = pl.multiple_of(2 * width + j * 128, 128)
    gjoined_ref[:, pl.ds(at_k, 128)] = jnp.where(left, g_k[0], g_k[1]).astype(BF16)
    gjoined_ref[:, pl.ds(at_v, 128)] = jnp.where(left, g_v[0], g_v[1]).astype(BF16)

    @pl.when(j == pl.num_programs(0) - 1)
    def _():
        for load in loads:
            load.wait()


def attend_back(sample, gone, w_proj, low, joined, probs, fetches):
    rows, width = low.shape
    pairs = HEADS // 2
    third = lambda c: pl.BlockSpec((rows, 128), lambda j: (0, c * pairs + j))
    joined, probs, low = far(joined, probs, low)
    fetch = len(fetches)
    return pl.pallas_call(
        functools.partial(attend_back_kernel, sample, fetch),
        grid=(pairs,),
        in_specs=[VMEM] * 2
        + [pl.BlockSpec((rows, width), lambda j: (0, 0))]
        + [third(0), third(1), third(2), pl.BlockSpec((2, rows, rows), lambda j: (j, 0, 0))]
        + [ANY] * fetch,
        out_specs=[VMEM] * (1 + fetch),
        out_shape=[pltpu.VMEM((rows, 3 * width), BF16)] + [pltpu.VMEM(a.shape, a.dtype) for a in fetches],
        scratch_shapes=[
            pltpu.VMEM((rows, width), BF16),
            pltpu.VMEM((16, rows), F32),
            pltpu.SemaphoreType.DMA((max(fetch, 1),)),
        ],
        compiler_params=params(12),
        cost_estimate=cost(1),
        name=f"attend_back_{sample}",
    )(*near(gone, w_proj), low, joined, joined, joined, probs, *far(*fetches))


def weights_kernel(packed, fetch, g0_ref, g1_ref, gone_ref, a0_ref, a1_ref, l0_ref, l1_ref, *rest):
    fetches, sums_ref, fetched = rest[:fetch], rest[fetch], rest[fetch + 1 : 2 * fetch + 1]
    dw_refs, (result, sems) = rest[2 * fetch + 1 : -2], rest[-2:]
    loads = [pltpu.make_async_copy(a, b, sems.at[i]) for i, (a, b) in enumerate(zip(fetches, fetched))]
    j = pl.program_id(0)
    width = a0_ref.shape[0]
    me = place()[0]

    def put(which, value):
        if packed:
            result[...] = value
            order = (X_FIRST, Z_FIRST)[which] + (Z1,)
            store_packed(*dw_refs[2 * which : 2 * which + 2], order, me, result)
        else:
            dw_refs[which][...] = value

    def columns(c):
        at = slice(c * width, (c + 1) * width)
        put(c // 2, dot(a0_ref[...], g0_ref[:, at]) + dot(a1_ref[...], g1_ref[:, at]))
        sums_ref[c : c + 1] = row_sum(g0_ref[:, at]) + row_sum(g1_ref[:, at])

    @pl.when(j == 0)
    def _():
        for load in loads:
            load.start()
        put(1, dot(l0_ref[...], gone_ref[0]) + dot(l1_ref[...], gone_ref[1]))

    for c in range(3):
        pl.when(j == 3 - c)(functools.partial(columns, c))

    @pl.when(j == 3)
    def _():
        for load in loads:
            load.wait()


def weights(packed, g0, g1, gone, a0, a1, low0, low1, fetches):
    width, rows = a0.shape
    fetch = len(fetches)
    late = lambda j: (0, jnp.minimum(3 - j, 1), 0)
    early = lambda j: (0, jnp.maximum(1 - j, 0), 0)
    if packed:
        grad = lambda index: (pltpu.HBM((16, 12 * PER, 128), BF16), pl.BlockSpec((16, 6 * PER, 128), index))
        grads = [grad(late)] * 2 + [grad(early)] * 2
    else:
        grad = lambda index: (
            pltpu.HBM((width, 2 * width), F32),
            pl.BlockSpec((width, width), lambda j: index(j)[:2]),
        )
        grads = [grad(late), grad(early)]
    return pl.pallas_call(
        functools.partial(weights_kernel, packed, fetch),
        grid=(4,),
        in_specs=[VMEM] * 7 + [ANY] * fetch,
        out_specs=[VMEM] * (1 + fetch) + [g[1] for g in grads],
        out_shape=[pltpu.VMEM((8, width), F32)]
        + [pltpu.VMEM(a.shape, a.dtype) for a in fetches]
        + [g[0] for g in grads],
        scratch_shapes=[pltpu.VMEM((width, width), F32), pltpu.SemaphoreType.DMA((max(fetch, 1),))],
        compiler_params=params(16 if packed else 24),
        cost_estimate=cost(1),
        name="weights",
    )(*near(g0, g1, gone, a0, a1, low0, low1), *far(*fetches))


def finish_kernel(
    packed, g0_ref, g1_ref, w_ref, x0_ref, x1_ref, gmid_ref, ids0_ref, ids1_ref, vec_ref, small_ref, sums_ref,
    db1a_ref, db1b_ref, *rest,
):
    pgrad_refs, dw_refs, (grad_t, hot, result) = rest[:4], rest[4:-3], rest[-3:]
    xs, gs, ids = (x0_ref, x1_ref), (g0_ref, g1_ref), (ids0_ref, ids1_ref)
    rows, width = x0_ref.shape
    positions = hot.shape[0]
    piece = pgrad_refs[0].shape[1]
    tile = 2 * piece
    me = place()[0]
    g_gain = jnp.zeros((1, width), F32)
    g_bias = jnp.zeros((1, width), F32)
    for i in range(4):
        s, t = i // 2, i % 2
        cut = slice(t * tile, (t + 1) * tile)
        here = slice(i * tile, (i + 1) * tile)
        grad = dot(gs[s][cut], w_ref[...], NT)
        normed, inverse = normalize(xs[s][cut])
        total = gmid_ref[s, cut] + normalize_back(grad * vec_ref[0:1], normed, inverse)
        low = total.astype(BF16)
        for p in range(2):
            pgrad_refs[2 * t + p][s] = low[p * piece : (p + 1) * piece]
        grad_t[:, here] = low.T
        g_gain = g_gain + row_sum(grad * normed)
        g_bias = g_bias + row_sum(grad)
        wanted = ids[s][0:1, cut].astype(jnp.int32)
        iota = lax.broadcasted_iota(jnp.int32, (positions, tile), 0)
        hot[:, here] = (iota == wanted).astype(F32).astype(BF16)
    few = [g_gain, g_bias, sums_ref[0:1], sums_ref[2:3], small_ref[3:4], small_ref[0:3]]
    few = jnp.concatenate(few + [jnp.zeros((120, width), F32)], 0).T
    result[:, 0:positions] = dot(grad_t[...], hot[...], NT)
    result[:, positions:] = few
    if packed:
        half = (me // Z1) % 2
        a, b = db1a_ref[...], db1b_ref[...]
        sums = jnp.concatenate([jnp.where(half == 0, a, b), jnp.where(half == 0, b, a)], 0)
        share = 96
        for owner in range(32):
            c, start = owner // 8, owner % 8 * share
            row = jnp.concatenate([jnp.zeros((1, 16), F32), sums[c : c + 1, start : start + share], jnp.zeros((1, 16), F32)], 1)
            result[owner * PER : owner * PER + 1, positions:] += row
        store_packed(*dw_refs, Z_FIRST + (Z1,), me, result)
    else:
        dw_refs[0][...] = result[...]


def finish(packed, g0, g1, w_qkv, x0, x1, gmid, ids0, ids1, vec, small, sums, db1a, db1b, parts, positions):
    rows, width = x0.shape
    columns = positions + 128
    pgrad = [pltpu.VMEM((2, rows // parts, width), BF16)] * parts
    if packed:
        grads = [pltpu.VMEM((16, PER * columns // 128, 128), BF16)] * 2
    else:
        grads = [pltpu.VMEM((width, columns), F32)]
    return pl.pallas_call(
        functools.partial(finish_kernel, packed),
        in_specs=[VMEM] * 13,
        out_specs=[VMEM] * (parts + len(grads)),
        out_shape=pgrad + grads,
        scratch_shapes=[
            pltpu.VMEM((width, 2 * rows), BF16),
            pltpu.VMEM((positions, 2 * rows), BF16),
            pltpu.VMEM((width, columns), F32),
        ],
        compiler_params=params(16),
        cost_estimate=cost(1),
        name="finish",
    )(*near(g0, g1, w_qkv, x0, x1, gmid, ids0, ids1, vec, small, sums, db1a, db1b))


def swap_bit(x, bit, count):
    return lax.ppermute(x, AXES, [(d, d ^ bit) for d in range(count)])


def add(arrays):
    return sum(a.astype(F32) for a in arrays)


def stage(streams, bit, count):
    far_half = [[a[a.shape[0] // 2 :] for a in held] for held in streams]
    send = [add(held).astype(BF16) for held in far_half]
    got = swap_bit(send[0] if len(send) == 1 else jnp.concatenate(send, 1), bit, count)
    row, result = 0, []
    for held in streams:
        rows = held[0].shape[1]
        part = got if len(streams) == 1 else got[:, row : row + rows]
        result.append([a[: a.shape[0] // 2] for a in held] + [part])
        row += rows
    return result


def tiles_kernel(counts, layout, *refs):
    n = sum(counts)
    held, outs, result = refs[:n], refs[n:-1], refs[-1]
    row, at = 0, 0
    for count in counts:
        rows = held[at].shape[1]
        result[row : row + rows] = add([ref[0] for ref in held[at : at + count]])
        row, at = row + rows, at + count
    layout(result, outs)


def put_tiles(result, row, out, columns):
    for c in range(columns // 128):
        out[:, c * 128 : (c + 1) * 128] = result[row + c * PER : row + (c + 1) * PER]


def hidden_layout(result, outs):
    dw1, dw2 = outs
    n = 12 * PER
    low = (place()[0] // Z1) % 2 == 0
    first, second, other = 0, 4 * n, 8 * n
    mine = result[first : first + n] + result[other + n : other + 2 * n]
    theirs = result[second : second + n] + result[other : other + n]
    halves = jnp.where(low, mine, theirs), jnp.where(low, theirs, mine)
    for e, half in enumerate(halves):
        for c in range(12):
            dw1[:, (12 * e + c) * 128 : (12 * e + c + 1) * 128] = half[c * PER : (c + 1) * PER]
    for c in range(6):
        rows = [result[at + 2 * n + c * 96 : at + 2 * n + (c + 1) * 96] for at in (first, other)]
        dw2[:, c * 128 : (c + 1) * 128] = rows[0] + rows[1]


def rest_layout(result, outs):
    dwqkv, dwproj, table, *few = outs
    n = 6 * PER
    put_tiles(result, 0, dwqkv, dwqkv.shape[1])
    put_tiles(result, 3 * n, dwproj, dwproj.shape[1])
    put_tiles(result, 4 * n, table, table.shape[1])
    at = 4 * n + table.shape[1] // 128 * PER
    tile = result[at : at + PER]
    for k in range(8):
        few[k][...] = jnp.sum(jnp.where(lax.broadcasted_iota(jnp.int32, (PER, 128), 1) == k, tile, 0.0), axis=1)
    few[8][...] = tile[0, 16:112]


def tiles(streams, layout, outs, name):
    arrays = [a for held in streams for a in held]
    rows = sum(held[0].shape[1] for held in streams)
    first = lambda a: pl.BlockSpec((1,) + a.shape[1:], lambda i: (0, 0, 0))
    return pl.pallas_call(
        functools.partial(tiles_kernel, [len(held) for held in streams], layout),
        grid=(1,),
        in_specs=[first(a) for a in arrays],
        out_specs=[pl.BlockSpec(shape, lambda i, n=len(shape): (0,) * n) for shape in outs],
        out_shape=[jax.ShapeDtypeStruct(shape, F32) for shape in outs],
        scratch_shapes=[pltpu.VMEM((rows, 128), F32)],
        compiler_params=params(24),
        cost_estimate=cost(1),
        name=name,
    )(*arrays)


def shards(
    patches, pos_ids, lengths, pos_table, ln1_gain, ln1_bias, w_qkv, q_bias, v_bias, w_proj, proj_bias,
    ln2_gain, ln2_bias, w_fc1, fc1_bias, w_fc2, fc2_bias, cotangent, *, wide, parts,
):
    _, piece, width = patches.shape
    hidden, positions = w_fc1.shape[1], pos_table.shape[1]
    count = wide * parts
    packed = wide == 8 and parts == 4
    across = lambda a: [a[0]] + [
        lax.ppermute(b, "blk", [(d, d ^ k) for d in range(parts)]) for k, b in enumerate(a) if k
    ]

    xs = across(part(0, parts, pos_ids, patches))
    ys = across(part(1, parts, pos_ids, after(patches, xs[1])))
    cots = across(spread(parts, after(cotangent, ys[1])))
    vectors = (ln1_gain, ln1_bias, q_bias, v_bias, proj_bias, ln2_gain, ln2_bias, fc2_bias, fc1_bias)
    vec, table, wqkv, wproj = warm(vectors, (pos_table, w_qkv, w_proj))

    xs[0] = after(xs[0], cots[1])
    mid0, ids0, probs0, _, (x0, joined0, in0, low0, low0_t) = attend(0, lengths, xs, table, vec, wqkv, wproj, ())
    mid1, ids1, probs1, (w1, w2), (x1, joined1, in1, low1, low1_t) = attend(
        1, lengths, ys, table, vec, wqkv, wproj, (w_fc1, w_fc2)
    )
    *held, db1a, keep1, send1 = mlp(packed, False, mid0, mid1, cots, w1, w2, vec, None, w_proj)
    db1b, gone, small, wproj, gmid, *rest = mlp(packed, True, mid0, mid1, cots, w1, w2, vec, held, w_proj)
    mixed, (keep2, send2) = across(rest[:parts]), rest[parts:]
    if packed:
        hid1 = [[keep1, swap_bit(send1, CORE, count)]]
        gone = after(gone, hid1[0][1])
        hid1 = stage(hid1, X, count)
        hid2 = [[keep2, swap_bit(send2, CORE, count)]]
    g0, *_ = attend_back(0, gone, wproj, low0, joined0, probs0, ())
    if packed:
        gone = after(gone, g0, hid2[0][1])
        hid2 = stage(hid2, Z0, count)
    g1, in0, in1, low0_t, low1_t = attend_back(1, gone, wproj, low1, joined1, probs1, (in0, in1, low0_t, low1_t))
    sums, wqkv, x0, x1, gmid, *dwa = weights(packed, g0, g1, gone, in0, in1, low0_t, low1_t, (w_qkv, x0, x1, gmid))
    if packed:
        sums = after(sums, hid1[0][-1])
        hid1 = stage(hid1, Y, count)
        dwa1 = [[dwa[0], swap_bit(dwa[1], CORE, count)]]
        dwa2 = [[dwa[2], swap_bit(dwa[3], CORE, count)]]
        sums = after(sums, mixed[-1])
    out = finish(packed, g0, g1, wqkv, x0, x1, gmid, ids0, ids1, vec, small, sums, db1a, db1b, parts, positions)
    pgrad, grads = across(out[:parts]), out[parts:]
    mixed, pgrad = gather(mixed), gather(pgrad)
    if packed:
        dwa2.append([grads[0], swap_bit(grads[1], CORE, count)])
        for i in range(4):
            if i == 1:
                hid1 = stage(hid1, Z0, count)
            if i < 2:
                hid2 = stage(hid2, (X, Y)[i], count)
            dwa1 = stage(dwa1, (X_FIRST + (Z1,))[i + 1], count)
            dwa2 = stage(dwa2, (Z_FIRST + (Z1,))[i + 1], count)
        hid1, hid2, n = hid1[0], hid2[0], 12 * PER
        send = jnp.concatenate([add(hid1)[:, n : 2 * n], add(hid2)[:, n:]], 1).astype(BF16)
        last = [swap_bit(send, Z1, count)]
        dw1, dw2 = tiles(
            [hid1, hid2, last], hidden_layout, [(width // count, hidden), (hidden // count, width)], "hidden"
        )
        shapes = [(width // count, n) for n in (3 * width, width, positions)]
        shapes += [(width // count,)] * 8 + [(hidden // count,)]
        dwqkv, dwproj, table, *few = tiles(dwa1 + dwa2, rest_layout, shapes, "rest")
    else:
        share = lambda a: lax.psum_scatter(a.astype(BF16), AXES, scatter_dimension=0, tiled=True).astype(F32)
        dw1 = share(jnp.concatenate([keep1, keep2], 1))
        dw2 = share(jnp.concatenate([send1, send2], 0))
        dwa, dwb, misc = share(dwa[0]), share(dwa[1]), share(grads[0])
        dwqkv, dwproj = jnp.concatenate([dwa, dwb[:, :width]], 1), dwb[:, width:]
        table, few = misc[:, :positions], [misc[:, positions + k] for k in range(8)]
        few.append(share(jnp.concatenate([db1a, db1b], 0).reshape(-1)))
    (g_gain1, g_bias1, g_q, g_v, g_proj, g_gain2, g_bias2, g_fc2, g_fc1) = few
    return (
        mixed, pgrad, table, g_gain1, g_bias1, dwqkv, g_q, g_v, dwproj, g_proj, g_gain2, g_bias2,
        dw1, g_fc1, dw2, g_fc2,
    )


def solution(mesh):
    wide, parts = mesh.shape["wide"], mesh.shape["blk"]
    tokens = P("wide", "blk", None)
    in_specs = (tokens, P("wide", "blk"), P("wide")) + (P(),) * 14 + (tokens,)
    vector, matrix = P(AXES), P(AXES, None)
    out_specs = (
        tokens, tokens, matrix, vector, vector, matrix, vector, vector, matrix, vector, vector, vector,
        matrix, vector, matrix, vector,
    )
    return jax.shard_map(
        functools.partial(shards, wide=wide, parts=parts),
        mesh=mesh, in_specs=in_specs, out_specs=out_specs, check_vma=False,
    )
```

```python
import functools

import jax
import jax.numpy as jnp
from jax import lax
from jax.experimental import pallas as pl
from jax.experimental.pallas import tpu as pltpu
from jax.sharding import PartitionSpec as P

HEADS = 12
HALF = 64
F32, BF16 = jnp.float32, jnp.bfloat16
NN = (((1,), (0,)), ((), ()))
NT = (((1,), (1,)), ((), ()))
TN = (((0,), (0,)), ((), ()))
EPS = 1e-6
MASKED = -1e30
AXES = ("wide", "blk")
MIB = 2**20
CORE, Y, X, Z0, Z1 = 1, 2, 4, 8, 16
X_FIRST = (CORE, X, Y, Z0)
Z_FIRST = (CORE, Z0, X, Y)
PER = 24
LIGHT = pl.CostEstimate(flops=1, bytes_accessed=1, transcendentals=0)
HEAVY = pl.CostEstimate(flops=10**11, bytes_accessed=1, transcendentals=0)
VMEM = pl.BlockSpec(memory_space=pltpu.VMEM)
ANY = pl.BlockSpec(memory_space=pl.ANY)
SMEM = pl.BlockSpec(memory_space=pltpu.SMEM)


def dot(a, b, dims=NN):
    return lax.dot_general(a, b, dims, preferred_element_type=F32)


def near(*arrays):
    return [pltpu.with_memory_space_constraint(a, pltpu.VMEM) for a in arrays]


def far(*arrays):
    return [pltpu.with_memory_space_constraint(a, pltpu.HBM) for a in arrays]


def call(body, tokens, ops, in_specs, vmem, aliases=None, cost=LIGHT, **rest):
    n = len(tokens)
    return pl.pallas_call(
        lambda *refs: body(*refs[n:]),
        in_specs=[ANY] * n + in_specs,
        input_output_aliases={n + a: b for a, b in (aliases or {}).items()},
        compiler_params=pltpu.CompilerParams(vmem_limit_bytes=int(vmem * MIB)),
        cost_estimate=cost,
        **rest,
    )(*tokens, *ops)


def place():
    lane = lax.axis_index("blk")
    return lax.axis_index("wide") * lax.axis_size("blk") + lane, lane


def normalize(x):
    center = x - jnp.mean(x, axis=-1, keepdims=True)
    inverse = lax.rsqrt(jnp.mean(center * center, axis=-1, keepdims=True) + EPS)
    return center * inverse, inverse


def normalize_back(g, normed, inverse):
    return inverse * (
        g - jnp.mean(g, axis=-1, keepdims=True) - normed * jnp.mean(g * normed, axis=-1, keepdims=True)
    )


def gelu_both(x):
    cdf = 0.5 + 0.5 * lax.erf(x * 0.7071067811865476)
    return x * cdf, cdf + x * (jnp.exp(x * x * -0.5) * 0.3989422804014327)


def row_sum(x):
    return jnp.sum(x.astype(F32), axis=0, keepdims=True)


def relative(position, order):
    return sum(bit for i, bit in enumerate(order) if (position >> (len(order) - 1 - i)) & 1)


def store_packed(keep_ref, send_ref, order, me, result_ref, base=0, extra=0, columns=None):
    half = 2 ** (len(order) - 1)
    first, last = columns or (0, result_ref.shape[1])
    for position in range(2 * half):
        ref = (keep_ref, send_ref)[position // half]
        start = pl.multiple_of((me ^ (relative(position, order) | extra)) * PER, 8)
        for c in range((last - first) // 256):
            two = [result_ref[pl.ds(start, PER), first + (2 * c + i) * 128 : first + (2 * c + i + 1) * 128] for i in range(2)]
            here = pl.ds(base + 2 * c * PER, 2 * PER)
            ref[position % half, here] = jnp.concatenate(two, 0).astype(BF16)


def prepare_kernel(patches_ref, cot_ref, ids_hbm, *refs):
    vectors, big, refs = refs[:9], refs[9:12], refs[12:]
    first, second, cots, vec_ref, loaded = refs[:3], refs[3:6], refs[6:9], refs[9], refs[10:13]
    ids_ref, raw, sems = refs[13], refs[14:-1], refs[-1]
    piece, width = patches_ref.shape[1:]
    lane_me = place()[1]
    copies = []

    def start(a, b):
        copies.append(pltpu.make_async_copy(a, b, sems.at[len(copies)]))
        copies[-1].start()
        return copies[-1]

    lay = lambda own, core, far_own: (own, core.at[0], far_own, core.at[1])
    few = [start(ids_hbm, ids_ref)]
    for s, outs in enumerate((first, second)):
        for k, out in enumerate(lay(*outs)):
            start(patches_ref.at[2 * (lane_me ^ k) + s], out.at[0:piece])
    few += [start(a, b) for a, b in zip(vectors, raw)]
    for a, b in zip(big, loaded):
        start(a, b)
    for k, out in enumerate(lay(*cots)):
        start(cot_ref.at[pl.ds(2 * (lane_me ^ k), 2)], out)
    for copy in few:
        copy.wait()
    for s, outs in enumerate((first, second)):
        for k, out in enumerate(lay(*outs)):
            ids = ids_ref[pl.ds(2 * (lane_me ^ k) + s, 1)]
            row = jnp.concatenate([ids >> 8, ids & 255, jnp.zeros((1, width - 2 * piece), jnp.int32)], 1)
            out[piece : piece + 16] = jnp.broadcast_to(row.astype(F32), (16, width)).astype(BF16)
    row = 0
    for ref in raw:
        for k in range(ref.shape[0] // width):
            vec_ref[row : row + 1] = ref[k * width : (k + 1) * width].astype(F32).reshape(1, width)
            row += 1
    vec_ref[row:] = jnp.zeros((vec_ref.shape[0] - row, width), F32)
    for i, copy in enumerate(copies):
        if not (i == 0 or 9 <= i < 9 + len(vectors)):
            copy.wait()


def prepare(pos_ids, patches, cotangent, vectors, big):
    _, piece, width = patches.shape
    messages = []
    for shape in ((piece + 16, width), (piece + 16, width), (2, piece, width)):
        messages += [pltpu.VMEM(shape, BF16), pltpu.VMEM((2,) + shape, BF16), pltpu.VMEM(shape, BF16)]
    out = call(
        prepare_kernel,
        (),
        far(patches, cotangent, pos_ids, *vectors, *big),
        [ANY] * (3 + len(vectors) + len(big)),
        2,
        out_specs=[VMEM] * (10 + len(big)),
        out_shape=messages + [pltpu.VMEM((16, width), F32)] + [pltpu.VMEM(a.shape, a.dtype) for a in big],
        scratch_shapes=[
            pltpu.VMEM(pos_ids.shape, pos_ids.dtype),
            *[pltpu.VMEM(a.shape, a.dtype) for a in vectors],
            pltpu.SemaphoreType.DMA((13 + len(vectors) + len(big),)),
        ],
        name="prepare",
    )
    return out[:3], out[3:6], out[6:9], out[9:]


def join_kernel(a_ref, b_ref, out, sems):
    copies = [
        pltpu.make_async_copy(a_ref, out.at[0], sems.at[0]),
        pltpu.make_async_copy(b_ref.at[1], out.at[1], sems.at[1]),
    ]
    for copy in copies:
        copy.start()
    for copy in copies:
        copy.wait()


def join(tokens, far_own, got):
    return call(
        join_kernel,
        tokens,
        near(far_own, got),
        [VMEM] * 2,
        1,
        out_specs=VMEM,
        out_shape=pltpu.VMEM(got.shape, BF16),
        scratch_shapes=[pltpu.SemaphoreType.DMA((2,))],
        name="join",
    )


def gather_kernel(samples, *refs):
    sets, out, sems = refs[: 3 * samples], refs[-2], refs[-1]
    lane_me = place()[1]
    copies = []
    for s in range(samples):
        own, got, other = sets[3 * s : 3 * s + 3]
        for k, a in enumerate((own, got.at[0], other.at[0], other.at[1])):
            at = 2 * (lane_me ^ k) + s
            where = out.at[pl.ds(at, 2)] if samples == 1 else out.at[at]
            copies.append(pltpu.make_async_copy(a, where, sems.at[4 * s + k]))
            copies[-1].start()
    for copy in copies:
        copy.wait()


def gather(tokens, *sets):
    ops = near(*[a for one in sets for a in one])
    return call(
        functools.partial(gather_kernel, len(sets)),
        tokens,
        ops,
        [VMEM] * len(ops),
        1,
        out_specs=ANY,
        out_shape=pltpu.HBM((8,) + ops[0].shape[-2:], BF16),
        scratch_shapes=[pltpu.SemaphoreType.DMA((4 * len(sets),))],
        name="gather",
    )


def attend_kernel(
    sample, fetch, lengths_ref, own_ref, got_ref, other_ref, table_ref, vec_ref, wqkv_ref, wproj_ref, *rest
):
    fetches, rest = rest[:fetch], rest[fetch:]
    mid_ref, ids_ref, probs_ref, rest = rest[0], rest[1], rest[2], rest[3:]
    fetched, rest = rest[:fetch], rest[fetch:]
    outs, (stream, joined, attn_in, attn_in_t, low, low_t, sems, fetch_sems) = rest[:5], rest[5:]
    saved = (stream, joined, attn_in_t, low, low_t)
    copies = [pltpu.make_async_copy(a, b, sems.at[i]) for i, (a, b) in enumerate(zip(saved, outs))]
    loads = [pltpu.make_async_copy(a, b, fetch_sems.at[i]) for i, (a, b) in enumerate(zip(fetches, fetched))]
    j = pl.program_id(0)
    pieces = (own_ref, got_ref.at[0], other_ref.at[0], other_ref.at[1])
    rows, width = stream.shape
    piece = rows // len(pieces)

    @pl.when(j == 0)
    def _():
        for load in loads:
            load.start()
        positions = table_ref.shape[1]
        ids = []
        for k, ref in enumerate(pieces):
            coded = ref[piece : piece + 16].astype(F32)
            ids.append(coded[0:8, 0:piece] * 256.0 + coded[0:8, piece : 2 * piece])
        ids_ref[...] = jnp.concatenate(ids, 1)
        for k, ref in enumerate(pieces):
            here = slice(k * piece, (k + 1) * piece)
            column = jnp.broadcast_to(ids[k][0:1], (piece, piece)).T.astype(jnp.int32)
            iota = lax.broadcasted_iota(jnp.int32, (piece, piece), 1)
            onehot = jnp.concatenate([(column == iota + piece * c).astype(F32) for c in range(positions // piece)], 1)
            value = ref[0:piece].astype(F32) + dot(onehot.astype(BF16), table_ref[...], NT)
            stream[here] = value
            normed, _ = normalize(value)
            normed = (normed * vec_ref[0:1] + vec_ref[1:2]).astype(BF16)
            attn_in[here] = normed
            attn_in_t[:, here] = normed.T
        copies[0].start()
        copies[2].start()
        for c in range(3):
            cols = slice(c * width, (c + 1) * width)
            part = dot(attn_in[...], wqkv_ref[:, cols])
            if c != 1:
                part = part + vec_ref[2 + c // 2 : 3 + c // 2]
            part = part.astype(BF16)
            if c == 0:
                part = part * jnp.asarray(HALF**-0.5, BF16)
            joined[:, cols] = part
        copies[1].start()

    at = pl.multiple_of(j * 128, 128)
    q = joined[:, pl.ds(at, 128)]
    k = joined[:, pl.ds(pl.multiple_of(width + j * 128, 128), 128)]
    v = joined[:, pl.ds(pl.multiple_of(2 * width + j * 128, 128), 128)]
    v_t = v.T
    left = lax.broadcasted_iota(jnp.int32, (rows, 128), 1) < HALF
    part = lax.broadcasted_iota(jnp.int32, (piece, rows), 0)
    lane_me = place()[1]
    length = lengths_ref[2 * lane_me + sample]
    visible = jnp.concatenate([part + (lane_me ^ i) * piece < length for i in range(len(pieces))], 0)
    heads = []
    for h in range(2):
        q_h = jnp.where(left == (h == 0), q, jnp.zeros_like(q))
        scores = jnp.where(visible, dot(k, q_h, NT), MASKED)
        weights = jnp.exp(scores - jnp.max(scores, axis=0, keepdims=True))
        probs = (weights * (1.0 / jnp.sum(weights, axis=0, keepdims=True))).astype(BF16)
        probs_ref[h] = probs
        heads.append(dot(v_t[h * HALF : (h + 1) * HALF], probs))
    heads = jnp.concatenate(heads, 0)
    low_t[pl.ds(at, 128)] = heads.astype(BF16)
    low[:, pl.ds(at, 128)] = heads.T.astype(BF16)

    @pl.when(j == pl.num_programs(0) - 1)
    def _():
        copies[3].start()
        copies[4].start()
        mid_ref[...] = stream[...] + dot(low[...], wproj_ref[...]) + vec_ref[4:5]
        for copy in copies + loads:
            copy.wait()


def attend(sample, tokens, lengths, pieces, table, vec, w_qkv, w_proj, fetches):
    rows = 4 * (pieces[0].shape[0] - 16)
    width = w_proj.shape[0]
    fetch = len(fetches)
    saved = [
        ((rows, width), F32),
        ((rows, 3 * width), BF16),
        ((width, rows), BF16),
        ((rows, width), BF16),
        ((width, rows), BF16),
    ]
    stream, joined, attn_in_t, low, low_t = [pltpu.VMEM(*a) for a in saved]
    mid, ids, probs, *rest = call(
        functools.partial(attend_kernel, sample, fetch),
        tokens,
        [lengths, *near(*pieces, table, vec, w_qkv, w_proj), *far(*fetches)],
        [SMEM] + [VMEM] * 7 + [ANY] * fetch,
        13,
        grid=(HEADS // 2,),
        out_specs=[VMEM] * 2 + [pl.BlockSpec((2, rows, rows), lambda j: (j, 0, 0))] + [VMEM] * fetch + [ANY] * 5,
        out_shape=[pltpu.VMEM((rows, width), F32), pltpu.VMEM((8, rows), F32), pltpu.HBM((HEADS, rows, rows), BF16)]
        + [pltpu.VMEM(a.shape, a.dtype) for a in fetches]
        + [pltpu.HBM(*a) for a in saved],
        scratch_shapes=[stream, joined, pltpu.VMEM((rows, width), BF16), attn_in_t, low, low_t]
        + [pltpu.SemaphoreType.DMA((5,)), pltpu.SemaphoreType.DMA((max(fetch, 1),))],
        cost=HEAVY,
        name=f"attend_{sample}",
    )
    return mid, ids, probs, rest[:fetch], rest[fetch:]


def mlp_kernel(packed, begin, end, chunks, x0_ref, x1_ref, w1_ref, w2_ref, vec_ref, *rest):
    take = lambda n: (rest[:n], rest[n:])
    if begin:
        (own_ref, got_ref, other_ref), rest = take(3)
        cots = (own_ref, got_ref.at[0], other_ref.at[0], other_ref.at[1])
        (mlp_in, mlp_in_t, gt, acc, gacc), rest = take(5)
    else:
        (mlp_in, mlp_in_t, gt), rest = take(3)
        rest = rest[2:]
        if chunks[0] % 2:
            rest = rest[5:]
        if end:
            (wproj_ref,), rest = take(1)
        (acc, gacc), rest = take(2)
    (db1_ref, *dw_refs), rest = take(5 if packed else 3)
    if end:
        (gone_ref, small_ref, wproj_out, own, core, far_own), rest = take(6)
        mixed_refs = (own, core.at[0], far_own, core.at[1])
    act, gpre, result, sem = rest
    j = pl.program_id(0)
    xs = (x0_ref, x1_ref)
    rows, width = x0_ref.shape
    columns = result.shape[1]
    tile = rows // 2
    piece = tile // 2
    per_sample = rows // tile
    tiles = len(xs) * per_sample
    me = place()[0]
    chunk = (chunks[0] + j) ^ (me // 8) if packed else chunks[0] + j

    @pl.when(j == 0)
    def _():
        if end:
            pltpu.make_async_copy(wproj_ref, wproj_out, sem).start()
        if not begin:
            return
        for i in range(tiles):
            s, t = i // per_sample, i % per_sample
            here = slice(i * tile, (i + 1) * tile)
            normed, _ = normalize(xs[s][t * tile : (t + 1) * tile])
            value = (normed * vec_ref[5:6] + vec_ref[6:7]).astype(BF16)
            mlp_in[here] = value
            mlp_in_t[:, here] = value.T
            for p in range(2):
                gt[i * tile + p * piece : i * tile + (p + 1) * piece] = cots[2 * t + p][s]
            acc[here] = jnp.zeros((tile, width), F32)
            gacc[here] = jnp.zeros((tile, width), F32)

    at = pl.ds(pl.multiple_of(chunk * columns, columns), columns)
    b1 = vec_ref[pl.ds(8 + chunk, 1)]
    db1 = jnp.zeros((1, columns), F32)
    for i in range(tiles):
        here = slice(i * tile, (i + 1) * tile)
        value, slope = gelu_both(dot(mlp_in[here], w1_ref[:, at]) + b1)
        value = value.astype(BF16)
        act[here] = value
        g = (dot(gt[here], w2_ref[at], NT) * slope).astype(BF16)
        gpre[here] = g
        db1 = db1 + row_sum(g)
        acc[here] += dot(value, w2_ref[at])
        gacc[here] += dot(g, w1_ref[:, at], NT)
    db1_ref[pl.ds(chunk % 2, 1)] = db1
    if packed:
        keep, send, keep2, send2 = dw_refs
        result[...] = dot(mlp_in_t[...], gpre[...])
        slot = pl.multiple_of((chunk % 2) * 6 * PER, 16)
        for e in range(2):
            store_packed(keep, send, X_FIRST, me, result, slot + e * 12 * PER, e * Z1)
        result[...] = dot(act[...], gt[...], TN)
        for position in range(16):
            owner = relative(position, Z_FIRST)
            if owner & Z0:
                continue
            start = pl.multiple_of(((me % 8) ^ (owner % 8)) * 96, 8)
            where = position % 8 + (chunks[0] % 2 + j) * 2 ** (3 - Z_FIRST.index(Z0))
            (keep2, send2)[position // 8][where] = result[pl.ds(start, 96)].astype(BF16)
    else:
        dw_refs[0][...] = dot(mlp_in_t[...], gpre[...])
        dw_refs[1][...] = dot(act[...], gt[...], TN)

    @pl.when(j == pl.num_programs(0) - 1)
    def _():
        if not end:
            return
        sums = [jnp.zeros((1, width), F32) for _ in range(4)]
        for i in range(tiles):
            s, t = i // per_sample, i % per_sample
            here = slice(i * tile, (i + 1) * tile)
            x = xs[s][t * tile : (t + 1) * tile]
            normed, inverse = normalize(x)
            mixed = (x + acc[here] + vec_ref[7:8]).astype(BF16)
            for p in range(2):
                mixed_refs[2 * t + p][s] = mixed[p * piece : (p + 1) * piece]
            cot = gt[here].astype(F32)
            g = gacc[here]
            gmid = cot + normalize_back(g * vec_ref[5:6], normed, inverse)
            gacc[here] = gmid
            low = gmid.astype(BF16)
            gone_ref[s, t * tile : (t + 1) * tile] = low
            sums = [a + row_sum(b) for a, b in zip(sums, (g * normed, g, cot, low))]
        for k in range(4):
            small_ref[k : k + 1] = sums[k]
        pltpu.make_async_copy(wproj_ref, wproj_out, sem).wait()


def mlp(packed, tokens, chunks, x0, x1, w1, w2, vec, cots=None, held=None, grads=None, w_proj=None):
    begin, end = held is None, w_proj is not None
    rows, width = x0.shape
    hidden = w1.shape[1]
    columns = width
    length = 2 * rows
    sums = [pltpu.VMEM((length, width), F32)] * 2
    ops = near(x0, x1, w1, w2, vec)
    outs = list(sums)
    aliases = {}
    if begin:
        ops += near(*cots)
        outs = [pltpu.VMEM(s, BF16) for s in ((length, width), (width, length), (length, width))] + outs
    else:
        aliases = {len(ops) + 3: 0, len(ops) + 4: 1}
        ops += near(*held)
    at = len(outs)
    db1 = pltpu.VMEM((2, columns), F32)
    if packed:
        outs += [db1] + [pltpu.VMEM((8, 24 * PER, 128), BF16)] * 2 + [pltpu.VMEM((8, 96, width), BF16)] * 2
        dw_specs = [VMEM] * 5
        if grads is not None:
            aliases.update({len(ops) + i: at + i for i in range(5)})
            ops += near(*grads)
    else:
        whole = len(chunks) * columns
        outs += [db1, pltpu.HBM((width, whole), F32), pltpu.HBM((whole, width), F32)]
        dw_specs = [VMEM, pl.BlockSpec((width, columns), lambda j: (0, j)), pl.BlockSpec((columns, width), lambda j: (j, 0))]
    specs = [VMEM] * at + dw_specs
    in_specs = [VMEM] * len(ops)
    if end:
        ops += far(w_proj)
        in_specs += [ANY]
        outs += [pltpu.VMEM((2, rows, width), BF16), pltpu.VMEM((4, width), F32), pltpu.VMEM(w_proj.shape, BF16)]
        share = (2, rows // 4, width)
        outs += [pltpu.VMEM(share, BF16), pltpu.VMEM((2,) + share, BF16), pltpu.VMEM(share, BF16)]
        specs += [VMEM] * 6
    return call(
        functools.partial(mlp_kernel, packed, begin, end, chunks),
        tokens,
        ops,
        in_specs,
        12 if packed else 26,
        aliases,
        grid=(len(chunks),),
        out_specs=specs,
        out_shape=outs,
        scratch_shapes=[
            pltpu.VMEM((length, columns), BF16),
            pltpu.VMEM((length, columns), BF16),
            pltpu.VMEM((width, columns), F32),
            pltpu.SemaphoreType.DMA(()),
        ],
        cost=HEAVY,
        name=f"mlp_{chunks[0]}",
    )


def attend_back_kernel(sample, first, fetch, *rest):
    take = lambda n: (rest[:n], rest[n:])
    if first:
        (q_ref, k_ref, v_ref, probs_ref, _, gatt, delta), rest = take(7)
    else:
        (q_ref, k_ref, v_ref, probs_ref, gone_ref, wproj_ref, low_ref), rest = take(7)
    fetches, rest = take(fetch)
    (gjoined_ref,), rest = take(1)
    if not first:
        (gatt, delta), rest = take(2)
    fetched, (sems,) = take(fetch)
    loads = [pltpu.make_async_copy(a, b, sems.at[i]) for i, (a, b) in enumerate(zip(fetches, fetched))]
    j = pl.program_id(0)
    rows, width = gatt.shape

    @pl.when(j == 0)
    def _():
        for load in loads:
            load.start()
        if first:
            return
        grad = dot(gone_ref[sample], wproj_ref[...], NT).astype(BF16)
        gatt[...] = grad
        product = grad.astype(F32) * low_ref[...].astype(F32)
        high = product.astype(BF16)
        rest = (product - high.astype(F32)).astype(BF16)
        heads = lax.broadcasted_iota(jnp.int32, (16, width), 0)
        owner = lax.broadcasted_iota(jnp.int32, (16, width), 1) // HALF
        pick = (heads == owner).astype(F32).astype(BF16)
        delta[...] = dot(pick, high, NT) + dot(pick, rest, NT)

    pair = first + j
    at = pl.multiple_of(pair * 128, 128)
    q, k, v = q_ref[...], k_ref[...], v_ref[...]
    g = gatt[:, pl.ds(at, 128)]
    k_t = k.T
    left = lax.broadcasted_iota(jnp.int32, (rows, 128), 1) < HALF
    g_q, g_k, g_v = [], [], []
    for h in range(2):
        g_h = jnp.where(left == (h == 0), g, jnp.zeros_like(g))
        probs = probs_ref[h]
        back = dot(v, g_h, NT) - delta[pl.ds(2 * pair + h, 1), :]
        scores = (probs.astype(F32) * back).astype(BF16)
        g_v.append(dot(probs, g))
        g_k.append(dot(scores, q))
        g_q.append(dot(k_t[h * HALF : (h + 1) * HALF], scores))
    gjoined_ref[:, pl.ds(at, 128)] = (jnp.concatenate(g_q, 0).T * HALF**-0.5).astype(BF16)
    at_k = pl.multiple_of(width + pair * 128, 128)
    at_v = pl.multiple_of(2 * width + pair * 128, 128)
    gjoined_ref[:, pl.ds(at_k, 128)] = jnp.where(left, g_k[0], g_k[1]).astype(BF16)
    gjoined_ref[:, pl.ds(at_v, 128)] = jnp.where(left, g_v[0], g_v[1]).astype(BF16)

    @pl.when(j == pl.num_programs(0) - 1)
    def _():
        for load in loads:
            load.wait()


def attend_back(sample, first, pairs, tokens, joined, probs, begin, go_on, fetches):
    rows, width = joined.shape[0], joined.shape[1] // 3
    third = lambda c: pl.BlockSpec((rows, 128), lambda j: (0, c * (HEADS // 2) + first + j))
    joined, probs = far(joined, probs)
    ops = [joined, joined, joined, probs]
    specs = [third(0), third(1), third(2), pl.BlockSpec((2, rows, rows), lambda j: (first + j, 0, 0))]
    outs = [pltpu.VMEM((rows, 3 * width), BF16)]
    aliases = {}
    if first:
        ops += near(*go_on)
        specs += [VMEM] * 3
        aliases = {4: 0}
    else:
        gone, w_proj, low = begin
        ops += near(gone, w_proj) + far(low)
        specs += [VMEM] * 2 + [pl.BlockSpec((rows, width), lambda j: (0, 0))]
        outs += [pltpu.VMEM((rows, width), BF16), pltpu.VMEM((16, rows), F32)]
    fetch = len(fetches)
    n = len(outs)
    out = call(
        functools.partial(attend_back_kernel, sample, first, fetch),
        tokens,
        [*ops, *far(*fetches)],
        specs + [ANY] * fetch,
        10,
        aliases,
        grid=(pairs,),
        out_specs=[VMEM] * (n + fetch),
        out_shape=outs + [pltpu.VMEM(a.shape, a.dtype) for a in fetches],
        scratch_shapes=[pltpu.SemaphoreType.DMA((max(fetch, 1),))],
        cost=HEAVY,
        name=f"attend_back_{sample}_{first}",
    )
    return out[:n], out[n:]


def weights_kernel(packed, half, g0_ref, g1_ref, a0_ref, a1_ref, *rest):
    if not half:
        (gone_ref, l0_ref, l1_ref), rest = rest[:3], rest[3:]
    sums_ref, dw_refs, result = rest[0], rest[1:-1], rest[-1]
    width = a0_ref.shape[0]
    part = width // 2
    for c in range(3):
        at = slice(c * width + half * part, c * width + (half + 1) * part)
        here = slice(c * part, (c + 1) * part)
        result[:, here] = dot(a0_ref[...], g0_ref[:, at]) + dot(a1_ref[...], g1_ref[:, at])
        total = row_sum(g0_ref[:, at]) + row_sum(g1_ref[:, at])
        sums_ref[:, here] = jnp.broadcast_to(total, (8, part))
    end = 3 * part
    if not half:
        result[:, end : end + width] = dot(l0_ref[...], gone_ref[0]) + dot(l1_ref[...], gone_ref[1])
        end += width
    result[:, end:] = jnp.zeros((width, result.shape[1] - end), F32)
    if packed:
        orders = ((X_FIRST, Z_FIRST), (X_FIRST,))[half]
        share = result.shape[1] // len(orders)
        for i, order in enumerate(orders):
            cut = (i * share, (i + 1) * share)
            store_packed(*dw_refs[2 * i : 2 * i + 2], order + (Z1,), place()[0], result, columns=cut)
    else:
        dw_refs[0][...] = result[...]


def weights(packed, half, tokens, g0, g1, a0, a1, proj=()):
    width = a0.shape[0]
    part = width // 2
    columns = -(-(3 * part + (0 if half else width)) // 256) * 256
    if packed:
        tiles = columns // 128 // (1 if half else 2)
        grads = [pltpu.VMEM((16, tiles * PER, 128), BF16)] * (2 if half else 4)
    else:
        grads = [pltpu.VMEM((width, columns), F32)]
    ops = near(g0, g1, a0, a1, *proj)
    return call(
        functools.partial(weights_kernel, packed, half),
        tokens,
        ops,
        [VMEM] * len(ops),
        10,
        out_specs=[VMEM] * (1 + len(grads)),
        out_shape=[pltpu.VMEM((8, 3 * part), F32)] + grads,
        scratch_shapes=[pltpu.VMEM((width, columns), F32)],
        cost=HEAVY,
        name=f"weights_{half}",
    )


def token_rows(sample, g_ref, w_ref, x_ref, gmid_ref, ids_ref, vec_ref, pgrad_refs, grad_t, hot):
    rows, width = x_ref.shape
    positions = hot.shape[0]
    piece = pgrad_refs[0].shape[0]
    tile = 2 * piece
    g_gain = jnp.zeros((1, width), F32)
    g_bias = jnp.zeros((1, width), F32)
    for t in range(rows // tile):
        cut = slice(t * tile, (t + 1) * tile)
        grad = dot(g_ref[cut], w_ref[...], NT)
        normed, inverse = normalize(x_ref[cut])
        gmid = gmid_ref[sample * rows + t * tile : sample * rows + (t + 1) * tile]
        total = gmid + normalize_back(grad * vec_ref[0:1], normed, inverse)
        low = total.astype(BF16)
        for p in range(2):
            pgrad_refs[2 * t + p][...] = low[p * piece : (p + 1) * piece]
        grad_t[:, cut] = low.T
        g_gain = g_gain + row_sum(grad * normed)
        g_bias = g_bias + row_sum(grad)
        wanted = ids_ref[0:1, cut].astype(jnp.int32)
        iota = lax.broadcasted_iota(jnp.int32, (positions, tile), 0)
        hot[:, cut] = (iota == wanted).astype(F32).astype(BF16)
    return g_gain, g_bias


def finish_first_kernel(g_ref, w_ref, x_ref, gmid_ref, ids_ref, vec_ref, own, core, far_own, table, sums, grad_t, hot):
    g_gain, g_bias = token_rows(
        0, g_ref, w_ref, x_ref, gmid_ref, ids_ref, vec_ref, (own, core.at[0], far_own, core.at[1]), grad_t, hot
    )
    sums[...] = jnp.concatenate([g_gain, g_bias, jnp.zeros((6, g_gain.shape[1]), F32)], 0)
    table[...] = dot(grad_t[...], hot[...], NT)


def finish_kernel(
    packed, g_ref, w_ref, x_ref, gmid_ref, ids_ref, vec_ref, small_ref, sums0_ref, sums1_ref, db1a_ref, db1b_ref,
    table_ref, before_ref, own, core, far_own, *rest,
):
    dw_refs, (grad_t, hot, result) = rest[:-3], rest[-3:]
    pgrad_refs = (own, core.at[0], far_own, core.at[1])
    width = x_ref.shape[1]
    positions = hot.shape[0]
    part = width // 2
    me = place()[0]
    g_gain, g_bias = token_rows(1, g_ref, w_ref, x_ref, gmid_ref, ids_ref, vec_ref, pgrad_refs, grad_t, hot)
    columns = lambda c: jnp.concatenate([ref[0:1, c * part : (c + 1) * part] for ref in (sums0_ref, sums1_ref)], 1)
    few = [g_gain + before_ref[0:1], g_bias + before_ref[1:2], columns(0), columns(2), small_ref[3:4], small_ref[0:3]]
    few = jnp.concatenate(few + [jnp.zeros((120, width), F32)], 0).T
    result[:, 0:positions] = table_ref[...] + dot(grad_t[...], hot[...], NT)
    result[:, positions:] = few
    if packed:
        half = (me // Z1) % 2
        a, b = db1a_ref[...], db1b_ref[...]
        sums = jnp.concatenate([jnp.where(half == 0, a, b), jnp.where(half == 0, b, a)], 0)
        share = 96
        for owner in range(32):
            c, start = owner // 8, owner % 8 * share
            row = jnp.concatenate([jnp.zeros((1, 16), F32), sums[c : c + 1, start : start + share], jnp.zeros((1, 16), F32)], 1)
            result[owner * PER : owner * PER + 1, positions:] += row
        store_packed(*dw_refs, Z_FIRST + (Z1,), me, result)
    else:
        dw_refs[0][...] = result[...]


def finish(packed, last, tokens, ops, positions):
    rows, width = ops[2].shape
    columns = positions + 128
    share = (rows // 4, width)
    outs = [pltpu.VMEM(share, BF16), pltpu.VMEM((2,) + share, BF16), pltpu.VMEM(share, BF16)]
    scratch = [pltpu.VMEM((width, rows), BF16), pltpu.VMEM((positions, rows), BF16)]
    if not last:
        outs += [pltpu.VMEM((width, positions), F32), pltpu.VMEM((8, width), F32)]
    else:
        scratch += [pltpu.VMEM((width, columns), F32)]
        if packed:
            outs += [pltpu.VMEM((16, PER * columns // 128, 128), BF16)] * 2
        else:
            outs += [pltpu.VMEM((width, columns), F32)]
    return call(
        functools.partial(finish_kernel, packed) if last else finish_first_kernel,
        tokens,
        near(*ops),
        [VMEM] * len(ops),
        14,
        out_specs=[VMEM] * len(outs),
        out_shape=outs,
        scratch_shapes=scratch,
        cost=HEAVY,
        name=f"finish_{int(last)}",
    )


def swap_bit(x, bit, count):
    return lax.ppermute(x, AXES, [(d, d ^ bit) for d in range(count)])


def add(arrays):
    return sum(a.astype(F32) for a in arrays)


def fold_kernel(counts, *refs):
    n = 2 * sum(counts)
    pairs, outs = refs[:n], refs[n:]
    for k, count in enumerate(counts):
        message, stay = outs[2 * k : 2 * k + 2]
        half = message.shape[0]
        row = 0
        for at in range(0, 2 * count, 2):
            rows = pairs[at].shape[1]
            here = slice(row, row + rows)
            for i in range(half):
                message[i, here] = add([ref[half + i] for ref in pairs[at : at + 2]]).astype(BF16)
            for i in range(half):
                stay[i, here] = add([ref[i] for ref in pairs[at : at + 2]]).astype(BF16)
            row += rows
        pairs = pairs[2 * count :]


class Sums:
    def __init__(self, count, order):
        self.count, self.bits, self.pairs = count, list(order), []

    def swap(self, send, bit):
        return lax.ppermute(send, AXES, [(d, d ^ bit) for d in range(self.count)])

    def begin(self, keep, send):
        got = self.swap(send, self.bits[0])
        self.pairs += [keep, got]
        return got


def fold(tokens, *sums):
    outs = []
    for one in sums:
        owners, _, lanes = one.pairs[0].shape
        rows = sum(a.shape[1] for a in one.pairs[::2])
        outs += [pltpu.VMEM((owners // 2, rows, lanes), BF16)] * 2
    pairs = [a for one in sums for a in one.pairs]
    out = call(
        functools.partial(fold_kernel, [len(one.pairs) // 2 for one in sums]),
        tokens,
        near(*pairs),
        [VMEM] * len(pairs),
        2,
        out_specs=[VMEM] * len(outs),
        out_shape=outs,
        name="fold",
    )
    for one, message, stay in zip(sums, out[::2], out[1::2]):
        one.bits = one.bits[1:]
        one.pairs = [stay, one.swap(message, one.bits[0])]
    return tuple(out[::2])


def turn_kernel(a0, a1, b0, b1, c0, c1, out):
    n = 12 * PER
    out[:, 0:768] = add([c0[0], c1[0]]).astype(BF16)
    for at, pair in ((768, (a0, a1)), (1152, (b0, b1))):
        for k in range(6):
            rows = slice(n + 48 * k, n + 48 * (k + 1))
            value = add([a[0, rows] for a in pair]).astype(BF16)
            out[48 * (k // 3) : 48 * (k // 3 + 1), at + 128 * (k % 3) : at + 128 * (k % 3 + 1)] = value


def hidden_kernel(a0, a1, b0, b1, c0, c1, other, dw1, dw2):
    n = 12 * PER
    low = (place()[0] // Z1) % 2 == 0
    dw2[...] = add([c0[0], c1[0], other[:, 0:768]])
    for k in range(6):
        rows = slice(48 * k, 48 * (k + 1))
        block = lambda at: other[48 * (k // 3) : 48 * (k // 3 + 1), at + 128 * (k % 3) : at + 128 * (k % 3 + 1)]
        mine = add([a0[0, rows], a1[0, rows], block(1152)])
        theirs = add([b0[0, rows], b1[0, rows], block(768)])
        for e, half in enumerate((jnp.where(low, mine, theirs), jnp.where(low, theirs, mine))):
            for i in range(2):
                at = (12 * e + 2 * k + i) * 128
                dw1[:, at : at + 128] = half[i * PER : (i + 1) * PER]


def tiles_kernel(counts, layout, *refs):
    n = sum(counts)
    held, outs, result = refs[:n], refs[n:-1], refs[-1]
    row, at = 0, 0
    for count in counts:
        rows = held[at].shape[1]
        result[row : row + rows] = add([ref[0] for ref in held[at : at + count]])
        row, at = row + rows, at + count
    layout(result, outs)


def put_tiles(result, row, out, columns):
    for c in range(columns // 128):
        out[:, c * 128 : (c + 1) * 128] = result[row + c * PER : row + (c + 1) * PER]


def rest_layout(result, outs):
    dwqkv, dwproj, table, *few = outs
    width = dwproj.shape[1]
    part = width // 2
    tiles = lambda n: n // 128 * PER
    second = tiles(5 * part + 128)
    for c in range(3):
        for half, row in enumerate((0, second)):
            at = c * width + half * part
            put_tiles(result, row + tiles(c * part), dwqkv.at[:, at : at + part], part)
    put_tiles(result, tiles(3 * part), dwproj, width)
    third = second + tiles(3 * part + 128)
    put_tiles(result, third, table, table.shape[1])
    at = third + tiles(table.shape[1])
    tile = result[at : at + PER]
    for k in range(8):
        few[k][...] = jnp.sum(jnp.where(lax.broadcasted_iota(jnp.int32, (PER, 128), 1) == k, tile, 0.0), axis=1)
    few[8][...] = tile[0, 16:112]


def tiles(streams, layout, outs, name):
    arrays = [a for held in streams for a in held]
    rows = sum(held[0].shape[1] for held in streams)
    first = lambda a: pl.BlockSpec((1,) + a.shape[1:], lambda i: (0, 0, 0))
    return call(
        functools.partial(tiles_kernel, [len(held) for held in streams], layout),
        (),
        arrays,
        [first(a) for a in arrays],
        8,
        grid=(1,),
        out_specs=[pl.BlockSpec(shape, lambda i, n=len(shape): (0,) * n) for shape in outs],
        out_shape=[jax.ShapeDtypeStruct(shape, F32) for shape in outs],
        scratch_shapes=[pltpu.VMEM((rows, 128), F32)],
        name=name,
    )


def shards(
    patches, pos_ids, lengths, pos_table, ln1_gain, ln1_bias, w_qkv, q_bias, v_bias, w_proj, proj_bias,
    ln2_gain, ln2_bias, w_fc1, fc1_bias, w_fc2, fc2_bias, cotangent, *, wide, parts,
):
    width = patches.shape[2]
    hidden, positions = w_fc1.shape[1], pos_table.shape[1]
    count = wide * parts
    packed = wide == 8 and parts == 4
    hop = lambda a, k: lax.ppermute(a, "blk", [(d, d ^ k) for d in range(parts)])

    def across(own, core, far_own, *tokens):
        got = hop(core, 1)
        message = join(tokens, far_own, got)
        return message, (own, got, hop(message, 2))

    vectors = (ln1_gain, ln1_bias, q_bias, v_bias, proj_bias, ln2_gain, ln2_bias, fc2_bias, fc1_bias)
    xs, ys, cots, (vec, table, wqkv, wproj) = prepare(
        pos_ids, patches, cotangent, vectors, (pos_table, w_qkv, w_proj)
    )
    _, xs = across(*xs)
    message, ys = across(*ys, xs[2])
    mid0, ids0, probs0, _, (x0, joined0, in0, low0, low0_t) = attend(
        0, (message,), lengths, xs, table, vec, wqkv, wproj, ()
    )
    message, cots = across(*cots, ys[2])
    mid1, ids1, probs1, (w1, w2), (x1, joined1, in1, low1, low1_t) = attend(
        1, (message,), lengths, ys, table, vec, wqkv, wproj, (w_fc1, w_fc2)
    )
    run = functools.partial(mlp, packed)
    *held, db1a = run((), (0, 1), mid0, mid1, w1, w2, vec, cots=cots)
    if packed:
        *held, db1a, a, b, c, d = held + [db1a]
        sum1 = Sums(count, X_FIRST), Sums(count, Z_FIRST)
        sum2 = Sums(count, X_FIRST), Sums(count, Z_FIRST)
        sum1[0].begin(a, b)
        sum1[1].begin(c, d)
        *held[3:], db1b, a, b, c, d = run((), (2,), mid0, mid1, w1, w2, vec, held=held)
        messages = fold((db1b,), *sum1)
        _, gmid, db1b, a, b, c, d, gone, small, wproj, *mixed = run(
            messages, (3,), mid0, mid1, w1, w2, vec, held=held, grads=(db1b, a, b, c, d), w_proj=w_proj
        )
        sum2[0].begin(a, b)
        sum2[1].begin(c, d)
    else:
        *held, db1a, a, b = held + [db1a]
        grads1 = a, b
        _, gmid, db1b, a, b, gone, small, wproj, *mixed = run(
            (), (2, 3), mid0, mid1, w1, w2, vec, held=held, w_proj=w_proj
        )
        grads2 = a, b
    tokens = fold((), *sum1) if packed else ()
    (g0, *_), (wqkv, x0) = attend_back(0, 0, 6, tokens, joined0, probs0, (gone, wproj, low0), (), (w_qkv, x0))
    tokens = (g0,)
    if packed:
        tokens = fold(tokens, *sum1, *sum2)
    message, mixed = across(*mixed, *tokens)
    (g1, *state), (in0, in1, low0_t, low1_t, x1) = attend_back(
        1, 0, 3, tokens + (message,), joined1, probs1, (gone, wproj, low1), (), (in0, in1, low0_t, low1_t, x1)
    )
    sums0, *dwa = weights(packed, 0, (), g0, g1, in0, in1, (gone, low0_t, low1_t))
    if packed:
        sum3 = Sums(count, X_FIRST + (Z1,)), Sums(count, Z_FIRST + (Z1,))
        sum3[0].begin(*dwa[:2])
        sum3[1].begin(*dwa[2:])
    *pgrad0, table0, before = finish(packed, False, (sums0,), (g0, wqkv, x0, gmid, ids0, vec), positions)
    tokens = (before, mixed[2])
    if packed:
        tokens += fold(tokens, *sum2, *sum3)
    (g1,), _ = attend_back(1, 3, 3, tokens, joined1, probs1, (), (g1, *state), ())
    tokens = (g1,)
    if packed:
        tokens = fold(tokens, *sum2)
    message, pgrad0 = across(*pgrad0, *tokens)
    sums1, *dwb = weights(packed, 1, tokens + (message,), g0, g1, in0, in1)
    tokens = (sums1,)
    if packed:
        sum4 = Sums(count, X_FIRST + (Z1,))
        sum4.begin(*dwb)
        tokens = fold(tokens, *sum3)
        send = call(
            turn_kernel,
            tokens,
            near(*sum1[0].pairs, *sum2[0].pairs, *sum2[1].pairs),
            [VMEM] * 6,
            2,
            out_specs=VMEM,
            out_shape=pltpu.VMEM((96, 2 * width), BF16),
            name="turn",
        )
        other = sum4.swap(send, Z1)
        tokens += (send,)
    *pgrad1, a, b = tuple(
        finish(
            packed,
            True,
            tokens,
            (g1, wqkv, x1, gmid, ids1, vec, small, sums0, sums1, db1a, db1b, table0, before),
            positions,
        )
    ) + (() if packed else (None,))
    message, pgrad1 = across(*pgrad1)
    if packed:
        sum5 = Sums(count, Z_FIRST + (Z1,))
        sum5.begin(a, b)
    mixed, pgrad = gather((message,), mixed), gather((), pgrad0, pgrad1)
    if packed:
        for i in range(4):
            fold((), sum4)
            fold((), sum5)
            if i < 2:
                fold((), *sum3)
        ops = near(*sum1[0].pairs, *sum2[0].pairs, *sum1[1].pairs, other)
        dw1, dw2 = call(
            hidden_kernel,
            (),
            ops,
            [VMEM] * 7,
            2,
            out_specs=[VMEM] * 2,
            out_shape=[jax.ShapeDtypeStruct((n // count, hidden + width - n), F32) for n in (width, hidden)],
            name="hidden",
        )
        shapes = [(width // count, n) for n in (3 * width, width, positions)]
        shapes += [(width // count,)] * 8 + [(hidden // count,)]
        dwqkv, dwproj, table, *few = tiles([one.pairs for one in (*sum3, sum4, sum5)], rest_layout, shapes, "rest")
    else:
        share = lambda a: lax.psum_scatter(a.astype(BF16), AXES, scatter_dimension=0, tiled=True).astype(F32)
        dw1 = share(jnp.concatenate([grads1[0], grads2[0]], 1))
        dw2 = share(jnp.concatenate([grads1[1], grads2[1]], 0))
        dwa, dwb, misc = share(dwa[0]), share(dwb[0]), share(a)
        n = width // 2
        dwqkv = jnp.concatenate([x[:, c * n : (c + 1) * n] for c in range(3) for x in (dwa, dwb)], 1)
        dwproj = dwa[:, 3 * n : 3 * n + width]
        table, few = misc[:, :positions], [misc[:, positions + k] for k in range(8)]
        few.append(share(jnp.concatenate([db1a, db1b], 0).reshape(-1)))
    (g_gain1, g_bias1, g_q, g_v, g_proj, g_gain2, g_bias2, g_fc2, g_fc1) = few
    return (
        mixed, pgrad, table, g_gain1, g_bias1, dwqkv, g_q, g_v, dwproj, g_proj, g_gain2, g_bias2,
        dw1, g_fc1, dw2, g_fc2,
    )


def solution(mesh):
    wide, parts = mesh.shape["wide"], mesh.shape["blk"]
    tokens = P("wide", "blk", None)
    in_specs = (tokens, P("wide", "blk"), P("wide")) + (P(),) * 14 + (tokens,)
    vector, matrix = P(AXES), P(AXES, None)
    out_specs = (
        tokens, tokens, matrix, vector, vector, matrix, vector, vector, matrix, vector, vector, vector,
        matrix, vector, matrix, vector,
    )
    return jax.shard_map(
        functools.partial(shards, wide=wide, parts=parts),
        mesh=mesh, in_specs=in_specs, out_specs=out_specs, check_vma=False,
    )
```

```python
import functools

import jax
import jax.numpy as jnp
from jax import lax
from jax.experimental import pallas as pl
from jax.experimental.pallas import tpu as pltpu
from jax.sharding import PartitionSpec as P

HEADS = 12
HALF = 64
F32, BF16 = jnp.float32, jnp.bfloat16
NN = (((1,), (0,)), ((), ()))
NT = (((1,), (1,)), ((), ()))
TN = (((0,), (0,)), ((), ()))
EPS = 1e-6
MASKED = -1e30
AXES = ("wide", "blk")
MIB = 2**20
CORE, Y, X, Z0, Z1 = 1, 2, 4, 8, 16
X_FIRST = (CORE, X, Y, Z0)
Z_FIRST = (CORE, Z0, X, Y)
LAST = (CORE, X, Z0, Y, Z1)
PER = 24
LIGHT = pl.CostEstimate(flops=1, bytes_accessed=1, transcendentals=0)
HEAVY = pl.CostEstimate(flops=10**11, bytes_accessed=1, transcendentals=0)
VMEM = pl.BlockSpec(memory_space=pltpu.VMEM)
ANY = pl.BlockSpec(memory_space=pl.ANY)
SMEM = pl.BlockSpec(memory_space=pltpu.SMEM)


def dot(a, b, dims=NN):
    return lax.dot_general(a, b, dims, preferred_element_type=F32)


def near(*arrays):
    return [pltpu.with_memory_space_constraint(a, pltpu.VMEM) for a in arrays]


def far(*arrays):
    return [pltpu.with_memory_space_constraint(a, pltpu.HBM) for a in arrays]


def call(body, tokens, ops, in_specs, vmem, aliases=None, cost=LIGHT, **rest):
    n = len(tokens)
    return pl.pallas_call(
        lambda *refs: body(*refs[n:]),
        in_specs=[ANY] * n + in_specs,
        input_output_aliases={n + a: b for a, b in (aliases or {}).items()},
        compiler_params=pltpu.CompilerParams(vmem_limit_bytes=int(vmem * MIB)),
        cost_estimate=cost,
        **rest,
    )(*tokens, *ops)


PIECES = 4


def brought(sources, targets, sems):
    copies = []
    for a, b in zip(sources, targets):
        step = a.shape[0] // PIECES
        for i in range(PIECES):
            here = pl.ds(i * step, step)
            copies.append(pltpu.make_async_copy(a.at[here], b.at[here], sems.at[len(copies)]))
    return copies


def place():
    lane = lax.axis_index("blk")
    return lax.axis_index("wide") * lax.axis_size("blk") + lane, lane


def normalize(x):
    center = x - jnp.mean(x, axis=-1, keepdims=True)
    inverse = lax.rsqrt(jnp.mean(center * center, axis=-1, keepdims=True) + EPS)
    return center * inverse, inverse


def normalize_back(g, normed, inverse):
    return inverse * (
        g - jnp.mean(g, axis=-1, keepdims=True) - normed * jnp.mean(g * normed, axis=-1, keepdims=True)
    )


def gelu_both(x):
    cdf = 0.5 + 0.5 * lax.erf(x * 0.7071067811865476)
    return x * cdf, cdf + x * (jnp.exp(x * x * -0.5) * 0.3989422804014327)


def row_sum(x):
    return jnp.sum(x.astype(F32), axis=0, keepdims=True)


def relative(position, order):
    return sum(bit for i, bit in enumerate(order) if (position >> (len(order) - 1 - i)) & 1)


def store_packed(keep_ref, send_ref, order, me, result_ref, base=0, extra=0, columns=None):
    half = 2 ** (len(order) - 1)
    first, last = columns or (0, result_ref.shape[1])
    for position in range(2 * half):
        ref = (keep_ref, send_ref)[position // half]
        start = pl.multiple_of((me ^ (relative(position, order) | extra)) * PER, 8)
        for c in range((last - first) // 256):
            two = [result_ref[pl.ds(start, PER), first + (2 * c + i) * 128 : first + (2 * c + i + 1) * 128] for i in range(2)]
            here = pl.ds(base + 2 * c * PER, 2 * PER)
            ref[position % half, here] = jnp.concatenate(two, 0).astype(BF16)


def lay(own, core, far_own):
    return own, core.at[0], far_own, core.at[1]


def pieces(sample, ids_ref, outs, lane_me):
    piece = ids_ref.shape[1]
    for k, out in enumerate(lay(*outs)):
        ids = ids_ref[pl.ds(2 * (lane_me ^ k) + sample, 1)]
        row = jnp.concatenate([ids >> 8, ids & 255, jnp.zeros((1, out.shape[1] - 2 * piece), jnp.int32)], 1)
        out[piece : piece + 16] = jnp.broadcast_to(row.astype(F32), (16, out.shape[1])).astype(BF16)


def first_kernel(patches_ref, ids_hbm, own, core, far_own, ids_ref, sems):
    piece = patches_ref.shape[1]
    lane_me = place()[1]
    copies = [pltpu.make_async_copy(ids_hbm, ids_ref, sems.at[4])]
    for k, out in enumerate(lay(own, core, far_own)):
        copies.append(pltpu.make_async_copy(patches_ref.at[2 * (lane_me ^ k)], out.at[0:piece], sems.at[k]))
    for copy in copies:
        copy.start()
    copies[0].wait()
    pieces(0, ids_ref, (own, core, far_own), lane_me)
    for copy in copies[1:]:
        copy.wait()


def second_kernel(patches_ref, cot_ref, ids_hbm, *refs):
    vectors, big, refs = refs[:9], refs[9:12], refs[12:]
    second, cots, vec_ref, loaded = refs[:3], refs[3:6], refs[6], refs[7:10]
    ids_ref, raw, sems = refs[10], refs[11:-1], refs[-1]
    piece, width = patches_ref.shape[1:]
    lane_me = place()[1]
    copies = []

    def start(a, b):
        copies.append(pltpu.make_async_copy(a, b, sems.at[len(copies)]))
        copies[-1].start()
        return copies[-1]

    few = [start(ids_hbm, ids_ref)] + [start(a, b) for a, b in zip(vectors, raw)]
    for k, out in enumerate(lay(*second)):
        start(patches_ref.at[2 * (lane_me ^ k) + 1], out.at[0:piece])
    for a, b in zip(big, loaded):
        start(a, b)
    for k, out in enumerate(lay(*cots)):
        start(cot_ref.at[pl.ds(2 * (lane_me ^ k), 2)], out)
    for copy in few:
        copy.wait()
    pieces(1, ids_ref, second, lane_me)
    row = 0
    for ref in raw:
        for k in range(ref.shape[0] // width):
            vec_ref[row : row + 1] = ref[k * width : (k + 1) * width].astype(F32).reshape(1, width)
            row += 1
    vec_ref[row:] = jnp.zeros((vec_ref.shape[0] - row, width), F32)
    for copy in copies[len(few) :]:
        copy.wait()


def message_shapes(shape):
    return [pltpu.VMEM(shape, BF16), pltpu.VMEM((2,) + shape, BF16), pltpu.VMEM(shape, BF16)]


def prepare_first(pos_ids, patches):
    _, piece, width = patches.shape
    return call(
        first_kernel,
        (),
        far(patches, pos_ids),
        [ANY] * 2,
        2,
        out_specs=[VMEM] * 3,
        out_shape=message_shapes((piece + 16, width)),
        scratch_shapes=[pltpu.VMEM(pos_ids.shape, pos_ids.dtype), pltpu.SemaphoreType.DMA((5,))],
        name="first",
    )


def prepare_second(tokens, pos_ids, patches, cotangent, vectors, big):
    _, piece, width = patches.shape
    out = call(
        second_kernel,
        tokens,
        far(patches, cotangent, pos_ids, *vectors, *big),
        [ANY] * (3 + len(vectors) + len(big)),
        2,
        out_specs=[VMEM] * (7 + len(big)),
        out_shape=message_shapes((piece + 16, width))
        + message_shapes((2, piece, width))
        + [pltpu.VMEM((16, width), F32)]
        + [pltpu.VMEM(a.shape, a.dtype) for a in big],
        scratch_shapes=[
            pltpu.VMEM(pos_ids.shape, pos_ids.dtype),
            *[pltpu.VMEM(a.shape, a.dtype) for a in vectors],
            pltpu.SemaphoreType.DMA((9 + len(vectors) + len(big),)),
        ],
        cost=HEAVY,
        name="second",
    )
    return out[:3], out[3:6], out[6:]


def join_kernel(a_ref, b_ref, out, sems):
    copies = [
        pltpu.make_async_copy(a_ref, out.at[0], sems.at[0]),
        pltpu.make_async_copy(b_ref.at[1], out.at[1], sems.at[1]),
    ]
    for copy in copies:
        copy.start()
    for copy in copies:
        copy.wait()


def join(tokens, far_own, got):
    return call(
        join_kernel,
        tokens,
        near(far_own, got),
        [VMEM] * 2,
        1,
        out_specs=VMEM,
        out_shape=pltpu.VMEM(got.shape, BF16),
        scratch_shapes=[pltpu.SemaphoreType.DMA((2,))],
        name="join",
    )


def gather_kernel(samples, *refs):
    sets, out, sems = refs[: 3 * samples], refs[-2], refs[-1]
    lane_me = place()[1]
    copies = []
    for s in range(samples):
        own, got, other = sets[3 * s : 3 * s + 3]
        for k, a in enumerate((own, got.at[0], other.at[0], other.at[1])):
            at = 2 * (lane_me ^ k) + s
            where = out.at[pl.ds(at, 2)] if samples == 1 else out.at[at]
            copies.append(pltpu.make_async_copy(a, where, sems.at[4 * s + k]))
            copies[-1].start()
    for copy in copies:
        copy.wait()


def gather(tokens, *sets):
    ops = near(*[a for one in sets for a in one])
    return call(
        functools.partial(gather_kernel, len(sets)),
        tokens,
        ops,
        [VMEM] * len(ops),
        1,
        out_specs=ANY,
        out_shape=pltpu.HBM((8,) + ops[0].shape[-2:], BF16),
        scratch_shapes=[pltpu.SemaphoreType.DMA((4 * len(sets),))],
        name="gather",
    )


def attend_kernel(
    sample, fetch, lengths_ref, own_ref, got_ref, other_ref, table_ref, vec_ref, wqkv_ref, wproj_ref, *rest
):
    fetches, rest = rest[:fetch], rest[fetch:]
    mid_ref, ids_ref, probs_ref, rest = rest[0], rest[1], rest[2], rest[3:]
    fetched, rest = rest[:fetch], rest[fetch:]
    outs, (stream, joined, attn_in, attn_in_t, low, low_t, hidden, sems, fetch_sems) = rest[:4], rest[4:]
    saved = (stream, joined, attn_in_t, low_t)
    copies = [pltpu.make_async_copy(a, b, sems.at[i]) for i, (a, b) in enumerate(zip(saved, outs))]
    loads = brought(fetches, fetched, fetch_sems)
    j = pl.program_id(0)
    pieces = (own_ref, got_ref.at[0], other_ref.at[0], other_ref.at[1])
    rows, width = stream.shape
    piece = rows // len(pieces)

    @pl.when(j == 0)
    def _():
        for load in loads:
            load.start()
        positions = table_ref.shape[1]
        ids = []
        for k, ref in enumerate(pieces):
            coded = ref[piece : piece + 16].astype(F32)
            ids.append(coded[0:8, 0:piece] * 256.0 + coded[0:8, piece : 2 * piece])
        ids_ref[...] = jnp.concatenate(ids, 1)
        for k, ref in enumerate(pieces):
            here = slice(k * piece, (k + 1) * piece)
            column = jnp.broadcast_to(ids[k][0:1], (piece, piece)).T.astype(jnp.int32)
            iota = lax.broadcasted_iota(jnp.int32, (piece, piece), 1)
            onehot = jnp.concatenate([(column == iota + piece * c).astype(F32) for c in range(positions // piece)], 1)
            value = ref[0:piece].astype(F32) + dot(onehot.astype(BF16), table_ref[...], NT)
            stream[here] = value
            normed, _ = normalize(value)
            normed = (normed * vec_ref[0:1] + vec_ref[1:2]).astype(BF16)
            attn_in[here] = normed
            attn_in_t[:, here] = normed.T
        copies[0].start()
        copies[2].start()
        for c in range(3):
            cols = slice(c * width, (c + 1) * width)
            part = dot(attn_in[...], wqkv_ref[:, cols])
            if c != 1:
                part = part + vec_ref[2 + c // 2 : 3 + c // 2]
            part = part.astype(BF16)
            if c == 0:
                part = part * jnp.asarray(HALF**-0.5, BF16)
            joined[:, cols] = part
        copies[1].start()
        lane_me = place()[1]
        length = lengths_ref[2 * lane_me + sample]
        part = lax.broadcasted_iota(jnp.int32, (piece, 128), 0)
        for i in range(len(pieces)):
            visible = part + (lane_me ^ i) * piece < length
            hidden[i * piece : (i + 1) * piece] = jnp.where(visible, 0.0, MASKED)

    at = pl.multiple_of(j * 128, 128)
    q = joined[:, pl.ds(at, 128)]
    k = joined[:, pl.ds(pl.multiple_of(width + j * 128, 128), 128)]
    v = joined[:, pl.ds(pl.multiple_of(2 * width + j * 128, 128), 128)]
    v_t = v.T
    lane = lax.broadcasted_iota(jnp.int32, (rows, 128), 1)
    ones = jnp.ones((16, rows), BF16)
    heads = []
    for h in range(2):
        own = (lane < HALF) == (h == 0)
        spare = lane == HALF * (1 - h)
        q_h = jnp.where(own, q, jnp.where(spare, 1.0, 0.0).astype(BF16))
        k_h = jnp.where(own, k, jnp.where(spare, hidden[...], 0.0).astype(BF16))
        scores = dot(k_h, q_h, NT)
        weights = jnp.exp(scores - jnp.max(scores, axis=0, keepdims=True)).astype(BF16)
        out = dot(jnp.concatenate([v_t[h * HALF : (h + 1) * HALF], ones], 0), weights)
        inverse = 1.0 / out[HALF : HALF + 1]
        probs_ref[h] = weights * inverse.astype(BF16)
        heads.append(out[0:HALF] * inverse)
    heads = jnp.concatenate(heads, 0)
    low_t[pl.ds(at, 128)] = heads.astype(BF16)
    low[:, pl.ds(at, 128)] = heads.T.astype(BF16)

    @pl.when(j == pl.num_programs(0) - 1)
    def _():
        copies[3].start()
        mid_ref[...] = stream[...] + dot(low[...], wproj_ref[...]) + vec_ref[4:5]
        for copy in copies + loads:
            copy.wait()


def attend(sample, tokens, lengths, pieces, table, vec, w_qkv, w_proj, fetches):
    rows = 4 * (pieces[0].shape[0] - 16)
    width = w_proj.shape[0]
    fetch = len(fetches)
    saved = [
        ((rows, width), F32),
        ((rows, 3 * width), BF16),
        ((width, rows), BF16),
        ((width, rows), BF16),
    ]
    stream, joined, attn_in_t, low_t = [pltpu.VMEM(*a) for a in saved]
    low = pltpu.VMEM((rows, width), BF16)
    mid, ids, probs, *rest = call(
        functools.partial(attend_kernel, sample, fetch),
        tokens,
        [lengths, *near(*pieces, table, vec, w_qkv, w_proj), *far(*fetches)],
        [SMEM] + [VMEM] * 7 + [ANY] * fetch,
        13,
        grid=(HEADS // 2,),
        out_specs=[VMEM] * 2 + [pl.BlockSpec((2, rows, rows), lambda j: (j, 0, 0))] + [VMEM] * fetch + [ANY] * 4,
        out_shape=[pltpu.VMEM((rows, width), F32), pltpu.VMEM((8, rows), F32)]
        + [pltpu.HBM((HEADS, rows, rows), BF16)]
        + [pltpu.VMEM(a.shape, a.dtype) for a in fetches]
        + [pltpu.HBM(*a) for a in saved],
        scratch_shapes=[stream, joined, pltpu.VMEM((rows, width), BF16), attn_in_t, low, low_t]
        + [pltpu.VMEM((rows, 128), F32)]
        + [pltpu.SemaphoreType.DMA((4,)), pltpu.SemaphoreType.DMA((max(fetch * PIECES, 1),))],
        cost=HEAVY,
        name=f"attend_{sample}",
    )
    return mid, ids, probs, rest[:fetch], rest[fetch:]


def mlp_kernel(packed, begin, end, chunks, x0_ref, x1_ref, w1_ref, w2_ref, vec_ref, *rest):
    take = lambda n: (rest[:n], rest[n:])
    if begin:
        (own_ref, got_ref, other_ref), rest = take(3)
        cots = (own_ref, got_ref.at[0], other_ref.at[0], other_ref.at[1])
        (mlp_in, mlp_in_t, gt, acc, gacc), rest = take(5)
    else:
        (mlp_in, mlp_in_t, gt), rest = take(3)
        rest = rest[2:]
        if chunks[0] % 2:
            rest = rest[5:]
        if end:
            (wproj_ref,), rest = take(1)
        (acc, gacc), rest = take(2)
    (db1_ref, *dw_refs), rest = take(5 if packed else 3)
    if end:
        (gone_ref, small_ref, wproj_out, own, core, far_own), rest = take(6)
        mixed_refs = (own, core.at[0], far_own, core.at[1])
    act, gpre, result, sem = rest
    j = pl.program_id(0)
    xs = (x0_ref, x1_ref)
    rows, width = x0_ref.shape
    columns = result.shape[1]
    tile = rows // 2
    piece = tile // 2
    per_sample = rows // tile
    tiles = len(xs) * per_sample
    me = place()[0]
    chunk = (chunks[0] + j) ^ (me // 8) if packed else chunks[0] + j

    @pl.when(j == 0)
    def _():
        if end:
            pltpu.make_async_copy(wproj_ref, wproj_out, sem).start()
        if not begin:
            return
        for i in range(tiles):
            s, t = i // per_sample, i % per_sample
            here = slice(i * tile, (i + 1) * tile)
            normed, _ = normalize(xs[s][t * tile : (t + 1) * tile])
            value = (normed * vec_ref[5:6] + vec_ref[6:7]).astype(BF16)
            mlp_in[here] = value
            mlp_in_t[:, here] = value.T
            for p in range(2):
                gt[i * tile + p * piece : i * tile + (p + 1) * piece] = cots[2 * t + p][s]
            acc[here] = jnp.zeros((tile, width), F32)
            gacc[here] = jnp.zeros((tile, width), F32)

    at = pl.ds(pl.multiple_of(chunk * columns, columns), columns)
    b1 = vec_ref[pl.ds(8 + chunk, 1)]
    db1 = jnp.zeros((1, columns), F32)
    for i in range(tiles):
        here = slice(i * tile, (i + 1) * tile)
        value, slope = gelu_both(dot(mlp_in[here], w1_ref[:, at]) + b1)
        value = value.astype(BF16)
        act[here] = value
        g = (dot(gt[here], w2_ref[at], NT) * slope).astype(BF16)
        gpre[here] = g
        db1 = db1 + row_sum(g)
        acc[here] += dot(value, w2_ref[at])
        gacc[here] += dot(g, w1_ref[:, at], NT)
    db1_ref[pl.ds(chunk % 2, 1)] = db1
    if packed:
        keep, send, keep2, send2 = dw_refs
        result[...] = dot(mlp_in_t[...], gpre[...])
        slot = pl.multiple_of((chunk % 2) * 6 * PER, 16)
        for e in range(2):
            store_packed(keep, send, X_FIRST, me, result, slot + e * 12 * PER, e * Z1)
        result[...] = dot(act[...], gt[...], TN)
        for position in range(16):
            owner = relative(position, Z_FIRST)
            if owner & Z0:
                continue
            start = pl.multiple_of(((me % 8) ^ (owner % 8)) * 96, 8)
            where = position % 8 + (chunks[0] % 2 + j) * 2 ** (3 - Z_FIRST.index(Z0))
            (keep2, send2)[position // 8][where] = result[pl.ds(start, 96)].astype(BF16)
    else:
        dw_refs[0][...] = dot(mlp_in_t[...], gpre[...])
        dw_refs[1][...] = dot(act[...], gt[...], TN)

    @pl.when(j == pl.num_programs(0) - 1)
    def _():
        if not end:
            return
        sums = [jnp.zeros((1, width), F32) for _ in range(4)]
        for i in range(tiles):
            s, t = i // per_sample, i % per_sample
            here = slice(i * tile, (i + 1) * tile)
            x = xs[s][t * tile : (t + 1) * tile]
            normed, inverse = normalize(x)
            mixed = (x + acc[here] + vec_ref[7:8]).astype(BF16)
            for p in range(2):
                mixed_refs[2 * t + p][s] = mixed[p * piece : (p + 1) * piece]
            cot = gt[here].astype(F32)
            g = gacc[here]
            gmid = cot + normalize_back(g * vec_ref[5:6], normed, inverse)
            gacc[here] = gmid
            low = gmid.astype(BF16)
            gone_ref[s, t * tile : (t + 1) * tile] = low
            sums = [a + row_sum(b) for a, b in zip(sums, (g * normed, g, cot, low))]
        for k in range(4):
            small_ref[k : k + 1] = sums[k]
        pltpu.make_async_copy(wproj_ref, wproj_out, sem).wait()


def mlp(packed, tokens, chunks, x0, x1, w1, w2, vec, cots=None, held=None, grads=None, w_proj=None):
    begin, end = held is None, w_proj is not None
    rows, width = x0.shape
    hidden = w1.shape[1]
    columns = width
    length = 2 * rows
    sums = [pltpu.VMEM((length, width), F32)] * 2
    ops = near(x0, x1, w1, w2, vec)
    outs = list(sums)
    aliases = {}
    if begin:
        ops += near(*cots)
        outs = [pltpu.VMEM(s, BF16) for s in ((length, width), (width, length), (length, width))] + outs
    else:
        aliases = {len(ops) + 3: 0, len(ops) + 4: 1}
        ops += near(*held)
    at = len(outs)
    db1 = pltpu.VMEM((2, columns), F32)
    if packed:
        outs += [db1] + [pltpu.VMEM((8, 24 * PER, 128), BF16)] * 2 + [pltpu.VMEM((8, 96, width), BF16)] * 2
        dw_specs = [VMEM] * 5
        if grads is not None:
            aliases.update({len(ops) + i: at + i for i in range(5)})
            ops += near(*grads)
    else:
        whole = len(chunks) * columns
        outs += [db1, pltpu.HBM((width, whole), F32), pltpu.HBM((whole, width), F32)]
        dw_specs = [VMEM, pl.BlockSpec((width, columns), lambda j: (0, j)), pl.BlockSpec((columns, width), lambda j: (j, 0))]
    specs = [VMEM] * at + dw_specs
    in_specs = [VMEM] * len(ops)
    if end:
        ops += far(w_proj)
        in_specs += [ANY]
        outs += [pltpu.VMEM((2, rows, width), BF16), pltpu.VMEM((4, width), F32), pltpu.VMEM(w_proj.shape, BF16)]
        share = (2, rows // 4, width)
        outs += [pltpu.VMEM(share, BF16), pltpu.VMEM((2,) + share, BF16), pltpu.VMEM(share, BF16)]
        specs += [VMEM] * 6
    return call(
        functools.partial(mlp_kernel, packed, begin, end, chunks),
        tokens,
        ops,
        in_specs,
        12 if packed else 26,
        aliases,
        grid=(len(chunks),),
        out_specs=specs,
        out_shape=outs,
        scratch_shapes=[
            pltpu.VMEM((length, columns), BF16),
            pltpu.VMEM((length, columns), BF16),
            pltpu.VMEM((width, columns), F32),
            pltpu.SemaphoreType.DMA(()),
        ],
        cost=HEAVY,
        name=f"mlp_{chunks[0]}",
    )


def attend_back_kernel(sample, first, fetch, far_away, *rest):
    take = lambda n: (rest[:n], rest[n:])
    if first:
        (joined, probs, _, gatt), rest = take(4)
    else:
        (joined, probs, gone_ref, wproj_ref), rest = take(4)
    fetches, rest = take(fetch)
    (gjoined_ref,), rest = take(1)
    if not first:
        (gatt,), rest = take(1)
    fetched, rest = take(fetch)
    own = []
    if far_away:
        (joined_near, probs_near, joined_sem, probs_sems), rest = take(4)
        joined, joined_hbm, probs, probs_hbm = joined_near, joined, probs_near, probs
        own = brought([joined_hbm], [joined], joined_sem)
        for k in range(HEADS // 2):
            pair_of = lambda ref: ref.at[pl.ds(2 * k, 2)]
            own.append(pltpu.make_async_copy(pair_of(probs_hbm), pair_of(probs), probs_sems.at[k]))
    (sems,) = rest
    loads = brought(fetches, fetched, sems)
    j = pl.program_id(0)
    rows, width = gatt.shape

    @pl.when(j == 0)
    def _():
        for load in own[: PIECES + 2] if own else loads:
            load.start()
        if not first:
            gatt[...] = dot(gone_ref[sample], wproj_ref[...], NT).astype(BF16)

    if own:
        for k, load in enumerate(own[PIECES + 2 :]):
            pl.when(j == k + 1)(load.start)

        @pl.when(j == 1)
        def _():
            for load in loads:
                load.start()

    pair = first + j
    at = pl.multiple_of(pair * 128, 128)
    if far_away:
        for load in own[:PIECES]:
            pl.when(j == 0)(load.wait)
        here = pl.ds(2 * pair, 2)
        pltpu.make_async_copy(probs_hbm.at[here], probs.at[here], probs_sems.at[pair]).wait()
    q, k, v = [joined[:, pl.ds(pl.multiple_of(c * width + pair * 128, 128), 128)] for c in range(3)]
    g = gatt[:, pl.ds(at, 128)]
    k_t = k.T
    left = lax.broadcasted_iota(jnp.int32, (rows, 128), 1) < HALF
    g_q, g_k, g_v = [], [], []
    for h in range(2):
        weights = probs[2 * pair + h]
        weighted = weights.astype(F32) * dot(v, jnp.where(left == (h == 0), g, jnp.zeros_like(g)), NT)
        delta = jnp.sum(weighted, axis=0, keepdims=True)
        scores = (weighted - weights.astype(F32) * delta).astype(BF16)
        g_v.append(dot(weights, g))
        g_k.append(dot(scores, q))
        g_q.append(dot(k_t[h * HALF : (h + 1) * HALF], scores))
    gjoined_ref[:, pl.ds(at, 128)] = (jnp.concatenate(g_q, 0).T * HALF**-0.5).astype(BF16)
    at_k = pl.multiple_of(width + pair * 128, 128)
    at_v = pl.multiple_of(2 * width + pair * 128, 128)
    gjoined_ref[:, pl.ds(at_k, 128)] = jnp.where(left, g_k[0], g_k[1]).astype(BF16)
    gjoined_ref[:, pl.ds(at_v, 128)] = jnp.where(left, g_v[0], g_v[1]).astype(BF16)

    @pl.when(j == pl.num_programs(0) - 1)
    def _():
        for load in loads:
            load.wait()


def attend_back(sample, first, pairs, tokens, joined, probs, begin, go_on, fetches):
    rows, width = joined.shape[0], joined.shape[1] // 3
    far_away = sample == 0
    bring = far if far_away else near
    ops = bring(joined, probs)
    specs = [ANY if far_away else VMEM] * 2
    outs = [pltpu.VMEM((rows, 3 * width), BF16)]
    scratch, aliases = [], {}
    if first:
        ops += near(*go_on)
        specs += [VMEM] * 2
        aliases = {2: 0}
    else:
        ops += near(*begin)
        specs += [VMEM] * 2
        outs += [pltpu.VMEM((rows, width), BF16)]
    if far_away:
        scratch += [pltpu.VMEM(joined.shape, BF16), pltpu.VMEM(probs.shape, BF16)]
        scratch += [pltpu.SemaphoreType.DMA((PIECES,)), pltpu.SemaphoreType.DMA((HEADS // 2,))]
    fetch = len(fetches)
    n = len(outs)
    out = call(
        functools.partial(attend_back_kernel, sample, first, fetch, far_away),
        tokens,
        [*ops, *far(*fetches)],
        specs + [ANY] * fetch,
        18 if far_away else 9,
        aliases,
        grid=(pairs,),
        out_specs=[VMEM] * (n + fetch),
        out_shape=outs + [pltpu.VMEM(a.shape, a.dtype) for a in fetches],
        scratch_shapes=scratch + [pltpu.SemaphoreType.DMA((max(fetch * PIECES, 1),))],
        cost=HEAVY,
        name=f"attend_back_{sample}_{first}",
    )
    return out[:n], out[n:]


def weights_kernel(packed, half, g0_ref, g1_ref, a0_ref, a1_ref, *rest):
    if not half:
        (gone_ref, l0_ref, l1_ref), rest = rest[:3], rest[3:]
    sums_ref, dw_refs, result = rest[0], rest[1:-1], rest[-1]
    width = a0_ref.shape[0]
    part = width // 2
    for c in range(3):
        at = slice(c * width + half * part, c * width + (half + 1) * part)
        here = slice(c * part, (c + 1) * part)
        result[:, here] = dot(a0_ref[...], g0_ref[:, at]) + dot(a1_ref[...], g1_ref[:, at])
        total = row_sum(g0_ref[:, at]) + row_sum(g1_ref[:, at])
        sums_ref[:, here] = jnp.broadcast_to(total, (8, part))
    end = 3 * part
    if not half:
        result[:, end : end + width] = dot(l0_ref[...], gone_ref[0]) + dot(l1_ref[...], gone_ref[1])
        end += width
    result[:, end:] = jnp.zeros((width, result.shape[1] - end), F32)
    if packed:
        orders = ((LAST, Z_FIRST + (Z1,)), (LAST,))[half]
        share = result.shape[1] // len(orders)
        for i, order in enumerate(orders):
            cut = (i * share, (i + 1) * share)
            store_packed(*dw_refs[2 * i : 2 * i + 2], order, place()[0], result, columns=cut)
    else:
        dw_refs[0][...] = result[...]


def weights(packed, half, tokens, g0, g1, a0, a1, proj=()):
    width = a0.shape[0]
    part = width // 2
    columns = -(-(3 * part + (0 if half else width)) // 256) * 256
    if packed:
        tiles = columns // 128 // (1 if half else 2)
        grads = [pltpu.VMEM((16, tiles * PER, 128), BF16)] * (2 if half else 4)
    else:
        grads = [pltpu.VMEM((width, columns), F32)]
    ops = near(g0, g1, a0, a1, *proj)
    return call(
        functools.partial(weights_kernel, packed, half),
        tokens,
        ops,
        [VMEM] * len(ops),
        10,
        out_specs=[VMEM] * (1 + len(grads)),
        out_shape=[pltpu.VMEM((8, 3 * part), F32)] + grads,
        scratch_shapes=[pltpu.VMEM((width, columns), F32)],
        cost=HEAVY,
        name=f"weights_{half}",
    )


def token_rows(sample, g_ref, w_ref, x_ref, gmid_ref, ids_ref, vec_ref, pgrad_refs, grad_t, hot):
    rows, width = x_ref.shape
    positions = hot.shape[0]
    piece = pgrad_refs[0].shape[0]
    tile = 2 * piece
    g_gain = jnp.zeros((1, width), F32)
    g_bias = jnp.zeros((1, width), F32)
    for t in range(rows // tile):
        cut = slice(t * tile, (t + 1) * tile)
        grad = dot(g_ref[cut], w_ref[...], NT)
        normed, inverse = normalize(x_ref[cut])
        gmid = gmid_ref[sample * rows + t * tile : sample * rows + (t + 1) * tile]
        total = gmid + normalize_back(grad * vec_ref[0:1], normed, inverse)
        low = total.astype(BF16)
        for p in range(2):
            pgrad_refs[2 * t + p][...] = low[p * piece : (p + 1) * piece]
        grad_t[:, cut] = low.T
        g_gain = g_gain + row_sum(grad * normed)
        g_bias = g_bias + row_sum(grad)
        wanted = ids_ref[0:1, cut].astype(jnp.int32)
        iota = lax.broadcasted_iota(jnp.int32, (positions, tile), 0)
        hot[:, cut] = (iota == wanted).astype(F32).astype(BF16)
    return g_gain, g_bias


def finish_first_kernel(g_ref, w_ref, x_ref, gmid_ref, ids_ref, vec_ref, own, core, far_own, table, sums, grad_t, hot):
    g_gain, g_bias = token_rows(
        0, g_ref, w_ref, x_ref, gmid_ref, ids_ref, vec_ref, (own, core.at[0], far_own, core.at[1]), grad_t, hot
    )
    sums[...] = jnp.concatenate([g_gain, g_bias, jnp.zeros((6, g_gain.shape[1]), F32)], 0)
    table[...] = dot(grad_t[...], hot[...], NT)


def finish_kernel(
    packed, g_ref, w_ref, x_ref, gmid_ref, ids_ref, vec_ref, small_ref, sums0_ref, sums1_ref, db1a_ref, db1b_ref,
    table_ref, before_ref, own, core, far_own, *rest,
):
    dw_refs, (grad_t, hot, result) = rest[:-3], rest[-3:]
    pgrad_refs = (own, core.at[0], far_own, core.at[1])
    width = x_ref.shape[1]
    positions = hot.shape[0]
    part = width // 2
    me = place()[0]
    g_gain, g_bias = token_rows(1, g_ref, w_ref, x_ref, gmid_ref, ids_ref, vec_ref, pgrad_refs, grad_t, hot)
    columns = lambda c: jnp.concatenate([ref[0:1, c * part : (c + 1) * part] for ref in (sums0_ref, sums1_ref)], 1)
    few = [g_gain + before_ref[0:1], g_bias + before_ref[1:2], columns(0), columns(2), small_ref[3:4], small_ref[0:3]]
    few = jnp.concatenate(few + [jnp.zeros((120, width), F32)], 0).T
    result[:, 0:positions] = table_ref[...] + dot(grad_t[...], hot[...], NT)
    result[:, positions:] = few
    if packed:
        half = (me // Z1) % 2
        a, b = db1a_ref[...], db1b_ref[...]
        sums = jnp.concatenate([jnp.where(half == 0, a, b), jnp.where(half == 0, b, a)], 0)
        share = 96
        for owner in range(32):
            c, start = owner // 8, owner % 8 * share
            row = jnp.concatenate([jnp.zeros((1, 16), F32), sums[c : c + 1, start : start + share], jnp.zeros((1, 16), F32)], 1)
            result[owner * PER : owner * PER + 1, positions:] += row
        store_packed(*dw_refs, LAST, me, result)
    else:
        dw_refs[0][...] = result[...]


def finish(packed, last, tokens, ops, positions):
    rows, width = ops[2].shape
    columns = positions + 128
    share = (rows // 4, width)
    outs = [pltpu.VMEM(share, BF16), pltpu.VMEM((2,) + share, BF16), pltpu.VMEM(share, BF16)]
    scratch = [pltpu.VMEM((width, rows), BF16), pltpu.VMEM((positions, rows), BF16)]
    if not last:
        outs += [pltpu.VMEM((width, positions), F32), pltpu.VMEM((8, width), F32)]
    else:
        scratch += [pltpu.VMEM((width, columns), F32)]
        if packed:
            outs += [pltpu.VMEM((16, PER * columns // 128, 128), BF16)] * 2
        else:
            outs += [pltpu.VMEM((width, columns), F32)]
    return call(
        functools.partial(finish_kernel, packed) if last else finish_first_kernel,
        tokens,
        near(*ops),
        [VMEM] * len(ops),
        14,
        out_specs=[VMEM] * len(outs),
        out_shape=outs,
        scratch_shapes=scratch,
        cost=HEAVY,
        name=f"finish_{int(last)}",
    )


def swap_bit(x, bit, count):
    return lax.ppermute(x, AXES, [(d, d ^ bit) for d in range(count)])


def add(arrays):
    return sum(a.astype(F32) for a in arrays)


def fold_kernel(counts, *refs):
    n = 2 * sum(counts)
    pairs, outs = refs[:n], refs[n:]
    for k, count in enumerate(counts):
        message, stay = outs[2 * k : 2 * k + 2]
        half = message.shape[0]
        row = 0
        for at in range(0, 2 * count, 2):
            rows = pairs[at].shape[1]
            here = slice(row, row + rows)
            for i in range(half):
                message[i, here] = pairs[at][half + i] + pairs[at + 1][half + i]
            for i in range(half):
                stay[i, here] = pairs[at][i] + pairs[at + 1][i]
            row += rows
        pairs = pairs[2 * count :]


class Sums:
    def __init__(self, count, order):
        self.count, self.bits, self.pairs = count, list(order), []

    def swap(self, send, bit):
        return lax.ppermute(send, AXES, [(d, d ^ bit) for d in range(self.count)])

    def begin(self, keep, send):
        got = self.swap(send, self.bits[0])
        self.pairs += [keep, got]
        return got


def fold(tokens, *sums, cost=LIGHT):
    outs = []
    for one in sums:
        owners, _, lanes = one.pairs[0].shape
        rows = sum(a.shape[1] for a in one.pairs[::2])
        outs += [pltpu.VMEM((owners // 2, rows, lanes), BF16)] * 2
    pairs = [a for one in sums for a in one.pairs]
    out = call(
        functools.partial(fold_kernel, [len(one.pairs) // 2 for one in sums]),
        tokens,
        near(*pairs),
        [VMEM] * len(pairs),
        2,
        out_specs=[VMEM] * len(outs),
        out_shape=outs,
        cost=cost,
        name="fold",
    )
    for one, message, stay in zip(sums, out[::2], out[1::2]):
        one.bits = one.bits[1:]
        one.pairs = [stay, one.swap(message, one.bits[0])]
    return tuple(out[::2])


def turn_kernel(a0, a1, b0, b1, c0, c1, out):
    n = 12 * PER
    out[:, 0:768] = add([c0[0], c1[0]]).astype(BF16)
    for at, pair in ((768, (a0, a1)), (1152, (b0, b1))):
        for k in range(6):
            rows = slice(n + 48 * k, n + 48 * (k + 1))
            value = add([a[0, rows] for a in pair]).astype(BF16)
            out[48 * (k // 3) : 48 * (k // 3 + 1), at + 128 * (k % 3) : at + 128 * (k % 3 + 1)] = value


def hidden_kernel(a0, a1, b0, b1, c0, c1, other, dw1, dw2):
    n = 12 * PER
    low = (place()[0] // Z1) % 2 == 0
    dw2[...] = add([c0[0], c1[0], other[:, 0:768]])
    for k in range(6):
        rows = slice(48 * k, 48 * (k + 1))
        block = lambda at: other[48 * (k // 3) : 48 * (k // 3 + 1), at + 128 * (k % 3) : at + 128 * (k % 3 + 1)]
        mine = add([a0[0, rows], a1[0, rows], block(1152)])
        theirs = add([b0[0, rows], b1[0, rows], block(768)])
        for e, half in enumerate((jnp.where(low, mine, theirs), jnp.where(low, theirs, mine))):
            for i in range(2):
                at = (12 * e + 2 * k + i) * 128
                dw1[:, at : at + 128] = half[i * PER : (i + 1) * PER]


def tiles_kernel(counts, layout, *refs):
    n = sum(counts)
    held, outs, result = refs[:n], refs[n:-1], refs[-1]
    row, at = 0, 0
    for count in counts:
        rows = held[at].shape[1]
        result[row : row + rows] = add([ref[0] for ref in held[at : at + count]])
        row, at = row + rows, at + count
    layout(result, outs)


def put_tiles(result, row, out, columns):
    for c in range(columns // 128):
        out[:, c * 128 : (c + 1) * 128] = result[row + c * PER : row + (c + 1) * PER]


def rest_layout(result, outs):
    dwqkv, dwproj, table, *few = outs
    width = dwproj.shape[1]
    part = width // 2
    tiles = lambda n: n // 128 * PER
    second = tiles(5 * part + 128)
    for c in range(3):
        for half, row in enumerate((0, second)):
            at = c * width + half * part
            put_tiles(result, row + tiles(c * part), dwqkv.at[:, at : at + part], part)
    put_tiles(result, tiles(3 * part), dwproj, width)
    third = second + tiles(3 * part + 128)
    put_tiles(result, third, table, table.shape[1])
    at = third + tiles(table.shape[1])
    tile = result[at : at + PER]
    for k in range(8):
        few[k][...] = jnp.sum(jnp.where(lax.broadcasted_iota(jnp.int32, (PER, 128), 1) == k, tile, 0.0), axis=1)
    few[8][...] = tile[0, 16:112]


def tiles(streams, layout, outs, name):
    arrays = [a for held in streams for a in held]
    rows = sum(held[0].shape[1] for held in streams)
    first = lambda a: pl.BlockSpec((1,) + a.shape[1:], lambda i: (0, 0, 0))
    return call(
        functools.partial(tiles_kernel, [len(held) for held in streams], layout),
        (),
        arrays,
        [first(a) for a in arrays],
        8,
        grid=(1,),
        out_specs=[pl.BlockSpec(shape, lambda i, n=len(shape): (0,) * n) for shape in outs],
        out_shape=[jax.ShapeDtypeStruct(shape, F32) for shape in outs],
        scratch_shapes=[pltpu.VMEM((rows, 128), F32)],
        name=name,
    )


def shards(
    patches, pos_ids, lengths, pos_table, ln1_gain, ln1_bias, w_qkv, q_bias, v_bias, w_proj, proj_bias,
    ln2_gain, ln2_bias, w_fc1, fc1_bias, w_fc2, fc2_bias, cotangent, *, wide, parts,
):
    width = patches.shape[2]
    hidden, positions = w_fc1.shape[1], pos_table.shape[1]
    count = wide * parts
    packed = wide == 8 and parts == 4
    hop = lambda a, k: lax.ppermute(a, "blk", [(d, d ^ k) for d in range(parts)])

    def across(own, core, far_own, *tokens):
        got = hop(core, 1)
        message = join(tokens, far_own, got)
        return message, (own, got, hop(message, 2))

    vectors = (ln1_gain, ln1_bias, q_bias, v_bias, proj_bias, ln2_gain, ln2_bias, fc2_bias, fc1_bias)
    message, xs = across(*prepare_first(pos_ids, patches))
    ys, cots, (vec, table, wqkv, wproj) = prepare_second(
        (message,), pos_ids, patches, cotangent, vectors, (pos_table, w_qkv, w_proj)
    )
    message, ys = across(*ys, xs[2])
    mid0, ids0, probs0, _, (x0, joined0, in0, low0_t) = attend(
        0, (message,), lengths, xs, table, vec, wqkv, wproj, ()
    )
    message, cots = across(*cots, ys[2])
    mid1, ids1, probs1, (w1, w2), (x1, joined1, in1, low1_t) = attend(
        1, (message,), lengths, ys, table, vec, wqkv, wproj, (w_fc1, w_fc2)
    )
    run = functools.partial(mlp, packed)
    *held, db1a = run((), (0, 1), mid0, mid1, w1, w2, vec, cots=cots)
    if packed:
        *held, db1a, a, b, c, d = held + [db1a]
        sum1 = Sums(count, X_FIRST), Sums(count, Z_FIRST)
        sum2 = Sums(count, X_FIRST), Sums(count, Z_FIRST)
        sum1[0].begin(a, b)
        sum1[1].begin(c, d)
        *held[3:], db1b, a, b, c, d = run((), (2,), mid0, mid1, w1, w2, vec, held=held)
        messages = fold((db1b,), *sum1)
        _, gmid, db1b, a, b, c, d, gone, small, wproj, *mixed = run(
            messages, (3,), mid0, mid1, w1, w2, vec, held=held, grads=(db1b, a, b, c, d), w_proj=w_proj
        )
        sum2[0].begin(a, b)
        sum2[1].begin(c, d)
    else:
        *held, db1a, a, b = held + [db1a]
        grads1 = a, b
        _, gmid, db1b, a, b, gone, small, wproj, *mixed = run(
            (), (2, 3), mid0, mid1, w1, w2, vec, held=held, w_proj=w_proj
        )
        grads2 = a, b
    tokens = fold((), *sum1) if packed else ()
    (g0, *_), (joined1, probs1) = attend_back(
        0, 0, 6, tokens, joined0, probs0, (gone, wproj), (), (joined1, probs1)
    )
    tokens = (g0,)
    if packed:
        tokens = fold(tokens, *sum1, *sum2)
    message, mixed = across(*mixed, *tokens)
    (g1, *state), (in0, in1, low0_t, low1_t, wqkv, x0, x1) = attend_back(
        1, 0, 3, tokens + (message,), joined1, probs1, (gone, wproj), (), (in0, in1, low0_t, low1_t, w_qkv, x0, x1)
    )
    sums0, *dwa = weights(packed, 0, (), g0, g1, in0, in1, (gone, low0_t, low1_t))
    if packed:
        sum3 = Sums(count, LAST), Sums(count, Z_FIRST + (Z1,))
        sum3[0].begin(*dwa[:2])
        sum3[1].begin(*dwa[2:])
    *pgrad0, table0, before = finish(packed, False, (sums0,), (g0, wqkv, x0, gmid, ids0, vec), positions)
    tokens = (before, mixed[2])
    if packed:
        tokens += (sum1[0].pairs[1], sum1[1].pairs[1])
        tokens += fold(tokens, *sum2, *sum3)
    (g1,), _ = attend_back(1, 3, 3, tokens, joined1, probs1, (), (g1, *state), ())
    tokens = (g1,)
    if packed:
        tokens = fold(tokens, *sum2)
    message, pgrad0 = across(*pgrad0, *tokens)
    sums1, *dwb = weights(packed, 1, tokens + (message,), g0, g1, in0, in1)
    tokens = (sums1,)
    if packed:
        sum4, sum5 = Sums(count, LAST), Sums(count, LAST)
        sum4.begin(*dwb)
        tokens = fold(tokens, *sum3) + (sum2[0].pairs[1], sum2[1].pairs[1])
    *pgrad1, a, b = tuple(
        finish(
            packed,
            True,
            tokens,
            (g1, wqkv, x1, gmid, ids1, vec, small, sums0, sums1, db1a, db1b, table0, before),
            positions,
        )
    ) + (() if packed else (None,))
    tokens = ()
    if packed:
        sum5.begin(a, b)
        tokens = fold((sum3[0].pairs[1], sum3[1].pairs[1], pgrad0[2]), sum4, cost=HEAVY)
        send = call(
            turn_kernel,
            tokens,
            near(*sum1[0].pairs, *sum2[0].pairs, *sum2[1].pairs),
            [VMEM] * 6,
            2,
            out_specs=VMEM,
            out_shape=pltpu.VMEM((96, 2 * width), BF16),
            name="turn",
        )
        other = sum4.swap(send, Z1)
        tokens = fold((send,), sum5)
    message, pgrad1 = across(*pgrad1, *tokens)
    if packed:
        tokens = fold((message, pgrad1[2]), sum4, *sum3)
        message = tokens[0]
        tokens = fold(tokens, sum5)
        tokens = fold(tokens + (other,), sum4)
        sum3[0].pairs += sum3[1].pairs
        tokens += fold(tokens, sum3[0])
        fold(tokens, sum5)
        sum4.pairs += sum5.pairs
        fold((), sum4)
    mixed, pgrad = gather((message,), mixed), gather((), pgrad0, pgrad1)
    if packed:
        ops = near(*sum1[0].pairs, *sum2[0].pairs, *sum1[1].pairs, other)
        dw1, dw2 = call(
            hidden_kernel,
            tokens,
            ops,
            [VMEM] * 7,
            2,
            out_specs=[VMEM] * 2,
            out_shape=[jax.ShapeDtypeStruct((n // count, hidden + width - n), F32) for n in (width, hidden)],
            name="hidden",
        )
        shapes = [(width // count, n) for n in (3 * width, width, positions)]
        shapes += [(width // count,)] * 8 + [(hidden // count,)]
        dwqkv, dwproj, table, *few = tiles([sum3[0].pairs, sum4.pairs], rest_layout, shapes, "rest")
    else:
        share = lambda a: lax.psum_scatter(a.astype(BF16), AXES, scatter_dimension=0, tiled=True).astype(F32)
        dw1 = share(jnp.concatenate([grads1[0], grads2[0]], 1))
        dw2 = share(jnp.concatenate([grads1[1], grads2[1]], 0))
        dwa, dwb, misc = share(dwa[0]), share(dwb[0]), share(a)
        n = width // 2
        dwqkv = jnp.concatenate([x[:, c * n : (c + 1) * n] for c in range(3) for x in (dwa, dwb)], 1)
        dwproj = dwa[:, 3 * n : 3 * n + width]
        table, few = misc[:, :positions], [misc[:, positions + k] for k in range(8)]
        few.append(share(jnp.concatenate([db1a, db1b], 0).reshape(-1)))
    (g_gain1, g_bias1, g_q, g_v, g_proj, g_gain2, g_bias2, g_fc2, g_fc1) = few
    return (
        mixed, pgrad, table, g_gain1, g_bias1, dwqkv, g_q, g_v, dwproj, g_proj, g_gain2, g_bias2,
        dw1, g_fc1, dw2, g_fc2,
    )


def solution(mesh):
    wide, parts = mesh.shape["wide"], mesh.shape["blk"]
    tokens = P("wide", "blk", None)
    in_specs = (tokens, P("wide", "blk"), P("wide")) + (P(),) * 14 + (tokens,)
    vector, matrix = P(AXES), P(AXES, None)
    out_specs = (
        tokens, tokens, matrix, vector, vector, matrix, vector, vector, matrix, vector, vector, vector,
        matrix, vector, matrix, vector,
    )
    return jax.shard_map(
        functools.partial(shards, wide=wide, parts=parts),
        mesh=mesh, in_specs=in_specs, out_specs=out_specs, check_vma=False,
    )
```

```python
import functools

import jax
import jax.numpy as jnp
from jax import lax
from jax.experimental import pallas as pl
from jax.experimental.pallas import tpu as pltpu
from jax.sharding import PartitionSpec as P

HEADS = 12
HALF = 64
F32, BF16 = jnp.float32, jnp.bfloat16
NN = (((1,), (0,)), ((), ()))
NT = (((1,), (1,)), ((), ()))
TN = (((0,), (0,)), ((), ()))
EPS = 1e-6
MASKED = -1e30
AXES = ("wide", "blk")
MIB = 2**20
CORE, Y, X, Z0, Z1 = 1, 2, 4, 8, 16
X_FIRST = (CORE, X, Y, Z0)
Z_FIRST = (CORE, Z0, X, Y)
HIDDEN = ((X_FIRST, (CORE, Z0, Y, X)), ((CORE, X, Z0, Y), Z_FIRST))
LAST = (CORE, X, Z0, Y, Z1)
PER = 24
LIGHT = pl.CostEstimate(flops=1, bytes_accessed=1, transcendentals=0)
HEAVY = pl.CostEstimate(flops=10**11, bytes_accessed=1, transcendentals=0)
VMEM = pl.BlockSpec(memory_space=pltpu.VMEM)
ANY = pl.BlockSpec(memory_space=pl.ANY)
SMEM = pl.BlockSpec(memory_space=pltpu.SMEM)


def dot(a, b, dims=NN):
    return lax.dot_general(a, b, dims, preferred_element_type=F32)


def near(*arrays):
    return [pltpu.with_memory_space_constraint(a, pltpu.VMEM) for a in arrays]


def far(*arrays):
    return [pltpu.with_memory_space_constraint(a, pltpu.HBM) for a in arrays]


def call(body, tokens, ops, in_specs, vmem, aliases=None, cost=LIGHT, **rest):
    n = len(tokens)
    return pl.pallas_call(
        lambda *refs: body(*refs[n:]),
        in_specs=[ANY] * n + in_specs,
        input_output_aliases={n + a: b for a, b in (aliases or {}).items()},
        compiler_params=pltpu.CompilerParams(vmem_limit_bytes=int(vmem * MIB)),
        cost_estimate=cost,
        **rest,
    )(*tokens, *ops)


PIECES = 4


def brought(sources, targets, sems):
    copies = []
    for a, b in zip(sources, targets):
        step = a.shape[0] // PIECES
        for i in range(PIECES):
            here = pl.ds(i * step, step)
            copies.append(pltpu.make_async_copy(a.at[here], b.at[here], sems.at[len(copies)]))
    return copies


def place():
    lane = lax.axis_index("blk")
    return lax.axis_index("wide") * lax.axis_size("blk") + lane, lane


def normalize(x):
    center = x - jnp.mean(x, axis=-1, keepdims=True)
    inverse = lax.rsqrt(jnp.mean(center * center, axis=-1, keepdims=True) + EPS)
    return center * inverse, inverse


def normalize_back(g, normed, inverse):
    return inverse * (
        g - jnp.mean(g, axis=-1, keepdims=True) - normed * jnp.mean(g * normed, axis=-1, keepdims=True)
    )


def gelu_both(x):
    cdf = 0.5 + 0.5 * lax.erf(x * 0.7071067811865476)
    return x * cdf, cdf + x * (jnp.exp(x * x * -0.5) * 0.3989422804014327)


def row_sum(x):
    return jnp.sum(x.astype(F32), axis=0, keepdims=True)


def relative(position, order):
    return sum(bit for i, bit in enumerate(order) if (position >> (len(order) - 1 - i)) & 1)


def store_packed(keep_ref, send_ref, order, me, result_ref, base=0, extra=0, columns=None):
    half = 2 ** (len(order) - 1)
    first, last = columns or (0, result_ref.shape[1])
    for position in range(2 * half):
        ref = (keep_ref, send_ref)[position // half]
        start = pl.multiple_of((me ^ (relative(position, order) | extra)) * PER, 8)
        for c in range((last - first) // 256):
            two = [result_ref[pl.ds(start, PER), first + (2 * c + i) * 128 : first + (2 * c + i + 1) * 128] for i in range(2)]
            here = pl.ds(base + 2 * c * PER, 2 * PER)
            ref[position % half, here] = jnp.concatenate(two, 0).astype(BF16)


def lay(own, core, far_own):
    return own, core.at[0], far_own, core.at[1]


def pieces(sample, ids_ref, outs, lane_me):
    piece = ids_ref.shape[1]
    for k, out in enumerate(lay(*outs)):
        ids = ids_ref[pl.ds(2 * (lane_me ^ k) + sample, 1)]
        row = jnp.concatenate([ids >> 8, ids & 255, jnp.zeros((1, out.shape[1] - 2 * piece), jnp.int32)], 1)
        out[piece : piece + 16] = jnp.broadcast_to(row.astype(F32), (16, out.shape[1])).astype(BF16)


def first_kernel(patches_ref, ids_hbm, own, core, far_own, ids_ref, sems):
    piece = patches_ref.shape[1]
    lane_me = place()[1]
    copies = [pltpu.make_async_copy(ids_hbm, ids_ref, sems.at[4])]
    for k, out in enumerate(lay(own, core, far_own)):
        copies.append(pltpu.make_async_copy(patches_ref.at[2 * (lane_me ^ k)], out.at[0:piece], sems.at[k]))
    for copy in copies:
        copy.start()
    copies[0].wait()
    pieces(0, ids_ref, (own, core, far_own), lane_me)
    for copy in copies[1:]:
        copy.wait()


def second_kernel(patches_ref, cot_ref, ids_hbm, *refs):
    vectors, big, refs = refs[:9], refs[9:12], refs[12:]
    second, cots, vec_ref, loaded = refs[:3], refs[3:6], refs[6], refs[7:10]
    ids_ref, raw, sems = refs[10], refs[11:-1], refs[-1]
    piece, width = patches_ref.shape[1:]
    lane_me = place()[1]
    copies = []

    def start(a, b):
        copies.append(pltpu.make_async_copy(a, b, sems.at[len(copies)]))
        copies[-1].start()
        return copies[-1]

    few = [start(ids_hbm, ids_ref)] + [start(a, b) for a, b in zip(vectors, raw)]
    for k, out in enumerate(lay(*second)):
        start(patches_ref.at[2 * (lane_me ^ k) + 1], out.at[0:piece])
    for a, b in zip(big, loaded):
        start(a, b)
    for k, out in enumerate(lay(*cots)):
        start(cot_ref.at[pl.ds(2 * (lane_me ^ k), 2)], out)
    for copy in few:
        copy.wait()
    pieces(1, ids_ref, second, lane_me)
    row = 0
    for ref in raw:
        for k in range(ref.shape[0] // width):
            vec_ref[row : row + 1] = ref[k * width : (k + 1) * width].astype(F32).reshape(1, width)
            row += 1
    vec_ref[row:] = jnp.zeros((vec_ref.shape[0] - row, width), F32)
    for copy in copies[len(few) :]:
        copy.wait()


def message_shapes(shape):
    return [pltpu.VMEM(shape, BF16), pltpu.VMEM((2,) + shape, BF16), pltpu.VMEM(shape, BF16)]


def prepare_first(pos_ids, patches):
    _, piece, width = patches.shape
    return call(
        first_kernel,
        (),
        far(patches, pos_ids),
        [ANY] * 2,
        2,
        out_specs=[VMEM] * 3,
        out_shape=message_shapes((piece + 16, width)),
        scratch_shapes=[pltpu.VMEM(pos_ids.shape, pos_ids.dtype), pltpu.SemaphoreType.DMA((5,))],
        name="first",
    )


def prepare_second(tokens, pos_ids, patches, cotangent, vectors, big):
    _, piece, width = patches.shape
    out = call(
        second_kernel,
        tokens,
        far(patches, cotangent, pos_ids, *vectors, *big),
        [ANY] * (3 + len(vectors) + len(big)),
        2,
        out_specs=[VMEM] * (7 + len(big)),
        out_shape=message_shapes((piece + 16, width))
        + message_shapes((2, piece, width))
        + [pltpu.VMEM((16, width), F32)]
        + [pltpu.VMEM(a.shape, a.dtype) for a in big],
        scratch_shapes=[
            pltpu.VMEM(pos_ids.shape, pos_ids.dtype),
            *[pltpu.VMEM(a.shape, a.dtype) for a in vectors],
            pltpu.SemaphoreType.DMA((9 + len(vectors) + len(big),)),
        ],
        cost=HEAVY,
        name="second",
    )
    return out[:3], out[3:6], out[6:]


def join_kernel(a_ref, b_ref, out, sems):
    copies = [
        pltpu.make_async_copy(a_ref, out.at[0], sems.at[0]),
        pltpu.make_async_copy(b_ref.at[1], out.at[1], sems.at[1]),
    ]
    for copy in copies:
        copy.start()
    for copy in copies:
        copy.wait()


def join(tokens, far_own, got):
    return call(
        join_kernel,
        tokens,
        near(far_own, got),
        [VMEM] * 2,
        1,
        out_specs=VMEM,
        out_shape=pltpu.VMEM(got.shape, BF16),
        scratch_shapes=[pltpu.SemaphoreType.DMA((2,))],
        name="join",
    )


def gather_kernel(samples, *refs):
    sets, out, done, sems = refs[: 3 * samples], refs[-3], refs[-2], refs[-1]
    done[...] = jnp.zeros_like(done)
    lane_me = place()[1]
    copies = []
    for s in range(samples):
        own, got, other = sets[3 * s : 3 * s + 3]
        for k, a in enumerate((own, got.at[0], other.at[0], other.at[1])):
            at = 2 * (lane_me ^ k) + s
            where = out.at[pl.ds(at, 2)] if samples == 1 else out.at[at]
            copies.append(pltpu.make_async_copy(a, where, sems.at[4 * s + k]))
            copies[-1].start()
    for copy in copies:
        copy.wait()


def gather(tokens, *sets):
    ops = near(*[a for one in sets for a in one])
    return call(
        functools.partial(gather_kernel, len(sets)),
        tokens,
        ops,
        [VMEM] * len(ops),
        1,
        out_specs=[ANY, VMEM],
        out_shape=[pltpu.HBM((8,) + ops[0].shape[-2:], BF16), pltpu.VMEM((8, 128), F32)],
        scratch_shapes=[pltpu.SemaphoreType.DMA((4 * len(sets),))],
        name="gather",
    )


def attend_kernel(
    sample, fetch, lengths_ref, own_ref, got_ref, other_ref, table_ref, vec_ref, wqkv_ref, wproj_ref, *rest
):
    fetches, rest = rest[:fetch], rest[fetch:]
    mid_ref, ids_ref, probs_ref, rest = rest[0], rest[1], rest[2], rest[3:]
    fetched, rest = rest[:fetch], rest[fetch:]
    outs, (stream, joined, attn_in, attn_in_t, low, low_t, hidden, sems, fetch_sems) = rest[:4], rest[4:]
    saved = (stream, joined, attn_in_t, low_t)
    copies = [pltpu.make_async_copy(a, b, sems.at[i]) for i, (a, b) in enumerate(zip(saved, outs))]
    loads = brought(fetches, fetched, fetch_sems)
    j = pl.program_id(0)
    pieces = (own_ref, got_ref.at[0], other_ref.at[0], other_ref.at[1])
    rows, width = stream.shape
    piece = rows // len(pieces)

    @pl.when(j == 0)
    def _():
        for load in loads:
            load.start()
        positions = table_ref.shape[1]
        ids = []
        for k, ref in enumerate(pieces):
            coded = ref[piece : piece + 16].astype(F32)
            ids.append(coded[0:8, 0:piece] * 256.0 + coded[0:8, piece : 2 * piece])
        ids_ref[...] = jnp.concatenate(ids, 1)
        for k, ref in enumerate(pieces):
            here = slice(k * piece, (k + 1) * piece)
            column = jnp.broadcast_to(ids[k][0:1], (piece, piece)).T.astype(jnp.int32)
            iota = lax.broadcasted_iota(jnp.int32, (piece, piece), 1)
            onehot = jnp.concatenate([(column == iota + piece * c).astype(F32) for c in range(positions // piece)], 1)
            value = ref[0:piece].astype(F32) + dot(onehot.astype(BF16), table_ref[...], NT)
            stream[here] = value
            normed, _ = normalize(value)
            normed = (normed * vec_ref[0:1] + vec_ref[1:2]).astype(BF16)
            attn_in[here] = normed
            attn_in_t[:, here] = normed.T
        copies[0].start()
        copies[2].start()
        for c in range(3):
            cols = slice(c * width, (c + 1) * width)
            part = dot(attn_in[...], wqkv_ref[:, cols])
            if c != 1:
                part = part + vec_ref[2 + c // 2 : 3 + c // 2]
            part = part.astype(BF16)
            if c == 0:
                part = part * jnp.asarray(HALF**-0.5, BF16)
            joined[:, cols] = part
        copies[1].start()
        lane_me = place()[1]
        length = lengths_ref[2 * lane_me + sample]
        part = lax.broadcasted_iota(jnp.int32, (piece, 128), 0)
        for i in range(len(pieces)):
            visible = part + (lane_me ^ i) * piece < length
            hidden[i * piece : (i + 1) * piece] = jnp.where(visible, 0.0, MASKED)

    at = pl.multiple_of(j * 128, 128)
    q = joined[:, pl.ds(at, 128)]
    k = joined[:, pl.ds(pl.multiple_of(width + j * 128, 128), 128)]
    v = joined[:, pl.ds(pl.multiple_of(2 * width + j * 128, 128), 128)]
    v_t = v.T
    lane = lax.broadcasted_iota(jnp.int32, (rows, 128), 1)
    ones = jnp.ones((16, rows), BF16)
    heads = []
    for h in range(2):
        own = (lane < HALF) == (h == 0)
        spare = lane == HALF * (1 - h)
        q_h = jnp.where(own, q, jnp.where(spare, 1.0, 0.0).astype(BF16))
        k_h = jnp.where(own, k, jnp.where(spare, hidden[...], 0.0).astype(BF16))
        scores = dot(k_h, q_h, NT)
        weights = jnp.exp(scores - jnp.max(scores, axis=0, keepdims=True)).astype(BF16)
        out = dot(jnp.concatenate([v_t[h * HALF : (h + 1) * HALF], ones], 0), weights)
        inverse = 1.0 / out[HALF : HALF + 1]
        probs_ref[h] = weights * inverse.astype(BF16)
        heads.append(out[0:HALF] * inverse)
    heads = jnp.concatenate(heads, 0)
    low_t[pl.ds(at, 128)] = heads.astype(BF16)
    low[:, pl.ds(at, 128)] = heads.T.astype(BF16)

    @pl.when(j == pl.num_programs(0) - 1)
    def _():
        copies[3].start()
        mid_ref[...] = stream[...] + dot(low[...], wproj_ref[...]) + vec_ref[4:5]
        for copy in copies + loads:
            copy.wait()


def attend(sample, tokens, lengths, pieces, table, vec, w_qkv, w_proj, fetches):
    rows = 4 * (pieces[0].shape[0] - 16)
    width = w_proj.shape[0]
    fetch = len(fetches)
    saved = [
        ((rows, width), F32),
        ((rows, 3 * width), BF16),
        ((width, rows), BF16),
        ((width, rows), BF16),
    ]
    stream, joined, attn_in_t, low_t = [pltpu.VMEM(*a) for a in saved]
    low = pltpu.VMEM((rows, width), BF16)
    mid, ids, probs, *rest = call(
        functools.partial(attend_kernel, sample, fetch),
        tokens,
        [lengths, *near(*pieces, table, vec, w_qkv, w_proj), *far(*fetches)],
        [SMEM] + [VMEM] * 7 + [ANY] * fetch,
        13,
        grid=(HEADS // 2,),
        out_specs=[VMEM] * 2 + [pl.BlockSpec((2, rows, rows), lambda j: (j, 0, 0))] + [VMEM] * fetch + [ANY] * 4,
        out_shape=[pltpu.VMEM((rows, width), F32), pltpu.VMEM((8, rows), F32)]
        + [pltpu.HBM((HEADS, rows, rows), BF16)]
        + [pltpu.VMEM(a.shape, a.dtype) for a in fetches]
        + [pltpu.HBM(*a) for a in saved],
        scratch_shapes=[stream, joined, pltpu.VMEM((rows, width), BF16), attn_in_t, low, low_t]
        + [pltpu.VMEM((rows, 128), F32)]
        + [pltpu.SemaphoreType.DMA((4,)), pltpu.SemaphoreType.DMA((max(fetch * PIECES, 1),))],
        cost=HEAVY,
        name=f"attend_{sample}",
    )
    return mid, ids, probs, rest[:fetch], rest[fetch:]


def mlp_kernel(packed, begin, end, chunks, x0_ref, x1_ref, w1_ref, w2_ref, vec_ref, *rest):
    take = lambda n: (rest[:n], rest[n:])
    if begin:
        (own_ref, got_ref, other_ref), rest = take(3)
        cots = (own_ref, got_ref.at[0], other_ref.at[0], other_ref.at[1])
        (mlp_in, mlp_in_t, gt, acc, gacc), rest = take(5)
    else:
        (mlp_in, mlp_in_t, gt), rest = take(3)
        rest = rest[2:]
        if chunks[0] % 2:
            rest = rest[3:]
        if end:
            (wproj_ref,), rest = take(1)
        (acc, gacc), rest = take(2)
    (db1_ref, *dw_refs), rest = take(3)
    if end:
        (gone_ref, small_ref, wproj_out, own, core, far_own), rest = take(6)
        (gmid_out,), rest = take(1)
        gmid_sems, rest = rest[-1], rest[:-1]
        mixed_refs = (own, core.at[0], far_own, core.at[1])
    act, gpre, result, sem = rest
    j = pl.program_id(0)
    xs = (x0_ref, x1_ref)
    rows, width = x0_ref.shape
    columns = result.shape[1]
    tile = rows // 2
    piece = tile // 2
    per_sample = rows // tile
    tiles = len(xs) * per_sample
    me = place()[0]
    chunk = (chunks[0] + j) ^ (me // 8) if packed else chunks[0] + j

    @pl.when(j == 0)
    def _():
        if end:
            pltpu.make_async_copy(wproj_ref, wproj_out, sem).start()
        if not begin:
            return
        for i in range(tiles):
            s, t = i // per_sample, i % per_sample
            here = slice(i * tile, (i + 1) * tile)
            normed, _ = normalize(xs[s][t * tile : (t + 1) * tile])
            value = (normed * vec_ref[5:6] + vec_ref[6:7]).astype(BF16)
            mlp_in[here] = value
            mlp_in_t[:, here] = value.T
            for p in range(2):
                gt[i * tile + p * piece : i * tile + (p + 1) * piece] = cots[2 * t + p][s]
            acc[here] = jnp.zeros((tile, width), F32)
            gacc[here] = jnp.zeros((tile, width), F32)

    at = pl.ds(pl.multiple_of(chunk * columns, columns), columns)
    b1 = vec_ref[pl.ds(8 + chunk, 1)]
    db1 = jnp.zeros((1, columns), F32)
    for i in range(tiles):
        here = slice(i * tile, (i + 1) * tile)
        value, slope = gelu_both(dot(mlp_in[here], w1_ref[:, at]) + b1)
        value = value.astype(BF16)
        act[here] = value
        g = (dot(gt[here], w2_ref[at], NT) * slope).astype(BF16)
        gpre[here] = g
        db1 = db1 + row_sum(g)
        acc[here] += dot(value, w2_ref[at])
        gacc[here] += dot(g, w1_ref[:, at], NT)
    db1_ref[pl.ds(chunk % 2, 1)] = db1
    if packed:
        keep, send = dw_refs
        result[...] = dot(mlp_in_t[...], gpre[...])
        slot = pl.multiple_of((chunk % 2) * 6 * PER, 16)
        for e in range(2):
            store_packed(keep, send, HIDDEN[chunks[0] // 2][0], me, result, slot + e * 12 * PER, e * Z1)
        result[...] = dot(act[...], gt[...], TN)
        for position in range(16):
            owner = relative(position, HIDDEN[chunks[0] // 2][1])
            if owner & Z0:
                continue
            start = pl.multiple_of(((me % 8) ^ (owner % 8)) * 96, 8)
            where = position % 8 + (chunks[0] % 2 + j) * 2 ** (3 - HIDDEN[chunks[0] // 2][1].index(Z0))
            for c in range(width // 128):
                part = result[pl.ds(start, 96), c * 128 : (c + 1) * 128].astype(BF16)
                (keep, send)[position // 8][where, 24 * PER + c * 96 : 24 * PER + (c + 1) * 96] = part
    else:
        dw_refs[0][...] = dot(mlp_in_t[...], gpre[...])
        dw_refs[1][...] = dot(act[...], gt[...], TN)

    @pl.when(j == pl.num_programs(0) - 1)
    def _():
        if not end:
            return
        sums = [jnp.zeros((1, width), F32) for _ in range(4)]
        leaving = []
        for i in range(tiles):
            s, t = i // per_sample, i % per_sample
            here = slice(i * tile, (i + 1) * tile)
            x = xs[s][t * tile : (t + 1) * tile]
            normed, inverse = normalize(x)
            mixed = (x + acc[here] + vec_ref[7:8]).astype(BF16)
            for p in range(2):
                mixed_refs[2 * t + p][s] = mixed[p * piece : (p + 1) * piece]
            cot = gt[here].astype(F32)
            g = gacc[here]
            gmid = cot + normalize_back(g * vec_ref[5:6], normed, inverse)
            gacc[here] = gmid
            leaving.append(pltpu.make_async_copy(gacc.at[here], gmid_out.at[here], gmid_sems.at[i]))
            leaving[-1].start()
            low = gmid.astype(BF16)
            gone_ref[s, t * tile : (t + 1) * tile] = low
            sums = [a + row_sum(b) for a, b in zip(sums, (g * normed, g, cot, low))]
        for k in range(4):
            small_ref[k : k + 1] = sums[k]
        for copy in leaving:
            copy.wait()
        pltpu.make_async_copy(wproj_ref, wproj_out, sem).wait()


def mlp(packed, tokens, chunks, x0, x1, w1, w2, vec, cots=None, held=None, grads=None, w_proj=None):
    begin, end = held is None, w_proj is not None
    rows, width = x0.shape
    hidden = w1.shape[1]
    columns = width
    length = 2 * rows
    sums = [pltpu.VMEM((length, width), F32)] * 2
    ops = near(x0, x1, w1, w2, vec)
    outs = list(sums)
    aliases = {}
    if begin:
        ops += near(*cots)
        outs = [pltpu.VMEM(s, BF16) for s in ((length, width), (width, length), (length, width))] + outs
    else:
        aliases = {len(ops) + 3: 0, len(ops) + 4: 1}
        ops += near(*held)
    at = len(outs)
    db1 = pltpu.VMEM((2, columns), F32)
    if packed:
        outs += [db1] + [pltpu.VMEM((8, 48 * PER, 128), BF16)] * 2
        dw_specs = [VMEM] * 3
        if grads is not None:
            aliases.update({len(ops) + i: at + i for i in range(3)})
            ops += near(*grads)
    else:
        whole = len(chunks) * columns
        outs += [db1, pltpu.HBM((width, whole), F32), pltpu.HBM((whole, width), F32)]
        dw_specs = [VMEM, pl.BlockSpec((width, columns), lambda j: (0, j)), pl.BlockSpec((columns, width), lambda j: (j, 0))]
    specs = [VMEM] * at + dw_specs
    in_specs = [VMEM] * len(ops)
    if end:
        ops += far(w_proj)
        in_specs += [ANY]
        outs += [pltpu.VMEM((2, rows, width), BF16), pltpu.VMEM((4, width), F32), pltpu.VMEM(w_proj.shape, BF16)]
        share = (2, rows // 4, width)
        outs += [pltpu.VMEM(share, BF16), pltpu.VMEM((2,) + share, BF16), pltpu.VMEM(share, BF16)]
        outs += [pltpu.HBM((length, width), F32)]
        specs += [VMEM] * 6 + [ANY]
    return call(
        functools.partial(mlp_kernel, packed, begin, end, chunks),
        tokens,
        ops,
        in_specs,
        12 if packed else 26,
        aliases,
        grid=(len(chunks),),
        out_specs=specs,
        out_shape=outs,
        scratch_shapes=[
            pltpu.VMEM((length, columns), BF16),
            pltpu.VMEM((length, columns), BF16),
            pltpu.VMEM((width, columns), F32),
            pltpu.SemaphoreType.DMA(()),
        ]
        + ([pltpu.SemaphoreType.DMA((4,))] if end else []),
        cost=HEAVY,
        name=f"mlp_{chunks[0]}",
    )


def attend_back_kernel(sample, first, fetch, far_away, *rest):
    take = lambda n: (rest[:n], rest[n:])
    if first:
        (joined, probs, _, gatt), rest = take(4)
    else:
        (joined, probs, gone_ref, wproj_ref), rest = take(4)
    fetches, rest = take(fetch)
    (gjoined_ref,), rest = take(1)
    if not first:
        (gatt,), rest = take(1)
    fetched, rest = take(fetch)
    own = []
    if far_away:
        (joined_near, probs_near, joined_sem, probs_sems), rest = take(4)
        joined, joined_hbm, probs, probs_hbm = joined_near, joined, probs_near, probs
        own = brought([joined_hbm], [joined], joined_sem)
        for k in range(HEADS // 2):
            pair_of = lambda ref: ref.at[pl.ds(2 * k, 2)]
            own.append(pltpu.make_async_copy(pair_of(probs_hbm), pair_of(probs), probs_sems.at[k]))
    (sems,) = rest
    loads = brought(fetches, fetched, sems)
    j = pl.program_id(0)
    rows, width = gatt.shape

    @pl.when(j == 0)
    def _():
        for load in own[: PIECES + 2] if own else loads:
            load.start()
        if not first:
            gatt[...] = dot(gone_ref[sample], wproj_ref[...], NT).astype(BF16)

    if own:
        for k, load in enumerate(own[PIECES + 2 :]):
            pl.when(j == k + 1)(load.start)

        @pl.when(j == 1)
        def _():
            for load in loads:
                load.start()

    pair = first + j
    at = pl.multiple_of(pair * 128, 128)
    if far_away:
        for load in own[:PIECES]:
            pl.when(j == 0)(load.wait)
        here = pl.ds(2 * pair, 2)
        pltpu.make_async_copy(probs_hbm.at[here], probs.at[here], probs_sems.at[pair]).wait()
    q, k, v = [joined[:, pl.ds(pl.multiple_of(c * width + pair * 128, 128), 128)] for c in range(3)]
    g = gatt[:, pl.ds(at, 128)]
    k_t = k.T
    left = lax.broadcasted_iota(jnp.int32, (rows, 128), 1) < HALF
    g_q, g_k, g_v = [], [], []
    for h in range(2):
        weights = probs[2 * pair + h]
        weighted = weights.astype(F32) * dot(v, jnp.where(left == (h == 0), g, jnp.zeros_like(g)), NT)
        delta = jnp.sum(weighted, axis=0, keepdims=True)
        scores = (weighted - weights.astype(F32) * delta).astype(BF16)
        g_v.append(dot(weights, g))
        g_k.append(dot(scores, q))
        g_q.append(dot(k_t[h * HALF : (h + 1) * HALF], scores))
    gjoined_ref[:, pl.ds(at, 128)] = (jnp.concatenate(g_q, 0).T * HALF**-0.5).astype(BF16)
    at_k = pl.multiple_of(width + pair * 128, 128)
    at_v = pl.multiple_of(2 * width + pair * 128, 128)
    gjoined_ref[:, pl.ds(at_k, 128)] = jnp.where(left, g_k[0], g_k[1]).astype(BF16)
    gjoined_ref[:, pl.ds(at_v, 128)] = jnp.where(left, g_v[0], g_v[1]).astype(BF16)

    @pl.when(j == pl.num_programs(0) - 1)
    def _():
        for load in loads:
            load.wait()


def attend_back(sample, first, pairs, tokens, joined, probs, begin, go_on, fetches):
    rows, width = joined.shape[0], joined.shape[1] // 3
    far_away = sample == 0
    bring = far if far_away else near
    ops = bring(joined, probs)
    specs = [ANY if far_away else VMEM] * 2
    outs = [pltpu.VMEM((rows, 3 * width), BF16)]
    scratch, aliases = [], {}
    if first:
        ops += near(*go_on)
        specs += [VMEM] * 2
        aliases = {2: 0}
    else:
        ops += near(*begin)
        specs += [VMEM] * 2
        outs += [pltpu.VMEM((rows, width), BF16)]
    if far_away:
        scratch += [pltpu.VMEM(joined.shape, BF16), pltpu.VMEM(probs.shape, BF16)]
        scratch += [pltpu.SemaphoreType.DMA((PIECES,)), pltpu.SemaphoreType.DMA((HEADS // 2,))]
    fetch = len(fetches)
    n = len(outs)
    out = call(
        functools.partial(attend_back_kernel, sample, first, fetch, far_away),
        tokens,
        [*ops, *far(*fetches)],
        specs + [ANY] * fetch,
        18 if far_away else 9,
        aliases,
        grid=(pairs,),
        out_specs=[VMEM] * (n + fetch),
        out_shape=outs + [pltpu.VMEM(a.shape, a.dtype) for a in fetches],
        scratch_shapes=scratch + [pltpu.SemaphoreType.DMA((max(fetch * PIECES, 1),))],
        cost=HEAVY,
        name=f"attend_back_{sample}_{first}",
    )
    return out[:n], out[n:]


def weights_kernel(packed, half, g0_ref, g1_ref, a0_ref, a1_ref, *rest):
    if not half:
        (gone_ref, l0_ref, l1_ref), rest = rest[:3], rest[3:]
    sums_ref, dw_refs, result = rest[0], rest[1:-1], rest[-1]
    width = a0_ref.shape[0]
    part = width // 2
    for c in range(3):
        at = slice(c * width + half * part, c * width + (half + 1) * part)
        here = slice(c * part, (c + 1) * part)
        result[:, here] = dot(a0_ref[...], g0_ref[:, at]) + dot(a1_ref[...], g1_ref[:, at])
        total = row_sum(g0_ref[:, at]) + row_sum(g1_ref[:, at])
        sums_ref[:, here] = jnp.broadcast_to(total, (8, part))
    end = 3 * part
    if not half:
        result[:, end : end + width] = dot(l0_ref[...], gone_ref[0]) + dot(l1_ref[...], gone_ref[1])
        end += width
    result[:, end:] = jnp.zeros((width, result.shape[1] - end), F32)
    if packed:
        orders = ((LAST, Z_FIRST + (Z1,)), (LAST,))[half]
        share = result.shape[1] // len(orders)
        for i, order in enumerate(orders):
            cut = (i * share, (i + 1) * share)
            store_packed(*dw_refs, order, place()[0], result, i * share // 128 * PER, columns=cut)
    else:
        dw_refs[0][...] = result[...]


def weights(packed, half, tokens, g0, g1, a0, a1, proj=()):
    width = a0.shape[0]
    part = width // 2
    columns = -(-(3 * part + (0 if half else width)) // 256) * 256
    if packed:
        grads = [pltpu.VMEM((16, columns // 128 * PER, 128), BF16)] * 2
    else:
        grads = [pltpu.VMEM((width, columns), F32)]
    ops = near(g0, g1, a0, a1, *proj)
    return call(
        functools.partial(weights_kernel, packed, half),
        tokens,
        ops,
        [VMEM] * len(ops),
        10,
        out_specs=[VMEM] * (1 + len(grads)),
        out_shape=[pltpu.VMEM((8, 3 * part), F32)] + grads,
        scratch_shapes=[pltpu.VMEM((width, columns), F32)],
        cost=HEAVY,
        name=f"weights_{half}",
    )


def token_rows(sample, g_ref, w_ref, x_ref, gmid_ref, ids_ref, vec_ref, pgrad_refs, grad_t, hot):
    rows, width = x_ref.shape
    positions = hot.shape[0]
    piece = pgrad_refs[0].shape[0]
    tile = 2 * piece
    g_gain = jnp.zeros((1, width), F32)
    g_bias = jnp.zeros((1, width), F32)
    for t in range(rows // tile):
        cut = slice(t * tile, (t + 1) * tile)
        grad = dot(g_ref[cut], w_ref[...], NT)
        normed, inverse = normalize(x_ref[cut])
        gmid = gmid_ref[sample * rows + t * tile : sample * rows + (t + 1) * tile]
        total = gmid + normalize_back(grad * vec_ref[0:1], normed, inverse)
        low = total.astype(BF16)
        for p in range(2):
            pgrad_refs[2 * t + p][...] = low[p * piece : (p + 1) * piece]
        grad_t[:, cut] = low.T
        g_gain = g_gain + row_sum(grad * normed)
        g_bias = g_bias + row_sum(grad)
        wanted = ids_ref[0:1, cut].astype(jnp.int32)
        iota = lax.broadcasted_iota(jnp.int32, (positions, tile), 0)
        hot[:, cut] = (iota == wanted).astype(F32).astype(BF16)
    return g_gain, g_bias


def finish_first_kernel(g_ref, w_ref, x_ref, gmid_ref, ids_ref, vec_ref, own, core, far_own, table, sums, grad_t, hot):
    g_gain, g_bias = token_rows(
        0, g_ref, w_ref, x_ref, gmid_ref, ids_ref, vec_ref, (own, core.at[0], far_own, core.at[1]), grad_t, hot
    )
    sums[...] = jnp.concatenate([g_gain, g_bias, jnp.zeros((6, g_gain.shape[1]), F32)], 0)
    table[...] = dot(grad_t[...], hot[...], NT)


def finish_kernel(
    packed, g_ref, w_ref, x_ref, gmid_ref, ids_ref, vec_ref, small_ref, sums0_ref, sums1_ref, db1a_ref, db1b_ref,
    table_ref, before_ref, own, core, far_own, *rest,
):
    dw_refs, (grad_t, hot, result) = rest[:-3], rest[-3:]
    pgrad_refs = (own, core.at[0], far_own, core.at[1])
    width = x_ref.shape[1]
    positions = hot.shape[0]
    part = width // 2
    me = place()[0]
    g_gain, g_bias = token_rows(1, g_ref, w_ref, x_ref, gmid_ref, ids_ref, vec_ref, pgrad_refs, grad_t, hot)
    columns = lambda c: jnp.concatenate([ref[0:1, c * part : (c + 1) * part] for ref in (sums0_ref, sums1_ref)], 1)
    few = [g_gain + before_ref[0:1], g_bias + before_ref[1:2], columns(0), columns(2), small_ref[3:4], small_ref[0:3]]
    few = jnp.concatenate(few + [jnp.zeros((120, width), F32)], 0).T
    result[:, 0:positions] = table_ref[...] + dot(grad_t[...], hot[...], NT)
    result[:, positions:] = few
    if packed:
        half = (me // Z1) % 2
        a, b = db1a_ref[...], db1b_ref[...]
        sums = jnp.concatenate([jnp.where(half == 0, a, b), jnp.where(half == 0, b, a)], 0)
        share = 96
        for owner in range(32):
            c, start = owner // 8, owner % 8 * share
            row = jnp.concatenate([jnp.zeros((1, 16), F32), sums[c : c + 1, start : start + share], jnp.zeros((1, 16), F32)], 1)
            result[owner * PER : owner * PER + 1, positions:] += row
        store_packed(*dw_refs, LAST, me, result)
    else:
        dw_refs[0][...] = result[...]


def finish(packed, last, tokens, ops, positions):
    rows, width = ops[2].shape
    columns = positions + 128
    share = (rows // 4, width)
    outs = [pltpu.VMEM(share, BF16), pltpu.VMEM((2,) + share, BF16), pltpu.VMEM(share, BF16)]
    scratch = [pltpu.VMEM((width, rows), BF16), pltpu.VMEM((positions, rows), BF16)]
    if not last:
        outs += [pltpu.VMEM((width, positions), F32), pltpu.VMEM((8, width), F32)]
    else:
        scratch += [pltpu.VMEM((width, columns), F32)]
        if packed:
            outs += [pltpu.VMEM((16, PER * columns // 128, 128), BF16)] * 2
        else:
            outs += [pltpu.VMEM((width, columns), F32)]
    return call(
        functools.partial(finish_kernel, packed) if last else finish_first_kernel,
        tokens,
        near(*ops),
        [VMEM] * len(ops),
        14,
        out_specs=[VMEM] * len(outs),
        out_shape=outs,
        scratch_shapes=scratch,
        cost=HEAVY,
        name=f"finish_{int(last)}",
    )


def swap_bit(x, bit, count):
    return lax.ppermute(x, AXES, [(d, d ^ bit) for d in range(count)])


def add(arrays):
    return sum(a.astype(F32) for a in arrays)


def fold_kernel(spans, *refs):
    n = 2 * sum(len(one) for one in spans)
    pairs, outs = refs[:n], refs[n:]
    for k, one in enumerate(spans):
        message, stay = outs[2 * k : 2 * k + 2]
        half = message.shape[0]
        row = 0
        for first, rows in one:
            (a, b), pairs = pairs[:2], pairs[2:]
            here, there = slice(row, row + rows), slice(first, first + rows)
            for i in range(half):
                message[i, here] = a[half + i, there] + b[half + i, there]
            for i in range(half):
                stay[i, here] = a[i, there] + b[i, there]
            row += rows


class Sums:
    def __init__(self, count, order):
        self.count, self.bits, self.pairs, self.spans = count, list(order), [], []

    def swap(self, send, bit):
        return lax.ppermute(send, AXES, [(d, d ^ bit) for d in range(self.count)])


def begin(keep, send, *sums):
    got = sums[0].swap(send, sums[0].bits[0])
    rows = keep.shape[1] // len(sums)
    for i, one in enumerate(sums):
        one.pairs += [keep, got]
        one.spans.append((i * rows, rows))


def fold(tokens, *sums, cost=LIGHT):
    outs = []
    for one in sums:
        rows = sum(span[1] for span in one.spans)
        outs += [pltpu.VMEM((one.pairs[0].shape[0] // 2, rows, 128), BF16)] * 2
    pairs = [a for one in sums for a in one.pairs]
    out = call(
        functools.partial(fold_kernel, [one.spans for one in sums]),
        tokens,
        near(*pairs),
        [VMEM] * len(pairs),
        2,
        out_specs=[VMEM] * len(outs),
        out_shape=outs,
        cost=cost,
        name="fold",
    )
    for one, message, stay in zip(sums, out[::2], out[1::2]):
        one.bits = one.bits[1:]
        one.pairs = [stay, one.swap(message, one.bits[0])]
        one.spans = [(0, stay.shape[1])]
    return tuple(out[::2])


def turn_kernel(a0, a1, b0, b1, c0, c1, out):
    n = 12 * PER
    for c in range(6):
        rows = slice(96 * c, 96 * (c + 1))
        out[:, 128 * c : 128 * (c + 1)] = add([c0[0, rows], c1[0, rows]]).astype(BF16)
    for at, pair in ((768, (a0, a1)), (1152, (b0, b1))):
        for k in range(6):
            rows = slice(n + 48 * k, n + 48 * (k + 1))
            value = add([a[0, rows] for a in pair]).astype(BF16)
            out[48 * (k // 3) : 48 * (k // 3 + 1), at + 128 * (k % 3) : at + 128 * (k % 3 + 1)] = value


def hidden_kernel(a0, a1, b0, b1, c0, c1, other, dw1, dw2, done):
    done[...] = jnp.zeros_like(done)
    n = 12 * PER
    low = (place()[0] // Z1) % 2 == 0
    for c in range(6):
        rows, cols = slice(96 * c, 96 * (c + 1)), slice(128 * c, 128 * (c + 1))
        dw2[:, cols] = add([c0[0, rows], c1[0, rows], other[:, cols]])
    for k in range(6):
        rows = slice(48 * k, 48 * (k + 1))
        block = lambda at: other[48 * (k // 3) : 48 * (k // 3 + 1), at + 128 * (k % 3) : at + 128 * (k % 3 + 1)]
        mine = add([a0[0, rows], a1[0, rows], block(1152)])
        theirs = add([b0[0, rows], b1[0, rows], block(768)])
        for e, half in enumerate((jnp.where(low, mine, theirs), jnp.where(low, theirs, mine))):
            for i in range(2):
                at = (12 * e + 2 * k + i) * 128
                dw1[:, at : at + 128] = half[i * PER : (i + 1) * PER]


def tiles_kernel(counts, layout, *refs):
    n = sum(counts)
    held, outs, result = refs[:n], refs[n:-1], refs[-1]
    row, at = 0, 0
    for count in counts:
        rows = held[at].shape[1]
        result[row : row + rows] = add([ref[0] for ref in held[at : at + count]])
        row, at = row + rows, at + count
    layout(result, outs)


def put_tiles(result, row, out, columns):
    for c in range(columns // 128):
        out[:, c * 128 : (c + 1) * 128] = result[row + c * PER : row + (c + 1) * PER]


def rest_layout(result, outs):
    dwqkv, dwproj, table, *few = outs
    width = dwproj.shape[1]
    part = width // 2
    tiles = lambda n: n // 128 * PER
    second = tiles(5 * part + 128)
    for c in range(3):
        for half, row in enumerate((0, second)):
            at = c * width + half * part
            put_tiles(result, row + tiles(c * part), dwqkv.at[:, at : at + part], part)
    put_tiles(result, tiles(3 * part), dwproj, width)
    third = second + tiles(3 * part + 128)
    put_tiles(result, third, table, table.shape[1])
    at = third + tiles(table.shape[1])
    tile = result[at : at + PER]
    for k in range(8):
        few[k][...] = jnp.sum(jnp.where(lax.broadcasted_iota(jnp.int32, (PER, 128), 1) == k, tile, 0.0), axis=1)
    few[8][...] = tile[0, 16:112]


def tiles(streams, layout, outs, name):
    arrays = [a for held in streams for a in held]
    rows = sum(held[0].shape[1] for held in streams)
    first = lambda a: pl.BlockSpec((1,) + a.shape[1:], lambda i: (0, 0, 0))
    return call(
        functools.partial(tiles_kernel, [len(held) for held in streams], layout),
        (),
        arrays,
        [first(a) for a in arrays],
        8,
        grid=(1,),
        out_specs=[pl.BlockSpec(shape, lambda i, n=len(shape): (0,) * n) for shape in outs],
        out_shape=[jax.ShapeDtypeStruct(shape, F32) for shape in outs],
        scratch_shapes=[pltpu.VMEM((rows, 128), F32)],
        name=name,
    )


def shards(
    patches, pos_ids, lengths, pos_table, ln1_gain, ln1_bias, w_qkv, q_bias, v_bias, w_proj, proj_bias,
    ln2_gain, ln2_bias, w_fc1, fc1_bias, w_fc2, fc2_bias, cotangent, *, wide, parts,
):
    width = patches.shape[2]
    hidden, positions = w_fc1.shape[1], pos_table.shape[1]
    count = wide * parts
    packed = wide == 8 and parts == 4
    hop = lambda a, k: lax.ppermute(a, "blk", [(d, d ^ k) for d in range(parts)])

    def across(own, core, far_own, *tokens):
        got = hop(core, 1)
        message = join(tokens, far_own, got)
        return message, (own, got, hop(message, 2))

    vectors = (ln1_gain, ln1_bias, q_bias, v_bias, proj_bias, ln2_gain, ln2_bias, fc2_bias, fc1_bias)
    message, xs = across(*prepare_first(pos_ids, patches))
    ys, cots, (vec, table, wqkv, wproj) = prepare_second(
        (message,), pos_ids, patches, cotangent, vectors, (pos_table, w_qkv, w_proj)
    )
    message, ys = across(*ys, xs[2])
    mid0, ids0, probs0, _, (x0, joined0, in0, low0_t) = attend(
        0, (message,), lengths, xs, table, vec, wqkv, wproj, ()
    )
    message, cots = across(*cots, ys[2])
    mid1, ids1, probs1, (w1, w2), (x1, joined1, in1, low1_t) = attend(
        1, (message,), lengths, ys, table, vec, wqkv, wproj, (w_fc1, w_fc2)
    )
    run = functools.partial(mlp, packed)
    *held, db1a = run((), (0, 1), mid0, mid1, w1, w2, vec, cots=cots)
    if packed:
        *held, db1a, a, b = held + [db1a]
        sum1, sum2 = [tuple(Sums(count, order) for order in orders) for orders in HIDDEN]
        begin(a, b, *sum1)
        *held[3:], db1b, a, b = run((), (2,), mid0, mid1, w1, w2, vec, held=held)
        messages = fold((db1b,), *sum1)
        _, _, db1b, a, b, gone, small, wproj, *mixed, gmid = run(
            messages, (3,), mid0, mid1, w1, w2, vec, held=held, grads=(db1b, a, b), w_proj=w_proj
        )
        begin(a, b, *sum2)
    else:
        *held, db1a, a, b = held + [db1a]
        grads1 = a, b
        _, _, db1b, a, b, gone, small, wproj, *mixed, gmid = run(
            (), (2, 3), mid0, mid1, w1, w2, vec, held=held, w_proj=w_proj
        )
        grads2 = a, b
    tokens = fold((), *sum1) if packed else ()
    (g0, *_), (joined1, probs1) = attend_back(
        0, 0, 6, tokens, joined0, probs0, (gone, wproj), (), (joined1, probs1)
    )
    message, mixed = across(*mixed, g0)
    tokens = (g0, message)
    if packed:
        tokens = fold(tokens, *sum1, *sum2)
    (g1, *state), (in0, in1, low0_t, low1_t, wqkv, x0, x1, gmid) = attend_back(
        1, 0, 3, tokens, joined1, probs1, (gone, wproj), (), (in0, in1, low0_t, low1_t, w_qkv, x0, x1, gmid)
    )
    tokens = (sum1[0].pairs[1], sum1[1].pairs[1]) if packed else ()
    sums0, *dwa = weights(packed, 0, tokens, g0, g1, in0, in1, (gone, low0_t, low1_t))
    if packed:
        sum3 = Sums(count, LAST), Sums(count, Z_FIRST + (Z1,))
        begin(*dwa, *sum3)
    *pgrad0, table0, before = finish(packed, False, (sums0,), (g0, wqkv, x0, gmid, ids0, vec), positions)
    tokens = (before, mixed[2])
    if packed:
        tokens += fold(tokens, *sum2, *sum3)
    (g1,), _ = attend_back(1, 3, 3, tokens, joined1, probs1, (), (g1, *state), ())
    tokens = (g1,)
    if packed:
        tokens = fold(tokens, *sum2)
    message, pgrad0 = across(*pgrad0, *tokens)
    sums1, *dwb = weights(packed, 1, tokens + (message,), g0, g1, in0, in1)
    tokens = (sums1,)
    if packed:
        sum4, sum5 = Sums(count, LAST), Sums(count, LAST)
        begin(*dwb, sum4)
        tokens = fold(tokens, *sum3) + (sum2[0].pairs[1], sum2[1].pairs[1])
    *pgrad1, a, b = tuple(
        finish(
            packed,
            True,
            tokens,
            (g1, wqkv, x1, gmid, ids1, vec, small, sums0, sums1, db1a, db1b, table0, before),
            positions,
        )
    ) + (() if packed else (None,))
    tokens = ()
    if packed:
        begin(a, b, sum5)
        tokens = fold((sum3[0].pairs[1], sum3[1].pairs[1], pgrad0[2]), sum4, cost=HEAVY)
        send = call(
            turn_kernel,
            tokens,
            near(*sum1[0].pairs, *sum2[0].pairs, *sum2[1].pairs),
            [VMEM] * 6,
            2,
            out_specs=VMEM,
            out_shape=pltpu.VMEM((96, 2 * width), BF16),
            name="turn",
        )
        other = sum4.swap(send, Z1)
        tokens = fold((send,), sum5)
    message, pgrad1 = across(*pgrad1, *tokens)
    if packed:
        tokens = fold((message, pgrad1[2]), sum4, *sum3)
        message = tokens[0]
        tokens = fold(tokens, sum5)
        mixed, done = gather((message,), mixed)
        tokens = fold(tokens + (other, done), sum4)
        sum3[0].pairs += sum3[1].pairs
        sum3[0].spans += sum3[1].spans
        tokens += fold(tokens, sum3[0])
        pgrad, done = gather(tokens, pgrad0, pgrad1)
        dw1, dw2, done = call(
            hidden_kernel,
            (done,),
            near(*sum1[0].pairs, *sum2[0].pairs, *sum1[1].pairs, other),
            [VMEM] * 7,
            2,
            out_specs=[VMEM] * 3,
            out_shape=[jax.ShapeDtypeStruct((n // count, hidden + width - n), F32) for n in (width, hidden)]
            + [pltpu.VMEM((8, 128), F32)],
            name="hidden",
        )
        fold(tokens, sum5)
        sum4.pairs += sum5.pairs
        sum4.spans += sum5.spans
        fold((), sum4)
        shapes = [(width // count, n) for n in (3 * width, width, positions)]
        shapes += [(width // count,)] * 8 + [(hidden // count,)]
        dwqkv, dwproj, table, *few = tiles([sum3[0].pairs, sum4.pairs], rest_layout, shapes, "rest")
    else:
        (mixed, _), (pgrad, _) = gather((message,), mixed), gather((), pgrad0, pgrad1)
        share = lambda a: lax.psum_scatter(a.astype(BF16), AXES, scatter_dimension=0, tiled=True).astype(F32)
        dw1 = share(jnp.concatenate([grads1[0], grads2[0]], 1))
        dw2 = share(jnp.concatenate([grads1[1], grads2[1]], 0))
        dwa, dwb, misc = share(dwa[0]), share(dwb[0]), share(a)
        n = width // 2
        dwqkv = jnp.concatenate([x[:, c * n : (c + 1) * n] for c in range(3) for x in (dwa, dwb)], 1)
        dwproj = dwa[:, 3 * n : 3 * n + width]
        table, few = misc[:, :positions], [misc[:, positions + k] for k in range(8)]
        few.append(share(jnp.concatenate([db1a, db1b], 0).reshape(-1)))
    (g_gain1, g_bias1, g_q, g_v, g_proj, g_gain2, g_bias2, g_fc2, g_fc1) = few
    return (
        mixed, pgrad, table, g_gain1, g_bias1, dwqkv, g_q, g_v, dwproj, g_proj, g_gain2, g_bias2,
        dw1, g_fc1, dw2, g_fc2,
    )


def solution(mesh):
    wide, parts = mesh.shape["wide"], mesh.shape["blk"]
    tokens = P("wide", "blk", None)
    in_specs = (tokens, P("wide", "blk"), P("wide")) + (P(),) * 14 + (tokens,)
    vector, matrix = P(AXES), P(AXES, None)
    out_specs = (
        tokens, tokens, matrix, vector, vector, matrix, vector, vector, matrix, vector, vector, vector,
        matrix, vector, matrix, vector,
    )
    return jax.shard_map(
        functools.partial(shards, wide=wide, parts=parts),
        mesh=mesh, in_specs=in_specs, out_specs=out_specs, check_vma=False,
    )
```

```python
import functools

import jax
import jax.numpy as jnp
from jax import lax
from jax.experimental import pallas as pl
from jax.experimental.pallas import tpu as pltpu
from jax.sharding import PartitionSpec as P

HEADS = 12
HALF = 64
F32, BF16 = jnp.float32, jnp.bfloat16
NN = (((1,), (0,)), ((), ()))
NT = (((1,), (1,)), ((), ()))
TN = (((0,), (0,)), ((), ()))
EPS = 1e-6
MASKED = -1e30
AXES = ("wide", "blk")
MIB = 2**20
CORE, Y, X, Z0, Z1 = 1, 2, 4, 8, 16
X_FIRST = (CORE, X, Y, Z0)
Z_FIRST = (CORE, Z0, X, Y)
HIDDEN = ((X_FIRST, (CORE, Z0, Y, X)), ((CORE, X, Z0, Y), Z_FIRST))
LAST = (CORE, X, Z0, Y, Z1)
PER = 24
LIGHT = pl.CostEstimate(flops=1, bytes_accessed=1, transcendentals=0)
HEAVY = pl.CostEstimate(flops=10**11, bytes_accessed=1, transcendentals=0)
VMEM = pl.BlockSpec(memory_space=pltpu.VMEM)
ANY = pl.BlockSpec(memory_space=pl.ANY)
SMEM = pl.BlockSpec(memory_space=pltpu.SMEM)


def dot(a, b, dims=NN):
    return lax.dot_general(a, b, dims, preferred_element_type=F32)


def near(*arrays):
    return [pltpu.with_memory_space_constraint(a, pltpu.VMEM) for a in arrays]


def far(*arrays):
    return [pltpu.with_memory_space_constraint(a, pltpu.HBM) for a in arrays]


def call(body, tokens, ops, in_specs, vmem, aliases=None, cost=LIGHT, **rest):
    n = len(tokens)
    return pl.pallas_call(
        lambda *refs: body(*refs[n:]),
        in_specs=[ANY] * n + in_specs,
        input_output_aliases={n + a: b for a, b in (aliases or {}).items()},
        compiler_params=pltpu.CompilerParams(vmem_limit_bytes=int(vmem * MIB)),
        cost_estimate=cost,
        **rest,
    )(*tokens, *ops)


PIECES = 4


def brought(sources, targets, sems):
    copies = []
    for a, b in zip(sources, targets):
        step = a.shape[0] // PIECES
        for i in range(PIECES):
            here = pl.ds(i * step, step)
            copies.append(pltpu.make_async_copy(a.at[here], b.at[here], sems.at[len(copies)]))
    return copies


def place():
    lane = lax.axis_index("blk")
    return lax.axis_index("wide") * lax.axis_size("blk") + lane, lane


def normalize(x):
    center = x - jnp.mean(x, axis=-1, keepdims=True)
    inverse = lax.rsqrt(jnp.mean(center * center, axis=-1, keepdims=True) + EPS)
    return center * inverse, inverse


def normalize_back(g, normed, inverse):
    return inverse * (
        g - jnp.mean(g, axis=-1, keepdims=True) - normed * jnp.mean(g * normed, axis=-1, keepdims=True)
    )


def gelu_both(x):
    cdf = 0.5 + 0.5 * lax.erf(x * 0.7071067811865476)
    return x * cdf, cdf + x * (jnp.exp(x * x * -0.5) * 0.3989422804014327)


def row_sum(x):
    return jnp.sum(x.astype(F32), axis=0, keepdims=True)


def relative(position, order):
    return sum(bit for i, bit in enumerate(order) if (position >> (len(order) - 1 - i)) & 1)


def store_packed(keep_ref, send_ref, order, me, result_ref, base=0, extra=0, columns=None):
    half = 2 ** (len(order) - 1)
    first, last = columns or (0, result_ref.shape[1])
    for position in range(2 * half):
        ref = (keep_ref, send_ref)[position // half]
        start = pl.multiple_of((me ^ (relative(position, order) | extra)) * PER, 8)
        for c in range((last - first) // 256):
            two = [result_ref[pl.ds(start, PER), first + (2 * c + i) * 128 : first + (2 * c + i + 1) * 128] for i in range(2)]
            here = pl.ds(base + 2 * c * PER, 2 * PER)
            ref[position % half, here] = jnp.concatenate(two, 0).astype(BF16)


def lay(own, core, far_own):
    return own, core.at[0], far_own, core.at[1]


def pieces(sample, ids_ref, outs, lane_me):
    piece = ids_ref.shape[1]
    for k, out in enumerate(lay(*outs)):
        ids = ids_ref[pl.ds(2 * (lane_me ^ k) + sample, 1)]
        row = jnp.concatenate([ids >> 8, ids & 255, jnp.zeros((1, out.shape[1] - 2 * piece), jnp.int32)], 1)
        out[piece : piece + 16] = jnp.broadcast_to(row.astype(F32), (16, out.shape[1])).astype(BF16)


def first_kernel(patches_ref, ids_hbm, own, core, far_own, ids_ref, sems):
    piece = patches_ref.shape[1]
    lane_me = place()[1]
    copies = [pltpu.make_async_copy(ids_hbm, ids_ref, sems.at[4])]
    for k, out in enumerate(lay(own, core, far_own)):
        copies.append(pltpu.make_async_copy(patches_ref.at[2 * (lane_me ^ k)], out.at[0:piece], sems.at[k]))
    for copy in copies:
        copy.start()
    copies[0].wait()
    pieces(0, ids_ref, (own, core, far_own), lane_me)
    for copy in copies[1:]:
        copy.wait()


def second_kernel(patches_ref, cot_ref, ids_hbm, *refs):
    vectors, big, refs = refs[:9], refs[9:12], refs[12:]
    second, cots, vec_ref, loaded = refs[:3], refs[3:6], refs[6], refs[7:10]
    ids_ref, raw, sems = refs[10], refs[11:-1], refs[-1]
    piece, width = patches_ref.shape[1:]
    lane_me = place()[1]
    copies = []

    def start(a, b):
        copies.append(pltpu.make_async_copy(a, b, sems.at[len(copies)]))
        copies[-1].start()
        return copies[-1]

    few = [start(ids_hbm, ids_ref)] + [start(a, b) for a, b in zip(vectors, raw)]
    for k, out in enumerate(lay(*second)):
        start(patches_ref.at[2 * (lane_me ^ k) + 1], out.at[0:piece])
    for a, b in zip(big, loaded):
        start(a, b)
    for k, out in enumerate(lay(*cots)):
        start(cot_ref.at[pl.ds(2 * (lane_me ^ k), 2)], out)
    for copy in few:
        copy.wait()
    pieces(1, ids_ref, second, lane_me)
    row = 0
    for ref in raw:
        for k in range(ref.shape[0] // width):
            vec_ref[row : row + 1] = ref[k * width : (k + 1) * width].astype(F32).reshape(1, width)
            row += 1
    vec_ref[row:] = jnp.zeros((vec_ref.shape[0] - row, width), F32)
    for copy in copies[len(few) :]:
        copy.wait()


def message_shapes(shape):
    return [pltpu.VMEM(shape, BF16), pltpu.VMEM((2,) + shape, BF16), pltpu.VMEM(shape, BF16)]


def prepare_first(pos_ids, patches):
    _, piece, width = patches.shape
    return call(
        first_kernel,
        (),
        far(patches, pos_ids),
        [ANY] * 2,
        2,
        out_specs=[VMEM] * 3,
        out_shape=message_shapes((piece + 16, width)),
        scratch_shapes=[pltpu.VMEM(pos_ids.shape, pos_ids.dtype), pltpu.SemaphoreType.DMA((5,))],
        name="first",
    )


def prepare_second(tokens, pos_ids, patches, cotangent, vectors, big):
    _, piece, width = patches.shape
    out = call(
        second_kernel,
        tokens,
        far(patches, cotangent, pos_ids, *vectors, *big),
        [ANY] * (3 + len(vectors) + len(big)),
        2,
        out_specs=[VMEM] * (7 + len(big)),
        out_shape=message_shapes((piece + 16, width))
        + message_shapes((2, piece, width))
        + [pltpu.VMEM((16, width), F32)]
        + [pltpu.VMEM(a.shape, a.dtype) for a in big],
        scratch_shapes=[
            pltpu.VMEM(pos_ids.shape, pos_ids.dtype),
            *[pltpu.VMEM(a.shape, a.dtype) for a in vectors],
            pltpu.SemaphoreType.DMA((9 + len(vectors) + len(big),)),
        ],
        cost=HEAVY,
        name="second",
    )
    return out[:3], out[3:6], out[6:]


def join_kernel(a_ref, b_ref, out, sems):
    copies = [
        pltpu.make_async_copy(a_ref, out.at[0], sems.at[0]),
        pltpu.make_async_copy(b_ref.at[1], out.at[1], sems.at[1]),
    ]
    for copy in copies:
        copy.start()
    for copy in copies:
        copy.wait()


def join(tokens, far_own, got, cost):
    return call(
        join_kernel,
        tokens,
        near(far_own, got),
        [VMEM] * 2,
        1,
        out_specs=VMEM,
        out_shape=pltpu.VMEM(got.shape, BF16),
        scratch_shapes=[pltpu.SemaphoreType.DMA((2,))],
        cost=cost,
        name="join",
    )


def gather_kernel(samples, *refs):
    sets, out, done, sems = refs[: 3 * samples], refs[-3], refs[-2], refs[-1]
    done[...] = jnp.zeros_like(done)
    lane_me = place()[1]
    copies = []
    for s in range(samples):
        own, got, other = sets[3 * s : 3 * s + 3]
        for k, a in enumerate((own, got.at[0], other.at[0], other.at[1])):
            at = 2 * (lane_me ^ k) + s
            where = out.at[pl.ds(at, 2)] if samples == 1 else out.at[at]
            copies.append(pltpu.make_async_copy(a, where, sems.at[4 * s + k]))
            copies[-1].start()
    for copy in copies:
        copy.wait()


def gather(tokens, *sets):
    ops = near(*[a for one in sets for a in one])
    return call(
        functools.partial(gather_kernel, len(sets)),
        tokens,
        ops,
        [VMEM] * len(ops),
        1,
        out_specs=[ANY, VMEM],
        out_shape=[pltpu.HBM((8,) + ops[0].shape[-2:], BF16), pltpu.VMEM((8, 128), F32)],
        scratch_shapes=[pltpu.SemaphoreType.DMA((4 * len(sets),))],
        name="gather",
    )


def attend_kernel(
    sample, fetch, lengths_ref, own_ref, got_ref, other_ref, table_ref, vec_ref, wqkv_ref, wproj_ref, *rest
):
    fetches, rest = rest[:fetch], rest[fetch:]
    mid_ref, ids_ref, probs_ref, rest = rest[0], rest[1], rest[2], rest[3:]
    fetched, rest = rest[:fetch], rest[fetch:]
    outs, (stream, joined, attn_in, attn_in_t, low, low_t, hidden, sems, fetch_sems) = rest[:4], rest[4:]
    saved = (stream, joined, attn_in_t, low_t)
    copies = [pltpu.make_async_copy(a, b, sems.at[i]) for i, (a, b) in enumerate(zip(saved, outs))]
    loads = brought(fetches, fetched, fetch_sems)
    j = pl.program_id(0)
    pieces = (own_ref, got_ref.at[0], other_ref.at[0], other_ref.at[1])
    rows, width = stream.shape
    piece = rows // len(pieces)

    @pl.when(j == 0)
    def _():
        for load in loads:
            load.start()
        positions = table_ref.shape[1]
        ids = []
        for k, ref in enumerate(pieces):
            coded = ref[piece : piece + 16].astype(F32)
            ids.append(coded[0:8, 0:piece] * 256.0 + coded[0:8, piece : 2 * piece])
        ids_ref[...] = jnp.concatenate(ids, 1)
        for k, ref in enumerate(pieces):
            here = slice(k * piece, (k + 1) * piece)
            column = jnp.broadcast_to(ids[k][0:1], (piece, piece)).T.astype(jnp.int32)
            iota = lax.broadcasted_iota(jnp.int32, (piece, piece), 1)
            onehot = jnp.concatenate([(column == iota + piece * c).astype(F32) for c in range(positions // piece)], 1)
            value = ref[0:piece].astype(F32) + dot(onehot.astype(BF16), table_ref[...], NT)
            stream[here] = value
            normed, _ = normalize(value)
            normed = (normed * vec_ref[0:1] + vec_ref[1:2]).astype(BF16)
            attn_in[here] = normed
            attn_in_t[:, here] = normed.T
        copies[0].start()
        copies[2].start()
        for c in range(3):
            cols = slice(c * width, (c + 1) * width)
            part = dot(attn_in[...], wqkv_ref[:, cols])
            if c != 1:
                part = part + vec_ref[2 + c // 2 : 3 + c // 2]
            part = part.astype(BF16)
            if c == 0:
                part = part * jnp.asarray(HALF**-0.5, BF16)
            joined[:, cols] = part
        copies[1].start()
        lane_me = place()[1]
        length = lengths_ref[2 * lane_me + sample]
        part = lax.broadcasted_iota(jnp.int32, (piece, 128), 0)
        for i in range(len(pieces)):
            visible = part + (lane_me ^ i) * piece < length
            hidden[i * piece : (i + 1) * piece] = jnp.where(visible, 0.0, MASKED)

    at = pl.multiple_of(j * 128, 128)
    q = joined[:, pl.ds(at, 128)]
    k = joined[:, pl.ds(pl.multiple_of(width + j * 128, 128), 128)]
    v = joined[:, pl.ds(pl.multiple_of(2 * width + j * 128, 128), 128)]
    v_t = v.T
    lane = lax.broadcasted_iota(jnp.int32, (rows, 128), 1)
    ones = jnp.ones((16, rows), BF16)
    heads = []
    for h in range(2):
        own = (lane < HALF) == (h == 0)
        spare = lane == HALF * (1 - h)
        q_h = jnp.where(own, q, jnp.where(spare, 1.0, 0.0).astype(BF16))
        k_h = jnp.where(own, k, jnp.where(spare, hidden[...], 0.0).astype(BF16))
        scores = dot(k_h, q_h, NT)
        weights = jnp.exp(scores - jnp.max(scores, axis=0, keepdims=True)).astype(BF16)
        out = dot(jnp.concatenate([v_t[h * HALF : (h + 1) * HALF], ones], 0), weights)
        inverse = 1.0 / out[HALF : HALF + 1]
        probs_ref[h] = weights * inverse.astype(BF16)
        heads.append(out[0:HALF] * inverse)
    heads = jnp.concatenate(heads, 0)
    low_t[pl.ds(at, 128)] = heads.astype(BF16)
    low[:, pl.ds(at, 128)] = heads.T.astype(BF16)

    @pl.when(j == pl.num_programs(0) - 1)
    def _():
        copies[3].start()
        mid_ref[...] = stream[...] + dot(low[...], wproj_ref[...]) + vec_ref[4:5]
        for copy in copies + loads:
            copy.wait()


def attend(sample, tokens, lengths, pieces, table, vec, w_qkv, w_proj, fetches):
    rows = 4 * (pieces[0].shape[0] - 16)
    width = w_proj.shape[0]
    fetch = len(fetches)
    saved = [
        ((rows, width), F32),
        ((rows, 3 * width), BF16),
        ((width, rows), BF16),
        ((width, rows), BF16),
    ]
    stream, joined, attn_in_t, low_t = [pltpu.VMEM(*a) for a in saved]
    low = pltpu.VMEM((rows, width), BF16)
    mid, ids, probs, *rest = call(
        functools.partial(attend_kernel, sample, fetch),
        tokens,
        [lengths, *near(*pieces, table, vec, w_qkv, w_proj), *far(*fetches)],
        [SMEM] + [VMEM] * 7 + [ANY] * fetch,
        13,
        grid=(HEADS // 2,),
        out_specs=[VMEM] * 2 + [pl.BlockSpec((2, rows, rows), lambda j: (j, 0, 0))] + [VMEM] * fetch + [ANY] * 4,
        out_shape=[pltpu.VMEM((rows, width), F32), pltpu.VMEM((8, rows), F32)]
        + [pltpu.HBM((HEADS, rows, rows), BF16)]
        + [pltpu.VMEM(a.shape, a.dtype) for a in fetches]
        + [pltpu.HBM(*a) for a in saved],
        scratch_shapes=[stream, joined, pltpu.VMEM((rows, width), BF16), attn_in_t, low, low_t]
        + [pltpu.VMEM((rows, 128), F32)]
        + [pltpu.SemaphoreType.DMA((4,)), pltpu.SemaphoreType.DMA((max(fetch * PIECES, 1),))],
        cost=HEAVY,
        name=f"attend_{sample}",
    )
    return mid, ids, probs, rest[:fetch], rest[fetch:]


def mlp_kernel(packed, begin, end, chunks, x0_ref, x1_ref, w1_ref, w2_ref, vec_ref, *rest):
    take = lambda n: (rest[:n], rest[n:])
    if begin:
        (own_ref, got_ref, other_ref), rest = take(3)
        cots = (own_ref, got_ref.at[0], other_ref.at[0], other_ref.at[1])
        (mlp_in, mlp_in_t, gt, acc, gacc), rest = take(5)
    else:
        (mlp_in, mlp_in_t, gt), rest = take(3)
        rest = rest[2:]
        if chunks[0] % 2:
            rest = rest[3:]
        if end:
            (wproj_ref,), rest = take(1)
        (acc, gacc), rest = take(2)
    (db1_ref, *dw_refs), rest = take(3)
    if end:
        (gone_ref, small_ref, wproj_out, own, core, far_own), rest = take(6)
        (gmid_out,), rest = take(1)
        gmid_sems, rest = rest[-1], rest[:-1]
        mixed_refs = (own, core.at[0], far_own, core.at[1])
    act, gpre, result, sem = rest
    j = pl.program_id(0)
    xs = (x0_ref, x1_ref)
    rows, width = x0_ref.shape
    columns = result.shape[1]
    tile = rows // 2
    piece = tile // 2
    per_sample = rows // tile
    tiles = len(xs) * per_sample
    me = place()[0]
    chunk = (chunks[0] + j) ^ (me // 8) if packed else chunks[0] + j

    @pl.when(j == 0)
    def _():
        if end:
            pltpu.make_async_copy(wproj_ref, wproj_out, sem).start()
        if not begin:
            return
        for i in range(tiles):
            s, t = i // per_sample, i % per_sample
            here = slice(i * tile, (i + 1) * tile)
            normed, _ = normalize(xs[s][t * tile : (t + 1) * tile])
            value = (normed * vec_ref[5:6] + vec_ref[6:7]).astype(BF16)
            mlp_in[here] = value
            mlp_in_t[:, here] = value.T
            for p in range(2):
                gt[i * tile + p * piece : i * tile + (p + 1) * piece] = cots[2 * t + p][s]
            acc[here] = jnp.zeros((tile, width), F32)
            gacc[here] = jnp.zeros((tile, width), F32)

    at = pl.ds(pl.multiple_of(chunk * columns, columns), columns)
    b1 = vec_ref[pl.ds(8 + chunk, 1)]
    db1 = jnp.zeros((1, columns), F32)
    for i in range(tiles):
        here = slice(i * tile, (i + 1) * tile)
        value, slope = gelu_both(dot(mlp_in[here], w1_ref[:, at]) + b1)
        value = value.astype(BF16)
        act[here] = value
        g = (dot(gt[here], w2_ref[at], NT) * slope).astype(BF16)
        gpre[here] = g
        db1 = db1 + row_sum(g)
        acc[here] += dot(value, w2_ref[at])
        gacc[here] += dot(g, w1_ref[:, at], NT)
    db1_ref[pl.ds(chunk % 2, 1)] = db1
    if packed:
        keep, send = dw_refs
        result[...] = dot(mlp_in_t[...], gpre[...])
        slot = pl.multiple_of((chunk % 2) * 6 * PER, 16)
        for e in range(2):
            store_packed(keep, send, HIDDEN[chunks[0] // 2][0], me, result, slot + e * 12 * PER, e * Z1)
        result[...] = dot(act[...], gt[...], TN)
        for position in range(16):
            owner = relative(position, HIDDEN[chunks[0] // 2][1])
            if owner & Z0:
                continue
            start = pl.multiple_of(((me % 8) ^ (owner % 8)) * 96, 8)
            where = position % 8 + (chunks[0] % 2 + j) * 2 ** (3 - HIDDEN[chunks[0] // 2][1].index(Z0))
            for c in range(width // 128):
                part = result[pl.ds(start, 96), c * 128 : (c + 1) * 128].astype(BF16)
                (keep, send)[position // 8][where, 24 * PER + c * 96 : 24 * PER + (c + 1) * 96] = part
    else:
        dw_refs[0][...] = dot(mlp_in_t[...], gpre[...])
        dw_refs[1][...] = dot(act[...], gt[...], TN)

    @pl.when(j == pl.num_programs(0) - 1)
    def _():
        if not end:
            return
        sums = [jnp.zeros((1, width), F32) for _ in range(4)]
        leaving = []
        for i in range(tiles):
            s, t = i // per_sample, i % per_sample
            here = slice(i * tile, (i + 1) * tile)
            x = xs[s][t * tile : (t + 1) * tile]
            normed, inverse = normalize(x)
            mixed = (x + acc[here] + vec_ref[7:8]).astype(BF16)
            for p in range(2):
                mixed_refs[2 * t + p][s] = mixed[p * piece : (p + 1) * piece]
            cot = gt[here].astype(F32)
            g = gacc[here]
            gmid = cot + normalize_back(g * vec_ref[5:6], normed, inverse)
            gacc[here] = gmid
            leaving.append(pltpu.make_async_copy(gacc.at[here], gmid_out.at[here], gmid_sems.at[i]))
            leaving[-1].start()
            low = gmid.astype(BF16)
            gone_ref[s, t * tile : (t + 1) * tile] = low
            sums = [a + row_sum(b) for a, b in zip(sums, (g * normed, g, cot, low))]
        for k in range(4):
            small_ref[k : k + 1] = sums[k]
        for copy in leaving:
            copy.wait()
        pltpu.make_async_copy(wproj_ref, wproj_out, sem).wait()


def mlp(packed, tokens, chunks, x0, x1, w1, w2, vec, cots=None, held=None, grads=None, w_proj=None):
    begin, end = held is None, w_proj is not None
    rows, width = x0.shape
    hidden = w1.shape[1]
    columns = width
    length = 2 * rows
    sums = [pltpu.VMEM((length, width), F32)] * 2
    ops = near(x0, x1, w1, w2, vec)
    outs = list(sums)
    aliases = {}
    if begin:
        ops += near(*cots)
        outs = [pltpu.VMEM(s, BF16) for s in ((length, width), (width, length), (length, width))] + outs
    else:
        aliases = {len(ops) + 3: 0, len(ops) + 4: 1}
        ops += near(*held)
    at = len(outs)
    db1 = pltpu.VMEM((2, columns), F32)
    if packed:
        outs += [db1] + [pltpu.VMEM((8, 48 * PER, 128), BF16)] * 2
        dw_specs = [VMEM] * 3
        if grads is not None:
            aliases.update({len(ops) + i: at + i for i in range(3)})
            ops += near(*grads)
    else:
        whole = len(chunks) * columns
        outs += [db1, pltpu.HBM((width, whole), F32), pltpu.HBM((whole, width), F32)]
        dw_specs = [VMEM, pl.BlockSpec((width, columns), lambda j: (0, j)), pl.BlockSpec((columns, width), lambda j: (j, 0))]
    specs = [VMEM] * at + dw_specs
    in_specs = [VMEM] * len(ops)
    if end:
        ops += far(w_proj)
        in_specs += [ANY]
        outs += [pltpu.VMEM((2, rows, width), BF16), pltpu.VMEM((4, width), F32), pltpu.VMEM(w_proj.shape, BF16)]
        share = (2, rows // 4, width)
        outs += [pltpu.VMEM(share, BF16), pltpu.VMEM((2,) + share, BF16), pltpu.VMEM(share, BF16)]
        outs += [pltpu.HBM((length, width), F32)]
        specs += [VMEM] * 6 + [ANY]
    return call(
        functools.partial(mlp_kernel, packed, begin, end, chunks),
        tokens,
        ops,
        in_specs,
        12 if packed else 26,
        aliases,
        grid=(len(chunks),),
        out_specs=specs,
        out_shape=outs,
        scratch_shapes=[
            pltpu.VMEM((length, columns), BF16),
            pltpu.VMEM((length, columns), BF16),
            pltpu.VMEM((width, columns), F32),
            pltpu.SemaphoreType.DMA(()),
        ]
        + ([pltpu.SemaphoreType.DMA((4,))] if end else []),
        cost=HEAVY,
        name=f"mlp_{chunks[0]}",
    )


def attend_back_kernel(sample, first, fetch, far_away, *rest):
    take = lambda n: (rest[:n], rest[n:])
    if first:
        (joined, probs, _, gatt), rest = take(4)
    else:
        (joined, probs, gone_ref, wproj_ref), rest = take(4)
    fetches, rest = take(fetch)
    (gjoined_ref,), rest = take(1)
    if not first:
        (gatt,), rest = take(1)
    fetched, rest = take(fetch)
    own = []
    if far_away:
        (joined_near, probs_near, joined_sem, probs_sems), rest = take(4)
        joined, joined_hbm, probs, probs_hbm = joined_near, joined, probs_near, probs
        own = brought([joined_hbm], [joined], joined_sem)
        for k in range(HEADS // 2):
            pair_of = lambda ref: ref.at[pl.ds(2 * k, 2)]
            own.append(pltpu.make_async_copy(pair_of(probs_hbm), pair_of(probs), probs_sems.at[k]))
    (sems,) = rest
    loads = brought(fetches, fetched, sems)
    j = pl.program_id(0)
    rows, width = gatt.shape

    @pl.when(j == 0)
    def _():
        for load in own[: PIECES + 2] if own else loads:
            load.start()
        if not first:
            gatt[...] = dot(gone_ref[sample], wproj_ref[...], NT).astype(BF16)

    if own:
        for k, load in enumerate(own[PIECES + 2 :]):
            pl.when(j == k + 1)(load.start)

        @pl.when(j == 1)
        def _():
            for load in loads:
                load.start()

    pair = first + j
    at = pl.multiple_of(pair * 128, 128)
    if far_away:
        for load in own[:PIECES]:
            pl.when(j == 0)(load.wait)
        here = pl.ds(2 * pair, 2)
        pltpu.make_async_copy(probs_hbm.at[here], probs.at[here], probs_sems.at[pair]).wait()
    q, k, v = [joined[:, pl.ds(pl.multiple_of(c * width + pair * 128, 128), 128)] for c in range(3)]
    g = gatt[:, pl.ds(at, 128)]
    k_t = k.T
    left = lax.broadcasted_iota(jnp.int32, (rows, 128), 1) < HALF
    g_q, g_k, g_v = [], [], []
    for h in range(2):
        weights = probs[2 * pair + h]
        weighted = weights.astype(F32) * dot(v, jnp.where(left == (h == 0), g, jnp.zeros_like(g)), NT)
        delta = jnp.sum(weighted, axis=0, keepdims=True)
        scores = (weighted - weights.astype(F32) * delta).astype(BF16)
        g_v.append(dot(weights, g))
        g_k.append(dot(scores, q))
        g_q.append(dot(k_t[h * HALF : (h + 1) * HALF], scores))
    gjoined_ref[:, pl.ds(at, 128)] = (jnp.concatenate(g_q, 0).T * HALF**-0.5).astype(BF16)
    at_k = pl.multiple_of(width + pair * 128, 128)
    at_v = pl.multiple_of(2 * width + pair * 128, 128)
    gjoined_ref[:, pl.ds(at_k, 128)] = jnp.where(left, g_k[0], g_k[1]).astype(BF16)
    gjoined_ref[:, pl.ds(at_v, 128)] = jnp.where(left, g_v[0], g_v[1]).astype(BF16)

    @pl.when(j == pl.num_programs(0) - 1)
    def _():
        for load in loads:
            load.wait()


def attend_back(sample, first, pairs, tokens, joined, probs, begin, go_on, fetches):
    rows, width = joined.shape[0], joined.shape[1] // 3
    far_away = sample == 0
    bring = far if far_away else near
    ops = bring(joined, probs)
    specs = [ANY if far_away else VMEM] * 2
    outs = [pltpu.VMEM((rows, 3 * width), BF16)]
    scratch, aliases = [], {}
    if first:
        ops += near(*go_on)
        specs += [VMEM] * 2
        aliases = {2: 0}
    else:
        ops += near(*begin)
        specs += [VMEM] * 2
        outs += [pltpu.VMEM((rows, width), BF16)]
    if far_away:
        scratch += [pltpu.VMEM(joined.shape, BF16), pltpu.VMEM(probs.shape, BF16)]
        scratch += [pltpu.SemaphoreType.DMA((PIECES,)), pltpu.SemaphoreType.DMA((HEADS // 2,))]
    fetch = len(fetches)
    n = len(outs)
    out = call(
        functools.partial(attend_back_kernel, sample, first, fetch, far_away),
        tokens,
        [*ops, *far(*fetches)],
        specs + [ANY] * fetch,
        18 if far_away else 9,
        aliases,
        grid=(pairs,),
        out_specs=[VMEM] * (n + fetch),
        out_shape=outs + [pltpu.VMEM(a.shape, a.dtype) for a in fetches],
        scratch_shapes=scratch + [pltpu.SemaphoreType.DMA((max(fetch * PIECES, 1),))],
        cost=HEAVY,
        name=f"attend_back_{sample}_{first}",
    )
    return out[:n], out[n:]


def weights_kernel(packed, half, g0_ref, g1_ref, a0_ref, a1_ref, *rest):
    if not half:
        (gone_ref, l0_ref, l1_ref), rest = rest[:3], rest[3:]
    sums_ref, dw_refs, result = rest[0], rest[1:-1], rest[-1]
    width = a0_ref.shape[0]
    part = width // 2
    for c in range(3):
        at = slice(c * width + half * part, c * width + (half + 1) * part)
        here = slice(c * part, (c + 1) * part)
        result[:, here] = dot(a0_ref[...], g0_ref[:, at]) + dot(a1_ref[...], g1_ref[:, at])
        total = row_sum(g0_ref[:, at]) + row_sum(g1_ref[:, at])
        sums_ref[:, here] = jnp.broadcast_to(total, (8, part))
    end = 3 * part
    if not half:
        result[:, end : end + width] = dot(l0_ref[...], gone_ref[0]) + dot(l1_ref[...], gone_ref[1])
        end += width
    result[:, end:] = jnp.zeros((width, result.shape[1] - end), F32)
    if packed:
        orders = ((LAST, Z_FIRST + (Z1,)), (LAST,))[half]
        share = result.shape[1] // len(orders)
        for i, order in enumerate(orders):
            cut = (i * share, (i + 1) * share)
            store_packed(*dw_refs, order, place()[0], result, i * share // 128 * PER, columns=cut)
    else:
        dw_refs[0][...] = result[...]


def weights(packed, half, tokens, g0, g1, a0, a1, proj=()):
    width = a0.shape[0]
    part = width // 2
    columns = -(-(3 * part + (0 if half else width)) // 256) * 256
    if packed:
        grads = [pltpu.VMEM((16, columns // 128 * PER, 128), BF16)] * 2
    else:
        grads = [pltpu.VMEM((width, columns), F32)]
    ops = near(g0, g1, a0, a1, *proj)
    return call(
        functools.partial(weights_kernel, packed, half),
        tokens,
        ops,
        [VMEM] * len(ops),
        10,
        out_specs=[VMEM] * (1 + len(grads)),
        out_shape=[pltpu.VMEM((8, 3 * part), F32)] + grads,
        scratch_shapes=[pltpu.VMEM((width, columns), F32)],
        cost=HEAVY,
        name=f"weights_{half}",
    )


def token_rows(sample, g_ref, w_ref, x_ref, gmid_ref, ids_ref, vec_ref, pgrad_refs, grad_t, hot):
    rows, width = x_ref.shape
    positions = hot.shape[0]
    piece = pgrad_refs[0].shape[0]
    tile = 2 * piece
    g_gain = jnp.zeros((1, width), F32)
    g_bias = jnp.zeros((1, width), F32)
    for t in range(rows // tile):
        cut = slice(t * tile, (t + 1) * tile)
        grad = dot(g_ref[cut], w_ref[...], NT)
        normed, inverse = normalize(x_ref[cut])
        gmid = gmid_ref[sample * rows + t * tile : sample * rows + (t + 1) * tile]
        total = gmid + normalize_back(grad * vec_ref[0:1], normed, inverse)
        low = total.astype(BF16)
        for p in range(2):
            pgrad_refs[2 * t + p][...] = low[p * piece : (p + 1) * piece]
        grad_t[:, cut] = low.T
        g_gain = g_gain + row_sum(grad * normed)
        g_bias = g_bias + row_sum(grad)
        wanted = ids_ref[0:1, cut].astype(jnp.int32)
        iota = lax.broadcasted_iota(jnp.int32, (positions, tile), 0)
        hot[:, cut] = (iota == wanted).astype(F32).astype(BF16)
    return g_gain, g_bias


def finish_first_kernel(g_ref, w_ref, x_ref, gmid_ref, ids_ref, vec_ref, own, core, far_own, table, sums, grad_t, hot):
    g_gain, g_bias = token_rows(
        0, g_ref, w_ref, x_ref, gmid_ref, ids_ref, vec_ref, (own, core.at[0], far_own, core.at[1]), grad_t, hot
    )
    sums[...] = jnp.concatenate([g_gain, g_bias, jnp.zeros((6, g_gain.shape[1]), F32)], 0)
    table[...] = dot(grad_t[...], hot[...], NT)


def finish_kernel(
    packed, g_ref, w_ref, x_ref, gmid_ref, ids_ref, vec_ref, small_ref, sums0_ref, sums1_ref, db1a_ref, db1b_ref,
    table_ref, before_ref, own, core, far_own, *rest,
):
    dw_refs, (grad_t, hot, result) = rest[:-3], rest[-3:]
    pgrad_refs = (own, core.at[0], far_own, core.at[1])
    width = x_ref.shape[1]
    positions = hot.shape[0]
    part = width // 2
    me = place()[0]
    g_gain, g_bias = token_rows(1, g_ref, w_ref, x_ref, gmid_ref, ids_ref, vec_ref, pgrad_refs, grad_t, hot)
    columns = lambda c: jnp.concatenate([ref[0:1, c * part : (c + 1) * part] for ref in (sums0_ref, sums1_ref)], 1)
    few = [g_gain + before_ref[0:1], g_bias + before_ref[1:2], columns(0), columns(2), small_ref[3:4], small_ref[0:3]]
    few = jnp.concatenate(few + [jnp.zeros((120, width), F32)], 0).T
    result[:, 0:positions] = table_ref[...] + dot(grad_t[...], hot[...], NT)
    result[:, positions:] = few
    if packed:
        half = (me // Z1) % 2
        a, b = db1a_ref[...], db1b_ref[...]
        sums = jnp.concatenate([jnp.where(half == 0, a, b), jnp.where(half == 0, b, a)], 0)
        share = 96
        for owner in range(32):
            c, start = owner // 8, owner % 8 * share
            row = jnp.concatenate([jnp.zeros((1, 16), F32), sums[c : c + 1, start : start + share], jnp.zeros((1, 16), F32)], 1)
            result[owner * PER : owner * PER + 1, positions:] += row
        store_packed(*dw_refs, LAST, me, result)
    else:
        dw_refs[0][...] = result[...]


def finish(packed, last, tokens, ops, positions):
    rows, width = ops[2].shape
    columns = positions + 128
    share = (rows // 4, width)
    outs = [pltpu.VMEM(share, BF16), pltpu.VMEM((2,) + share, BF16), pltpu.VMEM(share, BF16)]
    scratch = [pltpu.VMEM((width, rows), BF16), pltpu.VMEM((positions, rows), BF16)]
    if not last:
        outs += [pltpu.VMEM((width, positions), F32), pltpu.VMEM((8, width), F32)]
    else:
        scratch += [pltpu.VMEM((width, columns), F32)]
        if packed:
            outs += [pltpu.VMEM((16, PER * columns // 128, 128), BF16)] * 2
        else:
            outs += [pltpu.VMEM((width, columns), F32)]
    return call(
        functools.partial(finish_kernel, packed) if last else finish_first_kernel,
        tokens,
        near(*ops),
        [VMEM] * len(ops),
        14,
        out_specs=[VMEM] * len(outs),
        out_shape=outs,
        scratch_shapes=scratch,
        cost=HEAVY,
        name=f"finish_{int(last)}",
    )


def swap_bit(x, bit, count):
    return lax.ppermute(x, AXES, [(d, d ^ bit) for d in range(count)])


def add(arrays):
    return sum(a.astype(F32) for a in arrays)


def fold_kernel(spans, *refs):
    n = 2 * sum(len(one) for one in spans)
    pairs, outs = refs[:n], refs[n:]
    for k, one in enumerate(spans):
        message, stay = outs[2 * k : 2 * k + 2]
        half = message.shape[0]
        row = 0
        for first, rows in one:
            (a, b), pairs = pairs[:2], pairs[2:]
            here, there = slice(row, row + rows), slice(first, first + rows)
            for i in range(half):
                message[i, here] = a[half + i, there] + b[half + i, there]
            for i in range(half):
                stay[i, here] = a[i, there] + b[i, there]
            row += rows


class Sums:
    def __init__(self, count, order):
        self.count, self.bits, self.pairs, self.spans = count, list(order), [], []

    def swap(self, send, bit):
        return lax.ppermute(send, AXES, [(d, d ^ bit) for d in range(self.count)])


def begin(keep, send, *sums):
    got = sums[0].swap(send, sums[0].bits[0])
    rows = keep.shape[1] // len(sums)
    for i, one in enumerate(sums):
        one.pairs += [keep, got]
        one.spans.append((i * rows, rows))


def fold(tokens, *sums, cost=LIGHT):
    outs = []
    for one in sums:
        rows = sum(span[1] for span in one.spans)
        outs += [pltpu.VMEM((one.pairs[0].shape[0] // 2, rows, 128), BF16)] * 2
    pairs = [a for one in sums for a in one.pairs]
    out = call(
        functools.partial(fold_kernel, [one.spans for one in sums]),
        tokens,
        near(*pairs),
        [VMEM] * len(pairs),
        2,
        out_specs=[VMEM] * len(outs),
        out_shape=outs,
        cost=cost,
        name="fold",
    )
    for one, message, stay in zip(sums, out[::2], out[1::2]):
        one.bits = one.bits[1:]
        one.pairs = [stay, one.swap(message, one.bits[0])]
        one.spans = [(0, stay.shape[1])]
    return tuple(out[::2])


def turn_kernel(a0, a1, b0, b1, c0, c1, out):
    n = 12 * PER
    for c in range(6):
        rows = slice(96 * c, 96 * (c + 1))
        out[:, 128 * c : 128 * (c + 1)] = add([c0[0, rows], c1[0, rows]]).astype(BF16)
    for at, pair in ((768, (a0, a1)), (1152, (b0, b1))):
        for k in range(6):
            rows = slice(n + 48 * k, n + 48 * (k + 1))
            value = add([a[0, rows] for a in pair]).astype(BF16)
            out[48 * (k // 3) : 48 * (k // 3 + 1), at + 128 * (k % 3) : at + 128 * (k % 3 + 1)] = value


def hidden_kernel(a0, a1, b0, b1, c0, c1, other, dw1, dw2, done):
    done[...] = jnp.zeros_like(done)
    n = 12 * PER
    low = (place()[0] // Z1) % 2 == 0
    for c in range(6):
        rows, cols = slice(96 * c, 96 * (c + 1)), slice(128 * c, 128 * (c + 1))
        dw2[:, cols] = add([c0[0, rows], c1[0, rows], other[:, cols]])
    for k in range(6):
        rows = slice(48 * k, 48 * (k + 1))
        block = lambda at: other[48 * (k // 3) : 48 * (k // 3 + 1), at + 128 * (k % 3) : at + 128 * (k % 3 + 1)]
        mine = add([a0[0, rows], a1[0, rows], block(1152)])
        theirs = add([b0[0, rows], b1[0, rows], block(768)])
        for e, half in enumerate((jnp.where(low, mine, theirs), jnp.where(low, theirs, mine))):
            for i in range(2):
                at = (12 * e + 2 * k + i) * 128
                dw1[:, at : at + 128] = half[i * PER : (i + 1) * PER]


def tiles_kernel(counts, layout, *refs):
    n = sum(counts)
    held, outs, result = refs[:n], refs[n:-1], refs[-1]
    row, at = 0, 0
    for count in counts:
        rows = held[at].shape[1]
        result[row : row + rows] = add([ref[0] for ref in held[at : at + count]])
        row, at = row + rows, at + count
    layout(result, outs)


def put_tiles(result, row, out, columns):
    for c in range(columns // 128):
        out[:, c * 128 : (c + 1) * 128] = result[row + c * PER : row + (c + 1) * PER]


def rest_layout(result, outs):
    dwqkv, dwproj, table, *few = outs
    width = dwproj.shape[1]
    part = width // 2
    tiles = lambda n: n // 128 * PER
    second = tiles(5 * part + 128)
    for c in range(3):
        for half, row in enumerate((0, second)):
            at = c * width + half * part
            put_tiles(result, row + tiles(c * part), dwqkv.at[:, at : at + part], part)
    put_tiles(result, tiles(3 * part), dwproj, width)
    third = second + tiles(3 * part + 128)
    put_tiles(result, third, table, table.shape[1])
    at = third + tiles(table.shape[1])
    tile = result[at : at + PER]
    for k in range(8):
        few[k][...] = jnp.sum(jnp.where(lax.broadcasted_iota(jnp.int32, (PER, 128), 1) == k, tile, 0.0), axis=1)
    few[8][...] = tile[0, 16:112]


def tiles(streams, layout, outs, name):
    arrays = [a for held in streams for a in held]
    rows = sum(held[0].shape[1] for held in streams)
    first = lambda a: pl.BlockSpec((1,) + a.shape[1:], lambda i: (0, 0, 0))
    return call(
        functools.partial(tiles_kernel, [len(held) for held in streams], layout),
        (),
        arrays,
        [first(a) for a in arrays],
        8,
        grid=(1,),
        out_specs=[pl.BlockSpec(shape, lambda i, n=len(shape): (0,) * n) for shape in outs],
        out_shape=[jax.ShapeDtypeStruct(shape, F32) for shape in outs],
        scratch_shapes=[pltpu.VMEM((rows, 128), F32)],
        name=name,
    )


def shards(
    patches, pos_ids, lengths, pos_table, ln1_gain, ln1_bias, w_qkv, q_bias, v_bias, w_proj, proj_bias,
    ln2_gain, ln2_bias, w_fc1, fc1_bias, w_fc2, fc2_bias, cotangent, *, wide, parts,
):
    width = patches.shape[2]
    hidden, positions = w_fc1.shape[1], pos_table.shape[1]
    count = wide * parts
    packed = wide == 8 and parts == 4
    hop = lambda a, k: lax.ppermute(a, "blk", [(d, d ^ k) for d in range(parts)])

    def across(own, core, far_own, *tokens, cost=LIGHT):
        got = hop(core, 1)
        message = join(tokens, far_own, got, cost)
        return message, (own, got, hop(message, 2))

    vectors = (ln1_gain, ln1_bias, q_bias, v_bias, proj_bias, ln2_gain, ln2_bias, fc2_bias, fc1_bias)
    message, xs = across(*prepare_first(pos_ids, patches))
    ys, cots, (vec, table, wqkv, wproj) = prepare_second(
        (message,), pos_ids, patches, cotangent, vectors, (pos_table, w_qkv, w_proj)
    )
    message, ys = across(*ys, xs[2], cost=HEAVY)
    message2, cots = across(*cots, message)
    mid0, ids0, probs0, _, (x0, joined0, in0, low0_t) = attend(
        0, (message, message2), lengths, xs, table, vec, wqkv, wproj, ()
    )
    mid1, ids1, probs1, (w1, w2), (x1, joined1, in1, low1_t) = attend(
        1, (mid0,), lengths, ys, table, vec, wqkv, wproj, (w_fc1, w_fc2)
    )
    run = functools.partial(mlp, packed)
    *held, db1a = run((), (0, 1), mid0, mid1, w1, w2, vec, cots=cots)
    if packed:
        *held, db1a, a, b = held + [db1a]
        sum1, sum2 = [tuple(Sums(count, order) for order in orders) for orders in HIDDEN]
        begin(a, b, *sum1)
        *held[3:], db1b, a, b = run((), (2,), mid0, mid1, w1, w2, vec, held=held)
        messages = fold((db1b,), *sum1)
        _, _, db1b, a, b, gone, small, wproj, *mixed, gmid = run(
            messages, (3,), mid0, mid1, w1, w2, vec, held=held, grads=(db1b, a, b), w_proj=w_proj
        )
        begin(a, b, *sum2)
    else:
        *held, db1a, a, b = held + [db1a]
        grads1 = a, b
        _, _, db1b, a, b, gone, small, wproj, *mixed, gmid = run(
            (), (2, 3), mid0, mid1, w1, w2, vec, held=held, w_proj=w_proj
        )
        grads2 = a, b
    tokens = fold((), *sum1) if packed else ()
    (g0, *_), (joined1, probs1) = attend_back(
        0, 0, 6, tokens, joined0, probs0, (gone, wproj), (), (joined1, probs1)
    )
    message, mixed = across(*mixed, g0)
    tokens = (g0, message)
    if packed:
        tokens = fold(tokens, *sum1, *sum2)
    (g1, *state), (in0, in1, low0_t, low1_t, wqkv, x0, x1, gmid) = attend_back(
        1, 0, 3, tokens, joined1, probs1, (gone, wproj), (), (in0, in1, low0_t, low1_t, w_qkv, x0, x1, gmid)
    )
    tokens = (sum1[0].pairs[1], sum1[1].pairs[1]) if packed else ()
    sums0, *dwa = weights(packed, 0, tokens, g0, g1, in0, in1, (gone, low0_t, low1_t))
    if packed:
        sum3 = Sums(count, LAST), Sums(count, Z_FIRST + (Z1,))
        begin(*dwa, *sum3)
    *pgrad0, table0, before = finish(packed, False, (sums0,), (g0, wqkv, x0, gmid, ids0, vec), positions)
    tokens = (before, mixed[2])
    if packed:
        tokens += fold(tokens, *sum2, *sum3)
    (g1,), _ = attend_back(1, 3, 3, tokens, joined1, probs1, (), (g1, *state), ())
    tokens = (g1,)
    if packed:
        tokens = fold(tokens, *sum2)
    message, pgrad0 = across(*pgrad0, *tokens)
    sums1, *dwb = weights(packed, 1, tokens + (message,), g0, g1, in0, in1)
    tokens = (sums1,)
    if packed:
        sum4, sum5 = Sums(count, LAST), Sums(count, LAST)
        begin(*dwb, sum4)
        tokens = fold(tokens, *sum3) + (sum2[0].pairs[1], sum2[1].pairs[1])
    *pgrad1, a, b = tuple(
        finish(
            packed,
            True,
            tokens,
            (g1, wqkv, x1, gmid, ids1, vec, small, sums0, sums1, db1a, db1b, table0, before),
            positions,
        )
    ) + (() if packed else (None,))
    tokens = ()
    if packed:
        begin(a, b, sum5)
        tokens = fold((pgrad0[2],), sum4, cost=HEAVY)
        send = call(
            turn_kernel,
            tokens,
            near(*sum1[0].pairs, *sum2[0].pairs, *sum2[1].pairs),
            [VMEM] * 6,
            2,
            out_specs=VMEM,
            out_shape=pltpu.VMEM((96, 2 * width), BF16),
            name="turn",
        )
        other = sum4.swap(send, Z1)
        tokens = fold((send,), sum5)
    message, pgrad1 = across(*pgrad1, *tokens)
    if packed:
        tokens = fold((message, pgrad1[2]), sum4, *sum3)
        message = tokens[0]
        tokens = fold(tokens, sum5)
        mixed, done = gather((message,), mixed)
        tokens = fold(tokens + (other, done), sum4)
        sum3[0].pairs += sum3[1].pairs
        sum3[0].spans += sum3[1].spans
        tokens += fold(tokens, sum3[0])
        pgrad, done = gather(tokens, pgrad0, pgrad1)
        dw1, dw2, done = call(
            hidden_kernel,
            (done,),
            near(*sum1[0].pairs, *sum2[0].pairs, *sum1[1].pairs, other),
            [VMEM] * 7,
            2,
            out_specs=[VMEM] * 3,
            out_shape=[jax.ShapeDtypeStruct((n // count, hidden + width - n), F32) for n in (width, hidden)]
            + [pltpu.VMEM((8, 128), F32)],
            name="hidden",
        )
        fold(tokens, sum5)
        sum4.pairs += sum5.pairs
        sum4.spans += sum5.spans
        fold((), sum4)
        shapes = [(width // count, n) for n in (3 * width, width, positions)]
        shapes += [(width // count,)] * 8 + [(hidden // count,)]
        dwqkv, dwproj, table, *few = tiles([sum3[0].pairs, sum4.pairs], rest_layout, shapes, "rest")
    else:
        (mixed, _), (pgrad, _) = gather((message,), mixed), gather((), pgrad0, pgrad1)
        share = lambda a: lax.psum_scatter(a.astype(BF16), AXES, scatter_dimension=0, tiled=True).astype(F32)
        dw1 = share(jnp.concatenate([grads1[0], grads2[0]], 1))
        dw2 = share(jnp.concatenate([grads1[1], grads2[1]], 0))
        dwa, dwb, misc = share(dwa[0]), share(dwb[0]), share(a)
        n = width // 2
        dwqkv = jnp.concatenate([x[:, c * n : (c + 1) * n] for c in range(3) for x in (dwa, dwb)], 1)
        dwproj = dwa[:, 3 * n : 3 * n + width]
        table, few = misc[:, :positions], [misc[:, positions + k] for k in range(8)]
        few.append(share(jnp.concatenate([db1a, db1b], 0).reshape(-1)))
    (g_gain1, g_bias1, g_q, g_v, g_proj, g_gain2, g_bias2, g_fc2, g_fc1) = few
    return (
        mixed, pgrad, table, g_gain1, g_bias1, dwqkv, g_q, g_v, dwproj, g_proj, g_gain2, g_bias2,
        dw1, g_fc1, dw2, g_fc2,
    )


def solution(mesh):
    wide, parts = mesh.shape["wide"], mesh.shape["blk"]
    tokens = P("wide", "blk", None)
    in_specs = (tokens, P("wide", "blk"), P("wide")) + (P(),) * 14 + (tokens,)
    vector, matrix = P(AXES), P(AXES, None)
    out_specs = (
        tokens, tokens, matrix, vector, vector, matrix, vector, vector, matrix, vector, vector, vector,
        matrix, vector, matrix, vector,
    )
    return jax.shard_map(
        functools.partial(shards, wide=wide, parts=parts),
        mesh=mesh, in_specs=in_specs, out_specs=out_specs, check_vma=False,
    )
```
